32 devices in a mesh: gx: 8 (over z, y), gy: 4 (over x, core).
Axes of the slice: x: 2, y: 2, z: 4, core: 2. Of those that a mesh axis runs over, the one named last changes fastest.
Arguments:
- right_side: float32 [3, 32, 64, 256], P(None, 'gx', 'gy'), may hold values from -45 to 45
- diag_blocks: float32 [9, 32, 64, 256], P(None, 'gx', 'gy'), may hold values from -1.2 to 1.8
- off_blocks: float32 [6, 9, 32, 64, 256], P(None, None, 'gx', 'gy'), may hold values from -0.25 to 0.16
- cell_inverse: float32 [9, 32, 64, 256], P(None, 'gx', 'gy'), may hold values from -0.4 to 0.85
- send_cells: int32 [32, 3200], P(('gx', 'gy')), may hold values from 0 to 16383, as said below
- recv_index: int32 [256, 400], P(('gx', 'gy')), may hold values from 0 to 28799, as said below
- seg_count: int32 [256], P(('gx', 'gy')), may hold values from 50 to 400, as said below
- span_inverse: float32 [25, 48, 12288], P(None, None, ('gx', 'gy')), may hold values from -0.24 to 1.2
- span_couple: float32 [25, 9, 256], P(None, None, ('gx', 'gy')), may hold values from -3 to 3
Outputs:
- solution: float32 [3, 32, 64, 256], P(None, 'gx', 'gy')
- residual: float32 [3, 32, 64, 256], P(None, 'gx', 'gy')
The draws below stay inside these ranges and needn't reach their ends.
Inputs may be any that keep to these rules, and one draw needn't show every extreme that they name: `send_cells`: each row holds distinct local cells of its device. `recv_index`: over the live segments of one owner's wells the positions are distinct and name tiles inside the grid; entries of segments that are not live are arbitrary. `seg_count`: on one device in every draw all wells have 400 segments.
All inputs are finite; a program needn't handle non-finite values.
Results may differ from the reference program's by a relative error of at most 0.0001.
Values sent between devices are 32-bit elements; how exact they have to be, the bound alone decides.
No kernel may reach another device: no remote copies, remote signals or barrier semaphores. Data moves between devices by JAX's collectives and lax.ppermute only.
A program may use at most 128 MiB of HBM per device.

```python
import math
import jax
import jax.numpy as jnp
from jax import lax

CX = 4
CY = 16
CZ = 256
WELLS_DEV = 8
MAXSEG = 400
SPAN = 16
NCHUNK = 25
SLOTS = 3200
WELLS = 256
NX = 32
NY = 64
NZ = 256
N_GX = 8
N_GY = 4


def diagonal_mask(count):
    return jnp.arange(count) % 4 == 0


def draw_right_side(key, part):
    key_base, key_level = jax.random.split(jax.random.fold_in(key, 11))
    shape = (3, NX, NY, NZ)
    ramp = 1.0 + 2.0 * jnp.arange(NX, dtype=jnp.float32)[None, :, None, None] / max(NX - 1, 1)
    level = jnp.exp(jax.random.uniform(key_level, shape, jnp.float32, math.log(0.3), math.log(3.0)))
    base = jnp.clip(jax.random.normal(key_base, shape, jnp.float32), -5.0, 5.0)
    return base * ramp * level


def draw_diag_blocks(key, part):
    key_main, key_side = jax.random.split(jax.random.fold_in(key, 21))
    shape = (9, NX, NY, NZ)
    mask = diagonal_mask(9)[:, None, None, None]
    main = jax.random.uniform(key_main, shape, jnp.float32, 1.2, 1.8)
    side = 0.3 * jnp.clip(jax.random.normal(key_side, shape, jnp.float32), -4.0, 4.0)
    return jnp.where(mask, main, side)


def draw_off_blocks(key, part):
    key_main, key_side = jax.random.split(jax.random.fold_in(key, 31))
    shape = (6, 9, NX, NY, NZ)
    mask = diagonal_mask(9)[None, :, None, None, None]
    main = -jnp.exp(jax.random.uniform(key_main, shape, jnp.float32, math.log(0.05), math.log(0.25)))
    side = 0.04 * jnp.clip(jax.random.normal(key_side, shape, jnp.float32), -4.0, 4.0)
    return jnp.where(mask, main, side)


def draw_cell_inverse(key, part):
    key_main, key_side = jax.random.split(jax.random.fold_in(key, 41))
    shape = (9, NX, NY, NZ)
    mask = diagonal_mask(9)[:, None, None, None]
    main = jax.random.uniform(key_main, shape, jnp.float32, 0.55, 0.85)
    side = 0.1 * jnp.clip(jax.random.normal(key_side, shape, jnp.float32), -4.0, 4.0)
    return jnp.where(mask, main, side)


def draw_span_inverse(key, part):
    key_main, key_side = jax.random.split(jax.random.fold_in(key, 51))
    width = 3 * SPAN
    shape = (NCHUNK, width, WELLS * width)
    mask = (jnp.arange(width)[:, None] == jnp.arange(WELLS * width)[None, :] % width)[None]
    main = jax.random.uniform(key_main, shape, jnp.float32, 0.6, 1.2)
    side = 0.06 * jnp.clip(jax.random.normal(key_side, shape, jnp.float32), -4.0, 4.0)
    return jnp.where(mask, main, side)


def well_layout(key):
    base = jax.random.fold_in(key, 4242)
    keys = jax.random.split(base, 7)
    devices = N_GX * N_GY
    half = MAXSEG // 2
    device = jnp.arange(devices, dtype=jnp.int32)
    grid_x = device // N_GY
    grid_y = device % N_GY
    counts = jax.random.randint(keys[0], (devices, WELLS_DEV), MAXSEG // 4, MAXSEG + 1)
    full_x = jax.random.randint(keys[1], (), 1, N_GX - 1)
    full_y = jax.random.randint(keys[2], (), 1, N_GY - 1)
    near = (jnp.abs(grid_x - full_x) <= 1) & (jnp.abs(grid_y - full_y) <= 1)
    counts = jnp.where(near[:, None], MAXSEG, counts)
    phase = jax.random.randint(keys[3], (devices,), 0, 8)
    well = jnp.arange(WELLS_DEV, dtype=jnp.int32)
    heading = (well[None, :] + phase[:, None]) % 8
    step_x = jnp.take(jnp.array([-1, -1, -1, 0, 0, 1, 1, 1], jnp.int32), heading)
    step_y = jnp.take(jnp.array([-1, 0, 1, -1, 1, -1, 0, 1], jnp.int32), heading)
    host_x = grid_x[:, None] + step_x
    host_y = grid_y[:, None] + step_y
    inside = (host_x >= 0) & (host_x < N_GX) & (host_y >= 0) & (host_y < N_GY)
    tail = counts // 2
    head = counts - tail
    segs = jnp.where(inside, counts, head)
    place = (step_x + 1) * 3 + (step_y + 1)
    region = 8 * (well[None, :] // 8) + heading
    position = jnp.arange(MAXSEG, dtype=jnp.int32)[None, None, :]
    head_pos = 4 * SLOTS + well[None, :, None] * MAXSEG + position
    tail_pos = place[:, :, None] * SLOTS + region[:, :, None] * MAXSEG + half + position - head[:, :, None]
    live = position < segs[:, :, None]
    spare = jax.random.randint(keys[4], (devices, WELLS_DEV, MAXSEG), 0, 9 * SLOTS)
    index = jnp.where(position < head[:, :, None], head_pos, jnp.where(live, tail_pos, spare))
    columns = jax.vmap(lambda one_key: jax.random.permutation(one_key, CX * CY)[:2 * WELLS_DEV])(jax.random.split(keys[5], devices))
    depth = jax.random.randint(keys[6], (devices, 2 * WELLS_DEV), 0, CZ - half + 1)
    start = (columns * CZ + depth).reshape(devices, 2, WELLS_DEV).transpose(0, 2, 1)
    cells = start[:, :, :, None] + jnp.arange(half, dtype=jnp.int32)[None, None, None, :]
    return (segs.reshape(WELLS).astype(jnp.int32), index.reshape(WELLS, MAXSEG).astype(jnp.int32), cells.reshape(devices, SLOTS).astype(jnp.int32))


def draw_seg_count(key, part):
    return well_layout(key)[0]


def draw_recv_index(key, part):
    return well_layout(key)[1]


def draw_send_cells(key, part):
    return well_layout(key)[2]


def block_scale(rng, extent, cuts, low, top_value):
    def one(dim, blocks):
        steps = jax.random.uniform(jax.random.fold_in(jax.random.fold_in(rng, 6), dim), (blocks,), jnp.float32, low / len(cuts), top_value / len(cuts))
        return jnp.repeat(jnp.exp(steps), extent[dim] // blocks).reshape((-1,) + (1,) * (len(extent) - dim - 1))

    factor_of = one(*cuts[0])
    for cut in cuts[1:]:
        factor_of = factor_of * one(*cut)
    return factor_of


def normal_values(own_key, dims, scale, most, shards=(), held_as=jnp.bfloat16):
    result = scale * jax.random.normal(own_key, dims, jnp.float32)
    if shards:
        result = result * block_scale(own_key, dims, shards, -0.22, 0.18)
    return jnp.clip(result, -most, most).astype(held_as)


def setup_inputs(seed: int = 0) -> dict:
    splits = jax.random.split(jax.random.key(seed), 10)
    return {
        "right_side": draw_right_side(jax.random.fold_in(splits[9], 71), 0),
        "diag_blocks": draw_diag_blocks(jax.random.fold_in(splits[9], 71), 0),
        "off_blocks": draw_off_blocks(jax.random.fold_in(splits[9], 71), 0),
        "cell_inverse": draw_cell_inverse(jax.random.fold_in(splits[9], 71), 0),
        "send_cells": draw_send_cells(jax.random.fold_in(splits[9], 71), 0),
        "recv_index": draw_recv_index(jax.random.fold_in(splits[9], 71), 0),
        "seg_count": draw_seg_count(jax.random.fold_in(splits[9], 71), 0),
        "span_inverse": draw_span_inverse(jax.random.fold_in(splits[9], 71), 0),
        "span_couple": normal_values(splits[8], (NCHUNK, 9, WELLS), 0.5, 3.0, ((2, 32),), jnp.float32),
    }


def block_apply(matrix, vector):
    return jnp.stack([matrix[3 * a] * vector[0] + matrix[3 * a + 1] * vector[1] + matrix[3 * a + 2] * vector[2] for a in range(3)])

def apply_jacobian(field, diag_blocks, off_blocks):
    padded = jnp.pad(field, ((0, 0), (1, 1), (1, 1), (1, 1)))
    beside = [padded[:, :-2, 1:-1, 1:-1], padded[:, 2:, 1:-1, 1:-1], padded[:, 1:-1, :-2, 1:-1], padded[:, 1:-1, 2:, 1:-1], padded[:, 1:-1, 1:-1, :-2], padded[:, 1:-1, 1:-1, 2:]]
    total = block_apply(diag_blocks, field)
    for face in range(6):
        total = total + block_apply(off_blocks[face], beside[face])
    return total

def chain_solve(segments, span_inverse, span_couple):
    well_count = span_couple.shape[2]
    width = 3 * SPAN
    blocks = segments.reshape(3, well_count, NCHUNK, SPAN).transpose(2, 3, 0, 1).reshape(NCHUNK, width, well_count)
    inverse = span_inverse.reshape(NCHUNK, width, well_count, width)

    def advance(carry, packed):
        block_rhs, block_inverse, couple = packed
        first = block_rhs[:3] - block_apply(couple, carry)
        block_rhs = jnp.concatenate([first, block_rhs[3:]], axis=0)
        solved = lax.optimization_barrier(jnp.sum(block_inverse * block_rhs[:, :, None], axis=0)).T
        return (solved[width - 3:], solved)
    start = jnp.zeros((3, well_count), jnp.float32)
    _, solved = lax.scan(advance, start, (blocks, inverse, span_couple))
    return solved.reshape(NCHUNK, SPAN, 3, well_count).transpose(2, 3, 0, 1).reshape(3, well_count * MAXSEG)

def to_devices(field):
    count = field.shape[0]
    parts = field.reshape(count, N_GX, CX, N_GY, CY, NZ).transpose(0, 1, 3, 2, 4, 5)
    return parts.reshape(count, N_GX * N_GY, CX * CY * NZ)

def from_devices(parts):
    count = parts.shape[0]
    return parts.reshape(count, N_GX, N_GY, CX, CY, NZ).transpose(0, 1, 3, 2, 4, 5).reshape(count, NX, NY, NZ)

def neighbourhood(sent):
    count = sent.shape[0]
    grid = sent.reshape(count, N_GX, N_GY, SLOTS)
    padded = jnp.pad(grid, ((0, 0), (1, 1), (1, 1), (0, 0)))
    pieces = [padded[:, 1 + a:1 + a + N_GX, 1 + b:1 + b + N_GY] for a in (-1, 0, 1) for b in (-1, 0, 1)]
    return jnp.stack(pieces, axis=3).reshape(count, N_GX * N_GY, 9 * SLOTS)

def give_back(slots):
    count = slots.shape[0]
    grid = slots.reshape(count, N_GX, N_GY, 9, SLOTS)
    padded = jnp.pad(grid, ((0, 0), (1, 1), (1, 1), (0, 0), (0, 0)))
    total = jnp.zeros((count, N_GX, N_GY, SLOTS), jnp.float32)
    for a in (-1, 0, 1):
        for b in (-1, 0, 1):
            place = (1 - a) * 3 + (1 - b)
            total = total + padded[:, 1 + a:1 + a + N_GX, 1 + b:1 + b + N_GY, place]
    return total.reshape(count, N_GX * N_GY, SLOTS)

def least_squares(top_first, sub_first, top_second, mid_second, sub_second, beta):
    gram_first = top_first * top_first + sub_first * sub_first
    gram_cross = top_first * top_second + sub_first * mid_second
    gram_second = top_second * top_second + mid_second * mid_second + sub_second * sub_second
    determinant = gram_first * gram_second - gram_cross * gram_cross
    weight_one = (gram_second * beta * top_first - gram_cross * beta * top_second) / determinant
    weight_two = (gram_first * beta * top_second - gram_cross * beta * top_first) / determinant
    return (weight_one, weight_two)

def reference(right_side, diag_blocks, off_blocks, cell_inverse, send_cells, recv_index, seg_count, span_inverse, span_couple):
    devices = N_GX * N_GY
    cell_blocks = to_devices(diag_blocks)
    index = recv_index.reshape(devices, WELLS_DEV * MAXSEG)
    alive = (jnp.arange(MAXSEG)[None, :] < seg_count[:, None]).reshape(1, devices, WELLS_DEV * MAXSEG)
    sent_blocks = jnp.take_along_axis(cell_blocks, send_cells[None], axis=2)
    owner_blocks = jnp.take_along_axis(neighbourhood(sent_blocks), index[None], axis=2)

    def precondition(vector):
        parts = to_devices(vector)
        picked = jnp.take_along_axis(parts, send_cells[None], axis=2)
        arrived = jnp.take_along_axis(neighbourhood(picked), index[None], axis=2)
        segments = jnp.where(alive, block_apply(owner_blocks, arrived), 0.0)
        solved = chain_solve(segments.reshape(3, -1), span_inverse, span_couple).reshape(3, devices, -1)
        solved = jnp.where(alive, solved, 0.0)
        slots = jax.vmap(lambda where_to, values: jnp.zeros((3, 9 * SLOTS), jnp.float32).at[:, where_to].add(values), in_axes=(0, 1), out_axes=1)(index, solved)
        returned = give_back(slots)
        placed = jax.vmap(lambda cells, values: jnp.zeros((3, CX * CY * NZ), jnp.float32).at[:, cells].add(values), in_axes=(0, 1), out_axes=1)(send_cells, returned)
        return block_apply(cell_inverse, vector) + from_devices(placed)
    beta = jnp.sqrt(jnp.sum(right_side * right_side))
    basis = [right_side / beta]
    search = []
    entries = []
    for column in range(2):
        direction = precondition(basis[column])
        search.append(direction)
        image = apply_jacobian(direction, diag_blocks, off_blocks)
        coeffs = []
        for vector in basis:
            coeff = jnp.sum(image * vector)
            image = image - coeff * vector
            coeffs.append(coeff)
        size = jnp.sqrt(jnp.sum(image * image))
        entries.append((coeffs, size))
        basis.append(image / size)
    top_first, sub_first = (entries[0][0][0], entries[0][1])
    top_second, mid_second, sub_second = (entries[1][0][0], entries[1][0][1], entries[1][1])
    weight_one, weight_two = least_squares(top_first, sub_first, top_second, mid_second, sub_second, beta)
    solution = weight_one * search[0] + weight_two * search[1]
    residual = (beta - top_first * weight_one - top_second * weight_two) * basis[0] - (sub_first * weight_one + mid_second * weight_two) * basis[1] - sub_second * weight_two * basis[2]
    return (solution, residual)
```

```python
import functools

import jax
import jax.numpy as jnp
from jax import lax
from jax.experimental import pallas as pl
from jax.experimental.pallas import tpu as pltpu
from jax.sharding import PartitionSpec as P

LANES = 128
F32 = jnp.float32
BF16 = jnp.bfloat16


def round_up(value, unit):
    return -(-value // unit) * unit


def iota(shape, dim):
    return lax.broadcasted_iota(jnp.int32, shape, dim)


def split(value, pieces):
    out = []
    for _ in range(pieces - 1):
        piece = value.astype(BF16)
        out.append(piece)
        value = value - piece.astype(F32)
    out.append(value.astype(BF16))
    return out


def mm(left, right, trans=False):
    dims = (((1,), (1 if trans else 0,)), ((), ()))
    return lax.dot_general(left, right, dims, preferred_element_type=F32)


def mm_exact(value, choice):
    total = None
    for piece in split(value, 3):
        part = mm(piece, choice)
        total = part if total is None else total + part
    return total


def ones_where(mask):
    return jnp.where(mask, 1.0, 0.0).astype(BF16)


def call(kernel, outs, scratch=(), flops=0):
    def run(*args):
        moved = sum(a.size * 4 for a in args) + sum(
            4 * functools.reduce(lambda p, q: p * q, o) for o in outs
        )
        return pl.pallas_call(
            kernel,
            out_shape=[jax.ShapeDtypeStruct(o, F32) for o in outs],
            in_specs=[pl.BlockSpec(memory_space=pltpu.VMEM)] * len(args),
            out_specs=[pl.BlockSpec(memory_space=pltpu.VMEM)] * len(outs),
            scratch_shapes=[pltpu.VMEM(s, t) for s, t in scratch],
            cost_estimate=pl.CostEstimate(
                flops=flops, bytes_accessed=moved, transcendentals=0
            ),
            compiler_params=pltpu.CompilerParams(vmem_limit_bytes=40 * 2**20),
        )(*args)

    return run


def chunk_of(slots):
    for groups in (5, 4, 3, 2, 1):
        if slots % (groups * LANES) == 0:
            return groups * LANES


def pick(field, idx_ref, out_ref):
    _, rows, depth = field.shape
    slots = idx_ref.shape[1]
    blocks = slots // LANES
    chunk = chunk_of(slots)
    flat = field.reshape(3 * rows, depth)
    left = jnp.concatenate(split(flat, 2), axis=0)
    for start in range(0, slots, chunk):
        row = idx_ref[0:1, start : start + chunk]
        deep = idx_ref[1:2, start : start + chunk]
        right = ones_where(iota((depth, chunk), 0) == deep)
        found = mm(left, right)
        found = found[: 3 * rows] + found[3 * rows :]
        here = iota((rows, chunk), 0) == row
        for comp in range(3):
            part = jnp.where(here, found[comp * rows : (comp + 1) * rows], 0.0)
            line = jnp.sum(part, axis=0, keepdims=True)
            for piece in range(chunk // LANES):
                at = comp * blocks + start // LANES + piece
                out_ref[at : at + 1, :] = line[:, piece * LANES : (piece + 1) * LANES]
    pad = out_ref.shape[0] - 3 * blocks
    if pad:
        out_ref[3 * blocks :, :] = jnp.zeros((pad, LANES), F32)


def times_diag(d_ref, field):
    nx, ny, nz = d_ref.shape[1:]
    return jnp.stack(
        [
            sum(d_ref[3 * a + b] * field[b] for b in range(3)).reshape(nx * ny, nz)
            for a in range(3)
        ]
    )


def first_kernel(idx_ref, v_ref, d_ref, out_ref):
    pick(times_diag(d_ref, [v_ref[b] for b in range(3)]), idx_ref, out_ref)


def spread_matrix(wells, width):
    shape = (wells, wells * width)
    gap = iota(shape, 1) - width * iota(shape, 0)
    return ones_where((gap >= 0) & (gap < width))


def last_matrix(wells, width, comp):
    shape = (wells * width, wells)
    return ones_where(iota(shape, 0) == width * iota(shape, 1) + (width - 3 + comp))


def prep_kernel(g_ref, couple_ref, h_ref, e_ref, apart_ref, part_ref):
    chunks, width, span_all = g_ref.shape
    wells = couple_ref.shape[2]
    span = width // 3
    for lane in range(0, span_all, LANES):
        part_ref[...] = g_ref[:, :, lane : lane + LANES]
        for comp in range(3):
            apart_ref[comp, :, :, lane : lane + LANES] = part_ref[
                :, pl.ds(comp, span, stride=3), :
            ]
    spread = spread_matrix(wells, width)
    heads = [g_ref[:, d, :] for d in range(3)]
    for b in range(3):
        total = sum(
            heads[d] * mm_exact(couple_ref[3 * d + b], spread)[:chunks] for d in range(3)
        )
        h_ref[b] = jnp.zeros(h_ref.shape[1:], F32)
        h_ref[b, :chunks, :] = total
        full = h_ref[b]
        for a in range(3):
            e_ref[3 * a + b] = mm_exact(full, last_matrix(wells, width, a))


def solve_kernel(
    idx_ref, low_ref, mid_ref, high_ref, g_ref, h_ref, e_ref,
    down_ref, keep_ref, up_ref,
    pool_ref, r_ref, q_ref, tail_ref, p_ref, y_ref, ohr_ref, w_ref,
):
    _, chunks, span, span_all = g_ref.shape
    width = 3 * span
    wells = span_all // width
    slots = idx_ref.shape[1]
    blocks = slots // LANES
    rows = pool_ref.shape[1]
    tile = low_ref.shape[0] // 3
    group = wells * span
    pool_ref[:, 9 * blocks :, :] = jnp.zeros((3, rows - 9 * blocks, LANES), F32)
    for a in range(3):
        for b, src in enumerate((low_ref, mid_ref, high_ref)):
            for comp in range(3):
                at = (a * 3 + b) * blocks
                pool_ref[comp, at : at + blocks, :] = src[
                    a * tile + comp * blocks : a * tile + (comp + 1) * blocks, :
                ]
    pooled = pool_ref[...].reshape(3 * rows, LANES)
    left = jnp.concatenate(split(pooled, 2), axis=1)
    size = chunk_of(slots)
    r_ref[...] = jnp.zeros(r_ref.shape, F32)
    for start in range(0, slots, size):
        high = idx_ref[2:3, start : start + size]
        low = idx_ref[3:4, start : start + size]
        right = ones_where((iota((2 * LANES, size), 0) & (LANES - 1)) == low)
        found = mm(left, right)
        here = iota((rows, size), 0) == high
        ohr_ref[:, start : start + size] = ones_where(here)
        for comp in range(3):
            part = jnp.where(here, found[comp * rows : (comp + 1) * rows], 0.0)
            line = jnp.sum(part, axis=0, keepdims=True)
            for piece in range(size // group):
                at = start // group + piece
                r_ref[comp, at : at + 1, :] = line[:, piece * group : (piece + 1) * group]
    two = (2 * group, span_all)
    well_of = lax.shift_right_logical(iota(two, 0) & (group - 1), (span - 1).bit_length())
    gap = iota(two, 1) - width * well_of
    spread = ones_where((gap >= 0) & (gap < width))
    own = (iota((span, group), 1) & (span - 1)) == iota((span, group), 0)
    total = None
    for comp in range(3):
        values = r_ref[comp][:chunks]
        wide = jnp.where(own[None], values[:, None, :], 0.0).reshape(chunks * span, group)
        lifted = mm(jnp.concatenate(split(wide, 2), axis=1), spread)
        lifted = lifted.reshape(chunks, span, span_all)
        part = g_ref[comp] * lifted
        total = part if total is None else total + part
    q_ref[...] = jnp.zeros(q_ref.shape, F32)
    q_ref[:chunks, :] = jnp.sum(total, axis=1)
    plain = q_ref[...]
    for a in range(3):
        tail_ref[a] = mm_exact(plain, last_matrix(wells, width, a))
    p_ref[...] = jnp.zeros(p_ref.shape, F32)
    state = [jnp.zeros((1, wells), F32)] * 3
    for c in range(chunks - 1):
        state = [
            tail_ref[a, c : c + 1, :]
            - (
                e_ref[3 * a, c : c + 1, :] * state[0]
                + e_ref[3 * a + 1, c : c + 1, :] * state[1]
                + e_ref[3 * a + 2, c : c + 1, :] * state[2]
            )
            for a in range(3)
        ]
        for a in range(3):
            p_ref[a, c + 1 : c + 2, :] = state[a]
    wide_well = spread_matrix(wells, width)
    for b in range(3):
        plain = plain - h_ref[b] * mm_exact(p_ref[b], wide_well)
    square = (span_all, span_all)
    lane = iota((1, span_all), 1)
    comp_of = lax.div(lane, jnp.int32(group))
    rest = lax.rem(lane, jnp.int32(group))
    source = width * lax.div(rest, jnp.int32(span)) + 3 * lax.rem(rest, jnp.int32(span)) + comp_of
    y_ref[...] = mm_exact(plain, ones_where(iota(square, 0) == source))
    for c in range(chunks):
        low = idx_ref[3:4, c * group : (c + 1) * group]
        match = iota((LANES, group), 0) == low
        for comp in range(3):
            value = y_ref[c : c + 1, comp * group : (comp + 1) * group]
            for place, piece in enumerate(split(value, 2)):
                at = (place * 3 + comp) * LANES
                w_ref[at : at + LANES, c * group : (c + 1) * group] = jnp.where(
                    match, piece.astype(F32), 0.0
                ).astype(BF16)
    spread_out = mm(ohr_ref[...], w_ref[...], trans=True)
    spread_out = spread_out[:, : 3 * LANES] + spread_out[:, 3 * LANES :]
    pool_ref[0] = spread_out[:, :LANES]
    pool_ref[1] = spread_out[:, LANES : 2 * LANES]
    pool_ref[2] = spread_out[:, 2 * LANES :]
    for a, dst in enumerate((down_ref, keep_ref, up_ref)):
        dst[...] = jnp.zeros(dst.shape, F32)
        for b in range(3):
            for comp in range(3):
                at = (a * 3 + b) * blocks
                dst[b * tile + comp * blocks : b * tile + (comp + 1) * blocks, :] = pool_ref[
                    comp, at : at + blocks, :
                ]


def add_kernel(x_ref, y_ref, z_ref, low_ref, mid_ref, high_ref):
    tile = low_ref.shape[0]
    for place, dst in enumerate((low_ref, mid_ref, high_ref)):
        part = slice(place * tile, (place + 1) * tile)
        dst[...] = x_ref[part, :] + y_ref[part, :] + z_ref[part, :]


def place_kernel(
    idx_ref, v_ref, inv_ref, x_ref, y_ref, z_ref,
    out_ref, xl_ref, xh_ref, yl_ref, yh_ref,
    left_ref, right_ref,
):
    nx, ny, nz = v_ref.shape[1:]
    rows = nx * ny
    slots = idx_ref.shape[1]
    blocks = slots // LANES
    back = x_ref[...] + y_ref[...] + z_ref[...]
    pieces = [piece.astype(F32) for piece in split(back, 2)]
    for block in range(blocks):
        lanes = slice(block * LANES, (block + 1) * LANES)
        here = iota((rows, LANES), 0) == idx_ref[0:1, lanes]
        right_ref[:, lanes] = ones_where(iota((nz, LANES), 0) == idx_ref[1:2, lanes])
        for place, piece in enumerate(pieces):
            for comp in range(3):
                at = comp * blocks + block
                group = (place * 3 + comp) * rows
                left_ref[group : group + rows, lanes] = jnp.where(
                    here, piece[at : at + 1, :], 0.0
                ).astype(BF16)
    placed = mm(left_ref[...], right_ref[...], trans=True)
    placed = placed[: 3 * rows] + placed[3 * rows :]
    for a in range(3):
        own = sum(inv_ref[3 * a + b] * v_ref[b] for b in range(3))
        out_ref[a] = own + placed[a * rows : (a + 1) * rows].reshape(nx, ny, nz)
        xl_ref[a] = out_ref[a, 0]
        xh_ref[a] = out_ref[a, nx - 1]
        yl_ref[a] = out_ref[a, :, 0, :]
        yh_ref[a] = out_ref[a, :, ny - 1, :]


def jacobian(z_ref, xl_ref, xh_ref, yl_ref, yh_ref, d_ref, off_ref, store):
    nx, ny, nz = z_ref.shape[1:]
    row = iota((ny, nz), 0)
    lane = iota((ny, nz), 1)
    for x in range(nx):
        beside = []
        for b in range(3):
            own = z_ref[b, x]
            beside.append(
                [
                    z_ref[b, x - 1] if x else xl_ref[b],
                    z_ref[b, x + 1] if x < nx - 1 else xh_ref[b],
                    jnp.where(row == 0, yl_ref[b, x : x + 1, :], pltpu.roll(own, 1, 0)),
                    jnp.where(row == ny - 1, yh_ref[b, x : x + 1, :], pltpu.roll(own, ny - 1, 0)),
                    jnp.where(lane == 0, 0.0, pltpu.roll(own, 1, 1)),
                    jnp.where(lane == nz - 1, 0.0, pltpu.roll(own, nz - 1, 1)),
                ]
            )
        for a in range(3):
            total = sum(d_ref[3 * a + b, x] * z_ref[b, x] for b in range(3))
            for face in range(6):
                for b in range(3):
                    total = total + off_ref[face, 3 * a + b, x] * beside[b][face]
            store(a, x, total)


def next_kernel(
    idx_ref, z_ref, xl_ref, xh_ref, yl_ref, yh_ref, d_ref, off_ref, v_ref,
    w_ref, t_ref, out_ref,
):
    def store(a, x, value):
        w_ref[a, x] = value
        t_ref[a, x] = value - v_ref[a, x]

    jacobian(z_ref, xl_ref, xh_ref, yl_ref, yh_ref, d_ref, off_ref, store)
    pick(times_diag(d_ref, [t_ref[b] for b in range(3)]), idx_ref, out_ref)


def gram_kernel(
    z_ref, xl_ref, xh_ref, yl_ref, yh_ref, d_ref, off_ref, v_ref, w1_ref,
    w_ref, sums_ref,
):
    def store(a, x, value):
        w_ref[a, x] = value

    jacobian(z_ref, xl_ref, xh_ref, yl_ref, yh_ref, d_ref, off_ref, store)
    one, two, rhs = w1_ref[...], w_ref[...], v_ref[...]
    top_one = jnp.maximum(jnp.max(jnp.abs(one)), 1e-30)
    top_two = jnp.maximum(jnp.max(jnp.abs(two)), 1e-30)
    one = one * (1.0 / jnp.full((1, 1), top_one))
    two = two * (1.0 / jnp.full((1, 1), top_two))
    sums = [
        jnp.sum(one * one), jnp.sum(one * two), jnp.sum(two * two),
        jnp.sum(one * rhs), jnp.sum(two * rhs), top_one, top_two,
    ]
    line = iota(sums_ref.shape, 0)
    total = jnp.zeros(sums_ref.shape, F32)
    for place, value in enumerate(sums):
        total = jnp.where(line == place, value, total)
    sums_ref[...] = total


def final_kernel(
    all_ref, v_ref, z1_ref, z2_ref, w1_ref, w2_ref, sol_ref, res_ref
):
    every = [all_ref[:, place, :] for place in range(7)]
    top_one = jnp.max(every[5], axis=0, keepdims=True)
    top_two = jnp.max(every[6], axis=0, keepdims=True)
    one = every[5] / top_one
    two = every[6] / top_two

    def add(value):
        return jnp.sum(value, axis=0, keepdims=True)

    g11 = add(every[0] * one * one)
    g12 = add(every[1] * one * two)
    g22 = add(every[2] * two * two)
    r1 = add(every[3] * one)
    r2 = add(every[4] * two)
    det = g11 * g22 - g12 * g12
    y1 = ((g22 * r1 - g12 * r2) / det / top_one)[:, :1]
    y2 = ((g11 * r2 - g12 * r1) / det / top_two)[:, :1]
    sol_ref[...] = y1 * z1_ref[...] + y2 * z2_ref[...]
    res_ref[...] = v_ref[...] - y1 * w1_ref[...] - y2 * w2_ref[...]


def shift(value, axis, step):
    count = lax.axis_size(axis)
    pairs = [(i, i + step) for i in range(count) if 0 <= i + step < count]
    return lax.ppermute(value, axis, pairs)


def body(
    right_side,
    diag_blocks,
    off_blocks,
    cell_inverse,
    send_cells,
    recv_index,
    seg_count,
    span_inverse,
    span_couple,
):
    _, nx, ny, nz = right_side.shape
    slots = send_cells.shape[1]
    wells, longest = recv_index.shape
    chunks, width, span_all = span_inverse.shape
    span = width // 3
    blocks = slots // LANES
    tile = round_up(3 * blocks, 16)
    rows = round_up(9 * blocks, 16)
    tall = round_up(chunks, 16)
    live = jnp.arange(longest)[None, :] < seg_count[:, None]
    index = jnp.where(live, recv_index, -1)
    index = index.reshape(wells, chunks, span).transpose(1, 0, 2).reshape(1, wells * longest)
    idx = jnp.concatenate(
        [send_cells // nz, send_cells % nz, index >> 7, index & (LANES - 1)], axis=0
    )
    couple = jnp.pad(span_couple.transpose(1, 0, 2), ((0, 0), (0, tall - chunks), (0, 0)))
    h, e, apart = call(
        prep_kernel,
        [(3, tall, span_all), (9, tall, wells), (3, chunks, span, span_all)],
        [((chunks, width, LANES), F32)],
    )(span_inverse, couple)

    def precondition(vector, picked):
        left, right = shift(picked, "gx", 1), shift(picked, "gx", -1)
        mid = jnp.concatenate([left, picked, right], axis=0)
        low, high = shift(mid, "gy", 1), shift(mid, "gy", -1)
        down, keep, up = call(
            solve_kernel,
            [(3 * tile, LANES)] * 3,
            [
                ((3, rows, LANES), F32),
                ((3, tall, wells * span), F32),
                ((tall, span_all), F32),
                ((3, tall, wells), F32),
                ((3, tall, wells), F32),
                ((tall, span_all), F32),
                ((rows, slots), BF16),
                ((6 * LANES, slots), BF16),
            ],
            flops=4 * 10**9,
        )(idx, low, mid, high, apart, h, e)
        down, up = shift(down, "gx", -1), shift(up, "gx", 1)
        low, keep, high = call(add_kernel, [(tile, LANES)] * 3)(down, keep, up)
        low, high = shift(low, "gy", -1), shift(high, "gy", 1)
        z, xl, xh, yl, yh = call(
            place_kernel,
            [(3, nx, ny, nz), (3, ny, nz), (3, ny, nz), (3, nx, nz), (3, nx, nz)],
            [((6 * nx * ny, slots), BF16), ((nz, slots), BF16)],
            flops=10**9,
        )(idx, vector, cell_inverse, low, keep, high)
        xl, xh = shift(xh, "gx", 1), shift(xl, "gx", -1)
        yl, yh = shift(yh, "gy", 1), shift(yl, "gy", -1)
        return z, (xl, xh, yl, yh)

    field = right_side.shape
    (picked,) = call(first_kernel, [(tile, LANES)], flops=10**9)(idx, right_side, diag_blocks)
    z1, faces = precondition(right_side, picked)
    w1, turned, picked = call(next_kernel, [field, field, (tile, LANES)], flops=10**9)(
        idx, z1, *faces, diag_blocks, off_blocks, right_side
    )
    z2, faces = precondition(turned, picked)
    w2, sums = call(gram_kernel, [field, (8, LANES)])(
        z2, *faces, diag_blocks, off_blocks, right_side, w1
    )
    every = lax.all_gather(sums, ("gx", "gy"))
    return tuple(
        call(final_kernel, [field, field])(every, right_side, z1, z2, w1, w2)
    )


def solution(mesh):
    return jax.shard_map(
        body,
        mesh=mesh,
        in_specs=(
            P(None, "gx", "gy", None),
            P(None, "gx", "gy", None),
            P(None, None, "gx", "gy", None),
            P(None, "gx", "gy", None),
            P(("gx", "gy"), None),
            P(("gx", "gy"), None),
            P(("gx", "gy")),
            P(None, None, ("gx", "gy")),
            P(None, None, ("gx", "gy")),
        ),
        out_specs=(P(None, "gx", "gy", None), P(None, "gx", "gy", None)),
        check_vma=False,
    )
```

```python
import functools

import jax
import jax.numpy as jnp
from jax import lax
from jax.experimental import pallas as pl
from jax.experimental.pallas import tpu as pltpu
from jax.sharding import PartitionSpec as P

LANES = 128
F32 = jnp.float32
BF16 = jnp.bfloat16


def round_up(value, unit):
    return -(-value // unit) * unit


def iota(shape, dim):
    return lax.broadcasted_iota(jnp.int32, shape, dim)


def split(value, pieces):
    out = []
    for _ in range(pieces - 1):
        piece = value.astype(BF16)
        out.append(piece)
        value = value - piece.astype(F32)
    out.append(value.astype(BF16))
    return out


def mm(left, right, trans=False):
    dims = (((1,), (1 if trans else 0,)), ((), ()))
    return lax.dot_general(left, right, dims, preferred_element_type=F32)


def mm_exact(value, choice):
    total = None
    for piece in split(value, 3):
        part = mm(piece, choice)
        total = part if total is None else total + part
    return total


def ones_where(mask):
    return jnp.where(mask, 1.0, 0.0).astype(BF16)


def call(kernel, outs, scratch=(), flops=0, scalars=0):
    def run(*args):
        moved = sum(a.size * 4 for a in args) + sum(
            4 * functools.reduce(lambda p, q: p * q, o) for o in outs
        )
        return pl.pallas_call(
            kernel,
            out_shape=[jax.ShapeDtypeStruct(o, F32) for o in outs],
            in_specs=[pl.BlockSpec(memory_space=pltpu.SMEM)] * scalars
            + [pl.BlockSpec(memory_space=pltpu.VMEM)] * (len(args) - scalars),
            out_specs=[pl.BlockSpec(memory_space=pltpu.VMEM)] * len(outs),
            scratch_shapes=[pltpu.VMEM(s, t) for s, t in scratch],
            cost_estimate=pl.CostEstimate(
                flops=flops, bytes_accessed=moved, transcendentals=0
            ),
            compiler_params=pltpu.CompilerParams(vmem_limit_bytes=40 * 2**20),
        )(*args)

    return run


def chunk_of(slots):
    for groups in (5, 4, 3, 2, 1):
        if slots % (groups * LANES) == 0:
            return groups * LANES


def row_and_depth(cells, nz):
    if nz & (nz - 1) == 0:
        return lax.shift_right_logical(cells, nz.bit_length() - 1), cells & (nz - 1)
    return lax.div(cells, jnp.int32(nz)), lax.rem(cells, jnp.int32(nz))


def pick(field, cells_ref, out_ref):
    _, rows, depth = field.shape
    slots = cells_ref.shape[1]
    blocks = slots // LANES
    chunk = chunk_of(slots)
    flat = field.reshape(3 * rows, depth)
    left = jnp.concatenate(split(flat, 2), axis=0)
    for start in range(0, slots, chunk):
        row, deep = row_and_depth(cells_ref[:, start : start + chunk], depth)
        right = ones_where(iota((depth, chunk), 0) == deep)
        found = mm(left, right)
        found = found[: 3 * rows] + found[3 * rows :]
        here = iota((rows, chunk), 0) == row
        for comp in range(3):
            part = jnp.where(here, found[comp * rows : (comp + 1) * rows], 0.0)
            line = jnp.sum(part, axis=0, keepdims=True)
            for piece in range(chunk // LANES):
                at = comp * blocks + start // LANES + piece
                out_ref[at : at + 1, :] = line[:, piece * LANES : (piece + 1) * LANES]
    pad = out_ref.shape[0] - 3 * blocks
    if pad:
        out_ref[3 * blocks :, :] = jnp.zeros((pad, LANES), F32)


def times_diag(d_ref, field):
    nx, ny, nz = d_ref.shape[1:]
    return jnp.stack(
        [
            sum(d_ref[3 * a + b] * field[b] for b in range(3)).reshape(nx * ny, nz)
            for a in range(3)
        ]
    )


def first_kernel(cells_ref, v_ref, d_ref, out_ref):
    pick(times_diag(d_ref, [v_ref[b] for b in range(3)]), cells_ref, out_ref)


def spread_matrix(wells, width):
    shape = (wells, wells * width)
    gap = iota(shape, 1) - width * iota(shape, 0)
    return ones_where((gap >= 0) & (gap < width))


def last_matrix(wells, width, comp):
    shape = (wells * width, wells)
    return ones_where(iota(shape, 0) == width * iota(shape, 1) + (width - 3 + comp))


def prep_kernel(g_ref, couple_ref, h_ref, e_ref, apart_ref, part_ref):
    chunks, width, span_all = g_ref.shape
    wells = couple_ref.shape[2]
    span = width // 3
    for lane in range(0, span_all, LANES):
        part_ref[...] = g_ref[:, :, lane : lane + LANES]
        for comp in range(3):
            apart_ref[comp, :, :, lane : lane + LANES] = part_ref[
                :, pl.ds(comp, span, stride=3), :
            ]
    spread = spread_matrix(wells, width)
    heads = [g_ref[:, d, :] for d in range(3)]
    for b in range(3):
        total = sum(
            heads[d] * mm_exact(couple_ref[3 * d + b], spread)[:chunks] for d in range(3)
        )
        h_ref[b] = jnp.zeros(h_ref.shape[1:], F32)
        h_ref[b, :chunks, :] = total
        full = h_ref[b]
        for a in range(3):
            e_ref[3 * a + b] = mm_exact(full, last_matrix(wells, width, a))


def solve_kernel(
    odd_ref, idx_ref, own_ref, even_ref, next_ref, g_ref, h_ref, e_ref,
    keep_ref, to_even_ref, to_next_ref,
    pool_ref, r_ref, q_ref, tail_ref, p_ref, y_ref, ohr_ref, w_ref,
):
    _, chunks, span, span_all = g_ref.shape
    width = 3 * span
    wells = span_all // width
    slots = idx_ref.shape[1]
    blocks = slots // LANES
    rows = pool_ref.shape[1]
    tile = own_ref.shape[0] // 3
    group = wells * span
    odd_x, odd_y = odd_ref[0] == 1, odd_ref[1] == 1
    pool_ref[:, 9 * blocks :, :] = jnp.zeros((3, rows - 9 * blocks, LANES), F32)
    own, even, following = own_ref[...], even_ref[...], next_ref[...]
    columns = (
        jnp.where(odd_y, even, following), own, jnp.where(odd_y, following, even)
    )
    for b, column in enumerate(columns):
        own, even, following = column[:tile], column[tile : 2 * tile], column[2 * tile :]
        parts = (jnp.where(odd_x, even, following), own, jnp.where(odd_x, following, even))
        for a, part in enumerate(parts):
            for comp in range(3):
                at = (a * 3 + b) * blocks
                pool_ref[comp, at : at + blocks, :] = part[
                    comp * blocks : (comp + 1) * blocks
                ]
    pooled = pool_ref[...].reshape(3 * rows, LANES)
    left = jnp.concatenate(split(pooled, 2), axis=1)
    size = chunk_of(slots)
    r_ref[...] = jnp.zeros(r_ref.shape, F32)
    for start in range(0, slots, size):
        place = idx_ref[:, start : start + size]
        high = lax.shift_right_arithmetic(place, LANES.bit_length() - 1)
        low = place & (LANES - 1)
        right = ones_where((iota((2 * LANES, size), 0) & (LANES - 1)) == low)
        found = mm(left, right)
        here = iota((rows, size), 0) == high
        ohr_ref[:, start : start + size] = ones_where(here)
        for comp in range(3):
            part = jnp.where(here, found[comp * rows : (comp + 1) * rows], 0.0)
            line = jnp.sum(part, axis=0, keepdims=True)
            for piece in range(size // group):
                at = start // group + piece
                r_ref[comp, at : at + 1, :] = line[:, piece * group : (piece + 1) * group]
    two = (2 * group, span_all)
    well_of = lax.shift_right_logical(iota(two, 0) & (group - 1), (span - 1).bit_length())
    gap = iota(two, 1) - width * well_of
    spread = ones_where((gap >= 0) & (gap < width))
    own = (iota((span, group), 1) & (span - 1)) == iota((span, group), 0)
    total = None
    for comp in range(3):
        values = r_ref[comp][:chunks]
        wide = jnp.where(own[None], values[:, None, :], 0.0).reshape(chunks * span, group)
        lifted = mm(jnp.concatenate(split(wide, 2), axis=1), spread)
        lifted = lifted.reshape(chunks, span, span_all)
        part = g_ref[comp] * lifted
        total = part if total is None else total + part
    q_ref[...] = jnp.zeros(q_ref.shape, F32)
    q_ref[:chunks, :] = jnp.sum(total, axis=1)
    plain = q_ref[...]
    for a in range(3):
        tail_ref[a] = mm_exact(plain, last_matrix(wells, width, a))
    p_ref[...] = jnp.zeros(p_ref.shape, F32)
    state = [jnp.zeros((1, wells), F32)] * 3
    for c in range(chunks - 1):
        state = [
            tail_ref[a, c : c + 1, :]
            - (
                e_ref[3 * a, c : c + 1, :] * state[0]
                + e_ref[3 * a + 1, c : c + 1, :] * state[1]
                + e_ref[3 * a + 2, c : c + 1, :] * state[2]
            )
            for a in range(3)
        ]
        for a in range(3):
            p_ref[a, c + 1 : c + 2, :] = state[a]
    wide_well = spread_matrix(wells, width)
    for b in range(3):
        plain = plain - h_ref[b] * mm_exact(p_ref[b], wide_well)
    square = (span_all, span_all)
    lane = iota((1, span_all), 1)
    comp_of = lax.div(lane, jnp.int32(group))
    rest = lax.rem(lane, jnp.int32(group))
    source = width * lax.div(rest, jnp.int32(span)) + 3 * lax.rem(rest, jnp.int32(span)) + comp_of
    y_ref[...] = mm_exact(plain, ones_where(iota(square, 0) == source))
    for c in range(chunks):
        low = idx_ref[:, c * group : (c + 1) * group] & (LANES - 1)
        match = iota((LANES, group), 0) == low
        for comp in range(3):
            value = y_ref[c : c + 1, comp * group : (comp + 1) * group]
            for place, piece in enumerate(split(value, 2)):
                at = (place * 3 + comp) * LANES
                w_ref[at : at + LANES, c * group : (c + 1) * group] = jnp.where(
                    match, piece.astype(F32), 0.0
                ).astype(BF16)
    spread_out = mm(ohr_ref[...], w_ref[...], trans=True)
    spread_out = spread_out[:, : 3 * LANES] + spread_out[:, 3 * LANES :]
    pool_ref[0] = spread_out[:, :LANES]
    pool_ref[1] = spread_out[:, LANES : 2 * LANES]
    pool_ref[2] = spread_out[:, 2 * LANES :]
    for dst in (keep_ref, to_even_ref, to_next_ref):
        dst[...] = jnp.zeros(dst.shape, F32)
    for a in range(3):
        for comp in range(3):
            parts = []
            for b in range(3):
                at = (a * 3 + b) * blocks
                parts.append(pool_ref[comp, at : at + blocks, :])
            at = slice(a * tile + comp * blocks, a * tile + (comp + 1) * blocks)
            keep_ref[at, :] = parts[1]
            to_even_ref[at, :] = jnp.where(odd_y, parts[0], parts[2])
            to_next_ref[at, :] = jnp.where(odd_y, parts[2], parts[0])


def add_kernel(odd_ref, x_ref, y_ref, z_ref, keep_ref, to_even_ref, to_next_ref):
    tile = keep_ref.shape[0]
    odd_x = odd_ref[0] == 1
    low, mid, high = [
        x_ref[part, :] + y_ref[part, :] + z_ref[part, :]
        for part in [slice(place * tile, (place + 1) * tile) for place in range(3)]
    ]
    keep_ref[...] = mid
    to_even_ref[...] = jnp.where(odd_x, low, high)
    to_next_ref[...] = jnp.where(odd_x, high, low)


def place_kernel(
    odd_ref, cells_ref, v_ref, inv_ref, x_ref, y_ref, z_ref,
    out_ref, x_even_ref, x_next_ref, y_even_ref, y_next_ref,
    left_ref, right_ref,
):
    odd_x, odd_y = odd_ref[0] == 1, odd_ref[1] == 1
    nx, ny, nz = v_ref.shape[1:]
    rows = nx * ny
    slots = cells_ref.shape[1]
    blocks = slots // LANES
    back = x_ref[...] + y_ref[...] + z_ref[...]
    pieces = [piece.astype(F32) for piece in split(back, 2)]
    for block in range(blocks):
        lanes = slice(block * LANES, (block + 1) * LANES)
        row, deep = row_and_depth(cells_ref[:, lanes], nz)
        here = iota((rows, LANES), 0) == row
        right_ref[:, lanes] = ones_where(iota((nz, LANES), 0) == deep)
        for place, piece in enumerate(pieces):
            for comp in range(3):
                at = comp * blocks + block
                group = (place * 3 + comp) * rows
                left_ref[group : group + rows, lanes] = jnp.where(
                    here, piece[at : at + 1, :], 0.0
                ).astype(BF16)
    placed = mm(left_ref[...], right_ref[...], trans=True)
    placed = placed[: 3 * rows] + placed[3 * rows :]
    for a in range(3):
        own = sum(inv_ref[3 * a + b] * v_ref[b] for b in range(3))
        out_ref[a] = own + placed[a * rows : (a + 1) * rows].reshape(nx, ny, nz)
        low, high = out_ref[a, 0], out_ref[a, nx - 1]
        x_even_ref[a] = jnp.where(odd_x, low, high)
        x_next_ref[a] = jnp.where(odd_x, high, low)
        low, high = out_ref[a, :, 0, :], out_ref[a, :, ny - 1, :]
        y_even_ref[a] = jnp.where(odd_y, low, high)
        y_next_ref[a] = jnp.where(odd_y, high, low)


def jacobian(odd_ref, z_ref, faces, d_ref, off_ref, store):
    nx, ny, nz = z_ref.shape[1:]
    odd_x, odd_y = odd_ref[0] == 1, odd_ref[1] == 1
    x_even, x_next, y_even, y_next = [face[...] for face in faces]
    xl, xh = jnp.where(odd_x, x_even, x_next), jnp.where(odd_x, x_next, x_even)
    yl, yh = jnp.where(odd_y, y_even, y_next), jnp.where(odd_y, y_next, y_even)
    row = iota((ny, nz), 0)
    lane = iota((ny, nz), 1)
    for x in range(nx):
        beside = []
        for b in range(3):
            own = z_ref[b, x]
            beside.append(
                [
                    z_ref[b, x - 1] if x else xl[b],
                    z_ref[b, x + 1] if x < nx - 1 else xh[b],
                    jnp.where(row == 0, yl[b, x : x + 1, :], pltpu.roll(own, 1, 0)),
                    jnp.where(row == ny - 1, yh[b, x : x + 1, :], pltpu.roll(own, ny - 1, 0)),
                    jnp.where(lane == 0, 0.0, pltpu.roll(own, 1, 1)),
                    jnp.where(lane == nz - 1, 0.0, pltpu.roll(own, nz - 1, 1)),
                ]
            )
        for a in range(3):
            total = sum(d_ref[3 * a + b, x] * z_ref[b, x] for b in range(3))
            for face in range(6):
                for b in range(3):
                    total = total + off_ref[face, 3 * a + b, x] * beside[b][face]
            store(a, x, total)


def next_kernel(
    odd_ref, cells_ref, z_ref, f0_ref, f1_ref, f2_ref, f3_ref, d_ref, off_ref, v_ref,
    w_ref, t_ref, out_ref,
):
    def store(a, x, value):
        w_ref[a, x] = value
        t_ref[a, x] = value - v_ref[a, x]

    jacobian(odd_ref, z_ref, (f0_ref, f1_ref, f2_ref, f3_ref), d_ref, off_ref, store)
    pick(times_diag(d_ref, [t_ref[b] for b in range(3)]), cells_ref, out_ref)


def gram_kernel(
    odd_ref, z_ref, f0_ref, f1_ref, f2_ref, f3_ref, d_ref, off_ref, v_ref, w1_ref,
    w_ref, sums_ref,
):
    def store(a, x, value):
        w_ref[a, x] = value

    jacobian(odd_ref, z_ref, (f0_ref, f1_ref, f2_ref, f3_ref), d_ref, off_ref, store)
    one, two, rhs = w1_ref[...], w_ref[...], v_ref[...]
    top_one = jnp.maximum(jnp.max(jnp.abs(one)), 1e-30)
    top_two = jnp.maximum(jnp.max(jnp.abs(two)), 1e-30)
    one = one * (1.0 / jnp.full((1, 1), top_one))
    two = two * (1.0 / jnp.full((1, 1), top_two))
    sums = [
        jnp.sum(one * one), jnp.sum(one * two), jnp.sum(two * two),
        jnp.sum(one * rhs), jnp.sum(two * rhs), top_one, top_two,
    ]
    line = iota(sums_ref.shape, 0)
    total = jnp.zeros(sums_ref.shape, F32)
    for place, value in enumerate(sums):
        total = jnp.where(line == place, value, total)
    sums_ref[...] = total


def final_kernel(
    all_ref, v_ref, z1_ref, z2_ref, w1_ref, w2_ref, sol_ref, res_ref
):
    every = [all_ref[:, place, :] for place in range(7)]
    top_one = jnp.max(every[5], axis=0, keepdims=True)
    top_two = jnp.max(every[6], axis=0, keepdims=True)
    one = every[5] / top_one
    two = every[6] / top_two

    def add(value):
        return jnp.sum(value, axis=0, keepdims=True)

    g11 = add(every[0] * one * one)
    g12 = add(every[1] * one * two)
    g22 = add(every[2] * two * two)
    r1 = add(every[3] * one)
    r2 = add(every[4] * two)
    det = g11 * g22 - g12 * g12
    y1 = ((g22 * r1 - g12 * r2) / det / top_one)[:, :1]
    y2 = ((g11 * r2 - g12 * r1) / det / top_two)[:, :1]
    sol_ref[...] = y1 * z1_ref[...] + y2 * z2_ref[...]
    res_ref[...] = v_ref[...] - y1 * w1_ref[...] - y2 * w2_ref[...]


def swap(axis, to_even, to_next):
    count = lax.axis_size(axis)
    out = []
    for first, value in ((0, to_even), (1, to_next)):
        pairs = []
        for i in range(first, count - 1, 2):
            pairs += [(i, i + 1), (i + 1, i)]
        out.append(lax.ppermute(value, axis, pairs))
    return out


def body(
    right_side,
    diag_blocks,
    off_blocks,
    cell_inverse,
    send_cells,
    recv_index,
    seg_count,
    span_inverse,
    span_couple,
):
    _, nx, ny, nz = right_side.shape
    slots = send_cells.shape[1]
    wells, longest = recv_index.shape
    chunks, width, span_all = span_inverse.shape
    span = width // 3
    blocks = slots // LANES
    tile = round_up(3 * blocks, 16)
    rows = round_up(9 * blocks, 16)
    tall = round_up(chunks, 16)
    odd = jnp.stack([lax.axis_index("gx") % 2, lax.axis_index("gy") % 2]).astype(jnp.int32)
    field = right_side.shape
    (picked,) = call(first_kernel, [(tile, LANES)], flops=10**9)(
        send_cells, right_side, diag_blocks
    )
    live = jnp.arange(longest)[None, :] < seg_count[:, None]
    index = jnp.where(live, recv_index, -1)
    index = index.reshape(wells, chunks, span).transpose(1, 0, 2).reshape(1, wells * longest)
    couple = jnp.pad(span_couple.transpose(1, 0, 2), ((0, 0), (0, tall - chunks), (0, 0)))
    h, e, apart = call(
        prep_kernel,
        [(3, tall, span_all), (9, tall, wells), (3, chunks, span, span_all)],
        [((chunks, width, LANES), F32)],
    )(span_inverse, couple)

    def precondition(vector, picked):
        column = jnp.concatenate([picked, *swap("gx", picked, picked)], axis=0)
        even, following = swap("gy", column, column)
        keep, even, following = call(
            solve_kernel,
            [(3 * tile, LANES)] * 3,
            [
                ((3, rows, LANES), F32),
                ((3, tall, wells * span), F32),
                ((tall, span_all), F32),
                ((3, tall, wells), F32),
                ((3, tall, wells), F32),
                ((tall, span_all), F32),
                ((rows, slots), BF16),
                ((6 * LANES, slots), BF16),
            ],
            flops=4 * 10**9,
            scalars=1,
        )(odd, index, column, even, following, apart, h, e)
        even, following = swap("gy", even, following)
        keep, even, following = call(add_kernel, [(tile, LANES)] * 3, scalars=1)(
            odd, keep, even, following
        )
        even, following = swap("gx", even, following)
        z, *faces = call(
            place_kernel,
            [(3, nx, ny, nz)] + [(3, ny, nz)] * 2 + [(3, nx, nz)] * 2,
            [((6 * nx * ny, slots), BF16), ((nz, slots), BF16)],
            flops=10**9,
            scalars=1,
        )(odd, send_cells, vector, cell_inverse, keep, even, following)
        return z, swap("gx", *faces[:2]) + swap("gy", *faces[2:])

    z1, faces = precondition(right_side, picked)
    w1, turned, picked = call(
        next_kernel, [field, field, (tile, LANES)], flops=10**9, scalars=1
    )(odd, send_cells, z1, *faces, diag_blocks, off_blocks, right_side)
    z2, faces = precondition(turned, picked)
    w2, sums = call(gram_kernel, [field, (8, LANES)], scalars=1)(
        odd, z2, *faces, diag_blocks, off_blocks, right_side, w1
    )
    every = lax.all_gather(lax.all_gather(sums, "gy"), "gx").reshape(-1, 8, LANES)
    return tuple(
        call(final_kernel, [field, field])(every, right_side, z1, z2, w1, w2)
    )


def solution(mesh):
    return jax.shard_map(
        body,
        mesh=mesh,
        in_specs=(
            P(None, "gx", "gy", None),
            P(None, "gx", "gy", None),
            P(None, None, "gx", "gy", None),
            P(None, "gx", "gy", None),
            P(("gx", "gy"), None),
            P(("gx", "gy"), None),
            P(("gx", "gy")),
            P(None, None, ("gx", "gy")),
            P(None, None, ("gx", "gy")),
        ),
        out_specs=(P(None, "gx", "gy", None), P(None, "gx", "gy", None)),
        check_vma=False,
    )
```

```python
import functools

import jax
import jax.numpy as jnp
from jax import lax
from jax.experimental import pallas as pl
from jax.experimental.pallas import tpu as pltpu
from jax.sharding import PartitionSpec as P

LANES = 128
F32 = jnp.float32
BF16 = jnp.bfloat16


def round_up(value, unit):
    return -(-value // unit) * unit


def iota(shape, dim):
    return lax.broadcasted_iota(jnp.int32, shape, dim)


def split(value, pieces):
    out = []
    for _ in range(pieces - 1):
        piece = value.astype(BF16)
        out.append(piece)
        value = value - piece.astype(F32)
    out.append(value.astype(BF16))
    return out


def mm(left, right, trans=False):
    dims = (((1,), (1 if trans else 0,)), ((), ()))
    return lax.dot_general(left, right, dims, preferred_element_type=F32)


def mm_exact(value, choice):
    total = None
    for piece in split(value, 3):
        part = mm(piece, choice)
        total = part if total is None else total + part
    return total


def ones_where(mask):
    return jnp.where(mask, 1.0, 0.0).astype(BF16)


def call(kernel, outs, scratch=(), flops=0, space=pltpu.VMEM):
    def run(*args):
        moved = sum(a.size * 4 for a in args) + sum(
            4 * functools.reduce(lambda p, q: p * q, o) for o in outs
        )
        return pl.pallas_call(
            kernel,
            out_shape=[jax.ShapeDtypeStruct(o, F32) for o in outs],
            in_specs=[pl.BlockSpec(memory_space=space)] * len(args),
            out_specs=[pl.BlockSpec(memory_space=pltpu.VMEM)] * len(outs),
            scratch_shapes=[s if hasattr(s, "dtype") else pltpu.VMEM(*s) for s in scratch],
            cost_estimate=pl.CostEstimate(
                flops=flops, bytes_accessed=moved, transcendentals=0
            ),
            compiler_params=pltpu.CompilerParams(vmem_limit_bytes=40 * 2**20),
        )(*args)

    return run


def chunk_of(slots):
    for groups in (5, 4, 3, 2, 1):
        if slots % (groups * LANES) == 0:
            return groups * LANES


def is_odd(axis):
    return lax.rem(lax.axis_index(axis), 2) == 1


def row_and_depth(cells, nz):
    if nz & (nz - 1) == 0:
        return lax.shift_right_logical(cells, nz.bit_length() - 1), cells & (nz - 1)
    return lax.div(cells, jnp.int32(nz)), lax.rem(cells, jnp.int32(nz))


def pick(field, cells_ref, out_ref):
    _, rows, depth = field.shape
    slots = cells_ref.shape[1]
    blocks = slots // LANES
    chunk = chunk_of(slots)
    flat = field.reshape(3 * rows, depth)
    left = jnp.concatenate(split(flat, 2), axis=0)
    for start in range(0, slots, chunk):
        row, deep = row_and_depth(cells_ref[:, start : start + chunk], depth)
        right = ones_where(iota((depth, chunk), 0) == deep)
        found = mm(left, right)
        found = found[: 3 * rows] + found[3 * rows :]
        here = iota((rows, chunk), 0) == row
        for comp in range(3):
            part = jnp.where(here, found[comp * rows : (comp + 1) * rows], 0.0)
            line = jnp.sum(part, axis=0, keepdims=True)
            for piece in range(chunk // LANES):
                at = comp * blocks + start // LANES + piece
                out_ref[at : at + 1, :] = line[:, piece * LANES : (piece + 1) * LANES]
    pad = out_ref.shape[0] - 3 * blocks
    if pad:
        out_ref[3 * blocks :, :] = jnp.zeros((pad, LANES), F32)


def times_diag(d_ref, field):
    nx, ny, nz = d_ref.shape[1:]
    return jnp.stack(
        [
            sum(d_ref[3 * a + b] * field[b] for b in range(3)).reshape(nx * ny, nz)
            for a in range(3)
        ]
    )


def first_kernel(cells_hbm, v_hbm, d_hbm, out_ref, cells_ref, v_ref, d_ref, sem):
    pairs = ((cells_hbm, cells_ref), (v_hbm, v_ref), (d_hbm, d_ref))
    copies = [
        pltpu.make_async_copy(src, dst, sem.at[place])
        for place, (src, dst) in enumerate(pairs)
    ]
    for copy in copies:
        copy.start()
    for copy in copies:
        copy.wait()
    pick(times_diag(d_ref, [v_ref[b] for b in range(3)]), cells_ref, out_ref)


def spread_matrix(wells, width):
    shape = (wells, wells * width)
    gap = iota(shape, 1) - width * iota(shape, 0)
    return ones_where((gap >= 0) & (gap < width))


def last_matrix(wells, width, comp):
    shape = (wells * width, wells)
    return ones_where(iota(shape, 0) == width * iota(shape, 1) + (width - 3 + comp))


def prep_kernel(g_ref, couple_ref, h_ref, e_ref, apart_ref, part_ref):
    chunks, width, span_all = g_ref.shape
    wells = couple_ref.shape[2]
    span = width // 3
    for lane in range(0, span_all, LANES):
        part_ref[...] = g_ref[:, :, lane : lane + LANES]
        for comp in range(3):
            apart_ref[comp, :, :, lane : lane + LANES] = part_ref[
                :, pl.ds(comp, span, stride=3), :
            ]
    spread = spread_matrix(wells, width)
    heads = [g_ref[:, d, :] for d in range(3)]
    for b in range(3):
        total = sum(
            heads[d] * mm_exact(couple_ref[3 * d + b], spread)[:chunks] for d in range(3)
        )
        h_ref[b] = jnp.zeros(h_ref.shape[1:], F32)
        h_ref[b, :chunks, :] = total
        full = h_ref[b]
        for a in range(3):
            e_ref[3 * a + b] = mm_exact(full, last_matrix(wells, width, a))


def solve_kernel(
    idx_ref, own_ref, even_ref, next_ref, g_ref, h_ref, e_ref,
    keep_ref, to_even_ref, to_next_ref,
    pool_ref, r_ref, q_ref, tail_ref, p_ref, y_ref, ohr_ref, w_ref,
):
    _, chunks, span, span_all = g_ref.shape
    width = 3 * span
    wells = span_all // width
    slots = idx_ref.shape[1]
    blocks = slots // LANES
    rows = pool_ref.shape[1]
    tile = own_ref.shape[0] // 3
    group = wells * span
    odd_x, odd_y = is_odd("gx"), is_odd("gy")
    pool_ref[:, 9 * blocks :, :] = jnp.zeros((3, rows - 9 * blocks, LANES), F32)
    own, even, following = own_ref[...], even_ref[...], next_ref[...]
    columns = (
        jnp.where(odd_y, even, following), own, jnp.where(odd_y, following, even)
    )
    for b, column in enumerate(columns):
        own, even, following = column[:tile], column[tile : 2 * tile], column[2 * tile :]
        parts = (jnp.where(odd_x, even, following), own, jnp.where(odd_x, following, even))
        for a, part in enumerate(parts):
            for comp in range(3):
                at = (a * 3 + b) * blocks
                pool_ref[comp, at : at + blocks, :] = part[
                    comp * blocks : (comp + 1) * blocks
                ]
    pooled = pool_ref[...].reshape(3 * rows, LANES)
    left = jnp.concatenate(split(pooled, 2), axis=1)
    size = chunk_of(slots)
    r_ref[...] = jnp.zeros(r_ref.shape, F32)
    for start in range(0, slots, size):
        place = idx_ref[:, start : start + size]
        high = lax.shift_right_arithmetic(place, LANES.bit_length() - 1)
        low = place & (LANES - 1)
        right = ones_where((iota((2 * LANES, size), 0) & (LANES - 1)) == low)
        found = mm(left, right)
        here = iota((rows, size), 0) == high
        ohr_ref[:, start : start + size] = ones_where(here)
        for comp in range(3):
            part = jnp.where(here, found[comp * rows : (comp + 1) * rows], 0.0)
            line = jnp.sum(part, axis=0, keepdims=True)
            for piece in range(size // group):
                at = start // group + piece
                r_ref[comp, at : at + 1, :] = line[:, piece * group : (piece + 1) * group]
    two = (2 * group, span_all)
    well_of = lax.shift_right_logical(iota(two, 0) & (group - 1), (span - 1).bit_length())
    gap = iota(two, 1) - width * well_of
    spread = ones_where((gap >= 0) & (gap < width))
    own = (iota((span, group), 1) & (span - 1)) == iota((span, group), 0)
    total = None
    for comp in range(3):
        values = r_ref[comp][:chunks]
        wide = jnp.where(own[None], values[:, None, :], 0.0).reshape(chunks * span, group)
        lifted = mm(jnp.concatenate(split(wide, 2), axis=1), spread)
        lifted = lifted.reshape(chunks, span, span_all)
        part = g_ref[comp] * lifted
        total = part if total is None else total + part
    q_ref[...] = jnp.zeros(q_ref.shape, F32)
    q_ref[:chunks, :] = jnp.sum(total, axis=1)
    plain = q_ref[...]
    for a in range(3):
        tail_ref[a] = mm_exact(plain, last_matrix(wells, width, a))
    p_ref[...] = jnp.zeros(p_ref.shape, F32)
    state = [jnp.zeros((1, wells), F32)] * 3
    for c in range(chunks - 1):
        state = [
            tail_ref[a, c : c + 1, :]
            - (
                e_ref[3 * a, c : c + 1, :] * state[0]
                + e_ref[3 * a + 1, c : c + 1, :] * state[1]
                + e_ref[3 * a + 2, c : c + 1, :] * state[2]
            )
            for a in range(3)
        ]
        for a in range(3):
            p_ref[a, c + 1 : c + 2, :] = state[a]
    wide_well = spread_matrix(wells, width)
    for b in range(3):
        plain = plain - h_ref[b] * mm_exact(p_ref[b], wide_well)
    square = (span_all, span_all)
    lane = iota((1, span_all), 1)
    comp_of = lax.div(lane, jnp.int32(group))
    rest = lax.rem(lane, jnp.int32(group))
    source = width * lax.div(rest, jnp.int32(span)) + 3 * lax.rem(rest, jnp.int32(span)) + comp_of
    y_ref[...] = mm_exact(plain, ones_where(iota(square, 0) == source))
    for c in range(chunks):
        low = idx_ref[:, c * group : (c + 1) * group] & (LANES - 1)
        match = iota((LANES, group), 0) == low
        for comp in range(3):
            value = y_ref[c : c + 1, comp * group : (comp + 1) * group]
            for place, piece in enumerate(split(value, 2)):
                at = (place * 3 + comp) * LANES
                w_ref[at : at + LANES, c * group : (c + 1) * group] = jnp.where(
                    match, piece.astype(F32), 0.0
                ).astype(BF16)
    spread_out = mm(ohr_ref[...], w_ref[...], trans=True)
    spread_out = spread_out[:, : 3 * LANES] + spread_out[:, 3 * LANES :]
    pool_ref[0] = spread_out[:, :LANES]
    pool_ref[1] = spread_out[:, LANES : 2 * LANES]
    pool_ref[2] = spread_out[:, 2 * LANES :]
    for dst in (keep_ref, to_even_ref, to_next_ref):
        dst[...] = jnp.zeros(dst.shape, F32)
    for a in range(3):
        for comp in range(3):
            parts = []
            for b in range(3):
                at = (a * 3 + b) * blocks
                parts.append(pool_ref[comp, at : at + blocks, :])
            at = slice(a * tile + comp * blocks, a * tile + (comp + 1) * blocks)
            keep_ref[at, :] = parts[1]
            to_even_ref[at, :] = jnp.where(odd_y, parts[0], parts[2])
            to_next_ref[at, :] = jnp.where(odd_y, parts[2], parts[0])


def add_kernel(x_ref, y_ref, z_ref, keep_ref, to_even_ref, to_next_ref):
    tile = keep_ref.shape[0]
    odd_x = is_odd("gx")
    low, mid, high = [
        x_ref[part, :] + y_ref[part, :] + z_ref[part, :]
        for part in [slice(place * tile, (place + 1) * tile) for place in range(3)]
    ]
    keep_ref[...] = mid
    to_even_ref[...] = jnp.where(odd_x, low, high)
    to_next_ref[...] = jnp.where(odd_x, high, low)


def place_kernel(
    cells_ref, v_ref, inv_ref, x_ref, y_ref, z_ref,
    out_ref, x_even_ref, x_next_ref, y_even_ref, y_next_ref,
    left_ref, right_ref,
):
    (first_x, last_x), (first_y, last_y) = [
        (lax.axis_index(axis) == 0, lax.axis_index(axis) == lax.axis_size(axis) - 1)
        for axis in ("gx", "gy")
    ]
    odd_x, odd_y = is_odd("gx"), is_odd("gy")
    nx, ny, nz = v_ref.shape[1:]
    rows = nx * ny
    slots = cells_ref.shape[1]
    blocks = slots // LANES
    back = x_ref[...] + y_ref[...] + z_ref[...]
    pieces = [piece.astype(F32) for piece in split(back, 2)]
    for block in range(blocks):
        lanes = slice(block * LANES, (block + 1) * LANES)
        row, deep = row_and_depth(cells_ref[:, lanes], nz)
        here = iota((rows, LANES), 0) == row
        right_ref[:, lanes] = ones_where(iota((nz, LANES), 0) == deep)
        for place, piece in enumerate(pieces):
            for comp in range(3):
                at = comp * blocks + block
                group = (place * 3 + comp) * rows
                left_ref[group : group + rows, lanes] = jnp.where(
                    here, piece[at : at + 1, :], 0.0
                ).astype(BF16)
    placed = mm(left_ref[...], right_ref[...], trans=True)
    placed = placed[: 3 * rows] + placed[3 * rows :]
    for a in range(3):
        own = sum(inv_ref[3 * a + b] * v_ref[b] for b in range(3))
        out_ref[a] = own + placed[a * rows : (a + 1) * rows].reshape(nx, ny, nz)
        low = jnp.where(first_x, 0.0, out_ref[a, 0])
        high = jnp.where(last_x, 0.0, out_ref[a, nx - 1])
        x_even_ref[a] = jnp.where(odd_x, low, high)
        x_next_ref[a] = jnp.where(odd_x, high, low)
        low = jnp.where(first_y, 0.0, out_ref[a, :, 0, :])
        high = jnp.where(last_y, 0.0, out_ref[a, :, ny - 1, :])
        y_even_ref[a] = jnp.where(odd_y, low, high)
        y_next_ref[a] = jnp.where(odd_y, high, low)


def jacobian(z_ref, faces, d_ref, off_ref, store):
    nx, ny, nz = z_ref.shape[1:]
    odd_x, odd_y = is_odd("gx"), is_odd("gy")
    x_even, x_next, y_even, y_next = [face[...] for face in faces]
    xl, xh = jnp.where(odd_x, x_even, x_next), jnp.where(odd_x, x_next, x_even)
    yl, yh = jnp.where(odd_y, y_even, y_next), jnp.where(odd_y, y_next, y_even)
    row = iota((ny, nz), 0)
    lane = iota((ny, nz), 1)
    for x in range(nx):
        beside = []
        for b in range(3):
            own = z_ref[b, x]
            beside.append(
                [
                    z_ref[b, x - 1] if x else xl[b],
                    z_ref[b, x + 1] if x < nx - 1 else xh[b],
                    jnp.where(row == 0, yl[b, x : x + 1, :], pltpu.roll(own, 1, 0)),
                    jnp.where(row == ny - 1, yh[b, x : x + 1, :], pltpu.roll(own, ny - 1, 0)),
                    jnp.where(lane == 0, 0.0, pltpu.roll(own, 1, 1)),
                    jnp.where(lane == nz - 1, 0.0, pltpu.roll(own, nz - 1, 1)),
                ]
            )
        for a in range(3):
            total = sum(d_ref[3 * a + b, x] * z_ref[b, x] for b in range(3))
            for face in range(6):
                for b in range(3):
                    total = total + off_ref[face, 3 * a + b, x] * beside[b][face]
            store(a, x, total)


def next_kernel(
    cells_ref, z_ref, f0_ref, f1_ref, f2_ref, f3_ref, d_ref, off_ref, v_ref,
    w_ref, t_ref, out_ref,
):
    def store(a, x, value):
        w_ref[a, x] = value
        t_ref[a, x] = value - v_ref[a, x]

    jacobian(z_ref, (f0_ref, f1_ref, f2_ref, f3_ref), d_ref, off_ref, store)
    pick(times_diag(d_ref, [t_ref[b] for b in range(3)]), cells_ref, out_ref)


def gram_kernel(
    z_ref, f0_ref, f1_ref, f2_ref, f3_ref, d_ref, off_ref, v_ref, w1_ref,
    w_ref, sums_ref,
):
    def store(a, x, value):
        w_ref[a, x] = value

    jacobian(z_ref, (f0_ref, f1_ref, f2_ref, f3_ref), d_ref, off_ref, store)
    one, two, rhs = w1_ref[...], w_ref[...], v_ref[...]
    top_one = jnp.maximum(jnp.max(jnp.abs(one)), 1e-30)
    top_two = jnp.maximum(jnp.max(jnp.abs(two)), 1e-30)
    one = one * (1.0 / jnp.full((1, 1), top_one))
    two = two * (1.0 / jnp.full((1, 1), top_two))
    sums = [
        jnp.sum(one * one), jnp.sum(one * two), jnp.sum(two * two),
        jnp.sum(one * rhs), jnp.sum(two * rhs), top_one, top_two,
    ]
    line = iota(sums_ref.shape, 0)
    total = jnp.zeros(sums_ref.shape, F32)
    for place, value in enumerate(sums):
        total = jnp.where(line == place, value, total)
    sums_ref[...] = total


def final_kernel(
    all_ref, v_ref, z1_ref, z2_ref, w1_ref, w2_ref, sol_ref, res_ref
):
    every = [all_ref[:, place, :] for place in range(7)]
    top_one = jnp.max(every[5], axis=0, keepdims=True)
    top_two = jnp.max(every[6], axis=0, keepdims=True)
    one = every[5] / top_one
    two = every[6] / top_two

    def add(value):
        return jnp.sum(value, axis=0, keepdims=True)

    g11 = add(every[0] * one * one)
    g12 = add(every[1] * one * two)
    g22 = add(every[2] * two * two)
    r1 = add(every[3] * one)
    r2 = add(every[4] * two)
    det = g11 * g22 - g12 * g12
    y1 = ((g22 * r1 - g12 * r2) / det / top_one)[:, :1]
    y2 = ((g11 * r2 - g12 * r1) / det / top_two)[:, :1]
    sol_ref[...] = y1 * z1_ref[...] + y2 * z2_ref[...]
    res_ref[...] = v_ref[...] - y1 * w1_ref[...] - y2 * w2_ref[...]


def swap(axis, to_even, to_next):
    count = lax.axis_size(axis)
    out = []
    for first, value in ((0, to_even), (1, to_next)):
        pairs = []
        for i in range(first, count - 1, 2):
            pairs += [(i, i + 1), (i + 1, i)]
        taken = [source for source, _ in pairs]
        pairs += [(i, i) for i in range(count) if i not in taken]
        out.append(lax.ppermute(value, axis, pairs))
    return out


def gather_all(value, axis):
    count = lax.axis_size(axis)
    if count & (count - 1):
        return lax.all_gather(value, axis, tiled=True)
    step = 1
    while step < count:
        other = lax.ppermute(value, axis, [(i, i ^ step) for i in range(count)])
        value = jnp.concatenate([value, other], axis=0)
        step *= 2
    return value


def body(
    right_side,
    diag_blocks,
    off_blocks,
    cell_inverse,
    send_cells,
    recv_index,
    seg_count,
    span_inverse,
    span_couple,
):
    _, nx, ny, nz = right_side.shape
    slots = send_cells.shape[1]
    wells, longest = recv_index.shape
    chunks, width, span_all = span_inverse.shape
    span = width // 3
    blocks = slots // LANES
    tile = round_up(3 * blocks, 16)
    rows = round_up(9 * blocks, 16)
    tall = round_up(chunks, 16)
    field = right_side.shape
    (picked,) = call(
        first_kernel,
        [(tile, LANES)],
        [
            (send_cells.shape, jnp.int32),
            (field, F32),
            (diag_blocks.shape, F32),
            pltpu.SemaphoreType.DMA((3,)),
        ],
        flops=10**9,
        space=pltpu.HBM,
    )(send_cells, right_side, diag_blocks)
    live = jnp.arange(longest)[None, :] < seg_count[:, None]
    index = jnp.where(live, recv_index, -1)
    index = index.reshape(wells, chunks, span).transpose(1, 0, 2).reshape(1, wells * longest)
    couple = jnp.pad(span_couple.transpose(1, 0, 2), ((0, 0), (0, tall - chunks), (0, 0)))
    h, e, apart = call(
        prep_kernel,
        [(3, tall, span_all), (9, tall, wells), (3, chunks, span, span_all)],
        [((chunks, width, LANES), F32)],
    )(span_inverse, couple)

    def precondition(vector, picked):
        column = jnp.concatenate([picked, *swap("gx", picked, picked)], axis=0)
        even, following = swap("gy", column, column)
        keep, even, following = call(
            solve_kernel,
            [(3 * tile, LANES)] * 3,
            [
                ((3, rows, LANES), F32),
                ((3, tall, wells * span), F32),
                ((tall, span_all), F32),
                ((3, tall, wells), F32),
                ((3, tall, wells), F32),
                ((tall, span_all), F32),
                ((rows, slots), BF16),
                ((6 * LANES, slots), BF16),
            ],
            flops=4 * 10**9,
        )(index, column, even, following, apart, h, e)
        even, following = swap("gy", even, following)
        keep, even, following = call(add_kernel, [(tile, LANES)] * 3)(
            keep, even, following
        )
        even, following = swap("gx", even, following)
        z, *faces = call(
            place_kernel,
            [(3, nx, ny, nz)] + [(3, ny, nz)] * 2 + [(3, nx, nz)] * 2,
            [((6 * nx * ny, slots), BF16), ((nz, slots), BF16)],
            flops=10**9,
        )(send_cells, vector, cell_inverse, keep, even, following)
        return z, swap("gx", *faces[:2]) + swap("gy", *faces[2:])

    z1, faces = precondition(right_side, picked)
    w1, turned, picked = call(
        next_kernel, [field, field, (tile, LANES)], flops=10**9
    )(send_cells, z1, *faces, diag_blocks, off_blocks, right_side)
    z2, faces = precondition(turned, picked)
    w2, sums = call(gram_kernel, [field, (8, LANES)])(
        z2, *faces, diag_blocks, off_blocks, right_side, w1
    )
    every = gather_all(gather_all(sums, "gy"), "gx").reshape(-1, 8, LANES)
    return tuple(
        call(final_kernel, [field, field])(every, right_side, z1, z2, w1, w2)
    )


def solution(mesh):
    return jax.shard_map(
        body,
        mesh=mesh,
        in_specs=(
            P(None, "gx", "gy", None),
            P(None, "gx", "gy", None),
            P(None, None, "gx", "gy", None),
            P(None, "gx", "gy", None),
            P(("gx", "gy"), None),
            P(("gx", "gy"), None),
            P(("gx", "gy")),
            P(None, None, ("gx", "gy")),
            P(None, None, ("gx", "gy")),
        ),
        out_specs=(P(None, "gx", "gy", None), P(None, "gx", "gy", None)),
        check_vma=False,
    )
```

```python
import functools

import jax
import jax.numpy as jnp
from jax import lax
from jax.experimental import pallas as pl
from jax.experimental.pallas import tpu as pltpu
from jax.sharding import PartitionSpec as P

LANES = 128
F32 = jnp.float32
BF16 = jnp.bfloat16


def round_up(value, unit):
    return -(-value // unit) * unit


def iota(shape, dim):
    return lax.broadcasted_iota(jnp.int32, shape, dim)


def split(value, pieces):
    out = []
    for _ in range(pieces - 1):
        piece = value.astype(BF16)
        out.append(piece)
        value = value - piece.astype(F32)
    out.append(value.astype(BF16))
    return out


def mm(left, right, trans=False):
    dims = (((1,), (1 if trans else 0,)), ((), ()))
    return lax.dot_general(left, right, dims, preferred_element_type=F32)


def mm_exact(value, choice):
    total = None
    for piece in split(value, 3):
        part = mm(piece, choice)
        total = part if total is None else total + part
    return total


def ones_where(mask):
    return jnp.where(mask, 1.0, 0.0).astype(BF16)


def call(kernel, outs, scratch=(), flops=0, space=pltpu.VMEM, mib=40):
    def run(*args):
        moved = sum(a.size * 4 for a in args) + sum(
            4 * functools.reduce(lambda p, q: p * q, o) for o in outs
        )
        return pl.pallas_call(
            kernel,
            out_shape=[jax.ShapeDtypeStruct(o, F32) for o in outs],
            in_specs=[pl.BlockSpec(memory_space=space)] * len(args),
            out_specs=[pl.BlockSpec(memory_space=pltpu.VMEM)] * len(outs),
            scratch_shapes=[s if hasattr(s, "dtype") else pltpu.VMEM(*s) for s in scratch],
            cost_estimate=pl.CostEstimate(
                flops=flops, bytes_accessed=moved, transcendentals=0
            ),
            compiler_params=pltpu.CompilerParams(vmem_limit_bytes=mib * 2**20),
        )(*args)

    return run


def chunk_of(slots):
    for groups in (5, 4, 3, 2, 1):
        if slots % (groups * LANES) == 0:
            return groups * LANES


def is_odd(axis):
    return lax.rem(lax.axis_index(axis), 2) == 1


def row_and_depth(cells, nz):
    if nz & (nz - 1) == 0:
        return lax.shift_right_logical(cells, nz.bit_length() - 1), cells & (nz - 1)
    return lax.div(cells, jnp.int32(nz)), lax.rem(cells, jnp.int32(nz))


def pick(field, cells_ref, out_ref):
    _, rows, depth = field.shape
    slots = cells_ref.shape[1]
    blocks = slots // LANES
    chunk = chunk_of(slots)
    flat = field.reshape(3 * rows, depth)
    left = jnp.concatenate(split(flat, 2), axis=0)
    for start in range(0, slots, chunk):
        row, deep = row_and_depth(cells_ref[:, start : start + chunk], depth)
        right = ones_where(iota((depth, chunk), 0) == deep)
        found = mm(left, right)
        found = found[: 3 * rows] + found[3 * rows :]
        here = iota((rows, chunk), 0) == row
        for comp in range(3):
            part = jnp.where(here, found[comp * rows : (comp + 1) * rows], 0.0)
            line = jnp.sum(part, axis=0, keepdims=True)
            for piece in range(chunk // LANES):
                at = comp * blocks + start // LANES + piece
                out_ref[at : at + 1, :] = line[:, piece * LANES : (piece + 1) * LANES]
    pad = out_ref.shape[0] - 3 * blocks
    if pad:
        out_ref[3 * blocks :, :] = jnp.zeros((pad, LANES), F32)


def times_diag(d_ref, field):
    nx, ny, nz = d_ref.shape[1:]
    return jnp.stack(
        [
            sum(d_ref[3 * a + b] * field[b] for b in range(3)).reshape(nx * ny, nz)
            for a in range(3)
        ]
    )


def first_kernel(cells_hbm, v_hbm, d_hbm, out_ref, cells_ref, v_ref, d_ref, sem):
    pairs = ((cells_hbm, cells_ref), (v_hbm, v_ref), (d_hbm, d_ref))
    copies = [
        pltpu.make_async_copy(src, dst, sem.at[place])
        for place, (src, dst) in enumerate(pairs)
    ]
    for copy in copies:
        copy.start()
    for copy in copies:
        copy.wait()
    pick(times_diag(d_ref, [v_ref[b] for b in range(3)]), cells_ref, out_ref)


def spread_matrix(wells, width):
    shape = (wells, wells * width)
    gap = iota(shape, 1) - width * iota(shape, 0)
    return ones_where((gap >= 0) & (gap < width))


def last_matrix(wells, width, comp):
    shape = (wells * width, wells)
    return ones_where(iota(shape, 0) == width * iota(shape, 1) + (width - 3 + comp))


def prep_kernel(g_ref, couple_ref, h_ref, e_ref, apart_ref, part_ref):
    chunks, width, span_all = g_ref.shape
    wells = couple_ref.shape[2]
    span = width // 3
    for lane in range(0, span_all, LANES):
        part_ref[...] = g_ref[:, :, lane : lane + LANES]
        for comp in range(3):
            apart_ref[comp, :, :, lane : lane + LANES] = part_ref[
                :, pl.ds(comp, span, stride=3), :
            ]
    spread = spread_matrix(wells, width)
    heads = [g_ref[:, d, :] for d in range(3)]
    for b in range(3):
        total = sum(
            heads[d] * mm_exact(couple_ref[3 * d + b], spread)[:chunks] for d in range(3)
        )
        h_ref[b] = jnp.zeros(h_ref.shape[1:], F32)
        h_ref[b, :chunks, :] = total
        full = h_ref[b]
        for a in range(3):
            e_ref[3 * a + b] = mm_exact(full, last_matrix(wells, width, a))


def solve_kernel(
    idx_ref, own_ref, even_ref, next_ref, g_ref, h_ref, e_ref,
    keep_ref, to_even_ref, to_next_ref,
    pool_ref, r_ref, q_ref, tail_ref, p_ref, y_ref, ohr_ref, w_ref,
):
    _, chunks, span, span_all = g_ref.shape
    width = 3 * span
    wells = span_all // width
    slots = idx_ref.shape[1]
    blocks = slots // LANES
    rows = pool_ref.shape[1]
    tile = own_ref.shape[0] // 3
    group = wells * span
    odd_x, odd_y = is_odd("gx"), is_odd("gy")
    pool_ref[:, 9 * blocks :, :] = jnp.zeros((3, rows - 9 * blocks, LANES), F32)
    own, even, following = own_ref[...], even_ref[...], next_ref[...]
    columns = (
        jnp.where(odd_y, even, following), own, jnp.where(odd_y, following, even)
    )
    for b, column in enumerate(columns):
        own, even, following = column[:tile], column[tile : 2 * tile], column[2 * tile :]
        parts = (jnp.where(odd_x, even, following), own, jnp.where(odd_x, following, even))
        for a, part in enumerate(parts):
            for comp in range(3):
                at = (a * 3 + b) * blocks
                pool_ref[comp, at : at + blocks, :] = part[
                    comp * blocks : (comp + 1) * blocks
                ]
    pooled = pool_ref[...].reshape(3 * rows, LANES)
    left = jnp.concatenate(split(pooled, 2), axis=1)
    size = chunk_of(slots)
    r_ref[...] = jnp.zeros(r_ref.shape, F32)
    for start in range(0, slots, size):
        place = idx_ref[:, start : start + size]
        high = lax.shift_right_arithmetic(place, LANES.bit_length() - 1)
        low = place & (LANES - 1)
        right = ones_where((iota((2 * LANES, size), 0) & (LANES - 1)) == low)
        found = mm(left, right)
        here = iota((rows, size), 0) == high
        ohr_ref[:, start : start + size] = ones_where(here)
        for comp in range(3):
            part = jnp.where(here, found[comp * rows : (comp + 1) * rows], 0.0)
            line = jnp.sum(part, axis=0, keepdims=True)
            for piece in range(size // group):
                at = start // group + piece
                r_ref[comp, at : at + 1, :] = line[:, piece * group : (piece + 1) * group]
    two = (2 * group, span_all)
    well_of = lax.shift_right_logical(iota(two, 0) & (group - 1), (span - 1).bit_length())
    gap = iota(two, 1) - width * well_of
    spread = ones_where((gap >= 0) & (gap < width))
    own = (iota((span, group), 1) & (span - 1)) == iota((span, group), 0)
    total = None
    for comp in range(3):
        values = r_ref[comp][:chunks]
        wide = jnp.where(own[None], values[:, None, :], 0.0).reshape(chunks * span, group)
        lifted = mm(jnp.concatenate(split(wide, 2), axis=1), spread)
        lifted = lifted.reshape(chunks, span, span_all)
        part = g_ref[comp] * lifted
        total = part if total is None else total + part
    q_ref[...] = jnp.zeros(q_ref.shape, F32)
    q_ref[:chunks, :] = jnp.sum(total, axis=1)
    plain = q_ref[...]
    for a in range(3):
        tail_ref[a] = mm_exact(plain, last_matrix(wells, width, a))
    p_ref[...] = jnp.zeros(p_ref.shape, F32)
    state = [jnp.zeros((1, wells), F32)] * 3
    for c in range(chunks - 1):
        state = [
            tail_ref[a, c : c + 1, :]
            - (
                e_ref[3 * a, c : c + 1, :] * state[0]
                + e_ref[3 * a + 1, c : c + 1, :] * state[1]
                + e_ref[3 * a + 2, c : c + 1, :] * state[2]
            )
            for a in range(3)
        ]
        for a in range(3):
            p_ref[a, c + 1 : c + 2, :] = state[a]
    wide_well = spread_matrix(wells, width)
    for b in range(3):
        plain = plain - h_ref[b] * mm_exact(p_ref[b], wide_well)
    square = (span_all, span_all)
    lane = iota((1, span_all), 1)
    comp_of = lax.div(lane, jnp.int32(group))
    rest = lax.rem(lane, jnp.int32(group))
    source = width * lax.div(rest, jnp.int32(span)) + 3 * lax.rem(rest, jnp.int32(span)) + comp_of
    y_ref[...] = mm_exact(plain, ones_where(iota(square, 0) == source))
    for c in range(chunks):
        low = idx_ref[:, c * group : (c + 1) * group] & (LANES - 1)
        match = iota((LANES, group), 0) == low
        for comp in range(3):
            value = y_ref[c : c + 1, comp * group : (comp + 1) * group]
            for place, piece in enumerate(split(value, 2)):
                at = (place * 3 + comp) * LANES
                w_ref[at : at + LANES, c * group : (c + 1) * group] = jnp.where(
                    match, piece.astype(F32), 0.0
                ).astype(BF16)
    spread_out = mm(ohr_ref[...], w_ref[...], trans=True)
    spread_out = spread_out[:, : 3 * LANES] + spread_out[:, 3 * LANES :]
    pool_ref[0] = spread_out[:, :LANES]
    pool_ref[1] = spread_out[:, LANES : 2 * LANES]
    pool_ref[2] = spread_out[:, 2 * LANES :]
    for dst in (keep_ref, to_even_ref, to_next_ref):
        dst[...] = jnp.zeros(dst.shape, F32)
    for a in range(3):
        for comp in range(3):
            parts = []
            for b in range(3):
                at = (a * 3 + b) * blocks
                parts.append(pool_ref[comp, at : at + blocks, :])
            at = slice(a * tile + comp * blocks, a * tile + (comp + 1) * blocks)
            keep_ref[at, :] = parts[1]
            to_even_ref[at, :] = jnp.where(odd_y, parts[0], parts[2])
            to_next_ref[at, :] = jnp.where(odd_y, parts[2], parts[0])


def add_kernel(x_ref, y_ref, z_ref, keep_ref, to_even_ref, to_next_ref):
    tile = keep_ref.shape[0]
    odd_x = is_odd("gx")
    low, mid, high = [
        x_ref[part, :] + y_ref[part, :] + z_ref[part, :]
        for part in [slice(place * tile, (place + 1) * tile) for place in range(3)]
    ]
    keep_ref[...] = mid
    to_even_ref[...] = jnp.where(odd_x, low, high)
    to_next_ref[...] = jnp.where(odd_x, high, low)


def place_kernel(
    cells_ref, v_ref, inv_ref, x_ref, y_ref, z_ref,
    out_ref, x_even_ref, x_next_ref, y_even_ref, y_next_ref,
    left_ref, right_ref,
):
    (first_x, last_x), (first_y, last_y) = [
        (lax.axis_index(axis) == 0, lax.axis_index(axis) == lax.axis_size(axis) - 1)
        for axis in ("gx", "gy")
    ]
    odd_x, odd_y = is_odd("gx"), is_odd("gy")
    nx, ny, nz = v_ref.shape[1:]
    rows = nx * ny
    slots = cells_ref.shape[1]
    blocks = slots // LANES
    back = x_ref[...] + y_ref[...] + z_ref[...]
    pieces = [piece.astype(F32) for piece in split(back, 2)]
    for block in range(blocks):
        lanes = slice(block * LANES, (block + 1) * LANES)
        row, deep = row_and_depth(cells_ref[:, lanes], nz)
        here = iota((rows, LANES), 0) == row
        right_ref[:, lanes] = ones_where(iota((nz, LANES), 0) == deep)
        for place, piece in enumerate(pieces):
            for comp in range(3):
                at = comp * blocks + block
                group = (place * 3 + comp) * rows
                left_ref[group : group + rows, lanes] = jnp.where(
                    here, piece[at : at + 1, :], 0.0
                ).astype(BF16)
    placed = mm(left_ref[...], right_ref[...], trans=True)
    placed = placed[: 3 * rows] + placed[3 * rows :]
    for a in range(3):
        own = sum(inv_ref[3 * a + b] * v_ref[b] for b in range(3))
        out_ref[a] = own + placed[a * rows : (a + 1) * rows].reshape(nx, ny, nz)
        low = jnp.where(first_x, 0.0, out_ref[a, 0])
        high = jnp.where(last_x, 0.0, out_ref[a, nx - 1])
        x_even_ref[a] = jnp.where(odd_x, low, high)
        x_next_ref[a] = jnp.where(odd_x, high, low)
        low = jnp.where(first_y, 0.0, out_ref[a, :, 0, :])
        high = jnp.where(last_y, 0.0, out_ref[a, :, ny - 1, :])
        y_even_ref[a] = jnp.where(odd_y, low, high)
        y_next_ref[a] = jnp.where(odd_y, high, low)


def jacobian(z_ref, faces, d_ref, off_ref, store):
    nx, ny, nz = z_ref.shape[1:]
    odd_x, odd_y = is_odd("gx"), is_odd("gy")
    x_even, x_next, y_even, y_next = [face[...] for face in faces]
    xl, xh = jnp.where(odd_x, x_even, x_next), jnp.where(odd_x, x_next, x_even)
    yl, yh = jnp.where(odd_y, y_even, y_next), jnp.where(odd_y, y_next, y_even)
    row = iota((ny, nz), 0)
    lane = iota((ny, nz), 1)
    for x in range(nx):
        beside = []
        for b in range(3):
            own = z_ref[b, x]
            beside.append(
                [
                    z_ref[b, x - 1] if x else xl[b],
                    z_ref[b, x + 1] if x < nx - 1 else xh[b],
                    jnp.where(row == 0, yl[b, x : x + 1, :], pltpu.roll(own, 1, 0)),
                    jnp.where(row == ny - 1, yh[b, x : x + 1, :], pltpu.roll(own, ny - 1, 0)),
                    jnp.where(lane == 0, 0.0, pltpu.roll(own, 1, 1)),
                    jnp.where(lane == nz - 1, 0.0, pltpu.roll(own, nz - 1, 1)),
                ]
            )
        for a in range(3):
            total = sum(d_ref[3 * a + b, x] * z_ref[b, x] for b in range(3))
            for face in range(6):
                for b in range(3):
                    total = total + off_ref[face, 3 * a + b, x] * beside[b][face]
            store(a, x, total)


def next_kernel(
    cells_ref, z_ref, f0_ref, f1_ref, f2_ref, f3_ref, d_ref, off_ref, v_ref,
    w_ref, t_ref, out_ref,
):
    def store(a, x, value):
        w_ref[a, x] = value
        t_ref[a, x] = value - v_ref[a, x]

    jacobian(z_ref, (f0_ref, f1_ref, f2_ref, f3_ref), d_ref, off_ref, store)
    pick(times_diag(d_ref, [t_ref[b] for b in range(3)]), cells_ref, out_ref)


def gram_kernel(
    z_ref, f0_ref, f1_ref, f2_ref, f3_ref, d_ref, off_ref, v_ref, w1_ref,
    w_ref, sums_ref,
):
    def store(a, x, value):
        w_ref[a, x] = value

    jacobian(z_ref, (f0_ref, f1_ref, f2_ref, f3_ref), d_ref, off_ref, store)
    one, two, rhs = w1_ref[...], w_ref[...], v_ref[...]
    top_one = jnp.maximum(jnp.max(jnp.abs(one)), 1e-30)
    top_two = jnp.maximum(jnp.max(jnp.abs(two)), 1e-30)
    one = one * (1.0 / jnp.full((1, 1), top_one))
    two = two * (1.0 / jnp.full((1, 1), top_two))
    sums = [
        jnp.sum(one * one), jnp.sum(one * two), jnp.sum(two * two),
        jnp.sum(one * rhs), jnp.sum(two * rhs), top_one, top_two,
    ]
    line = iota(sums_ref.shape, 0)
    total = jnp.zeros(sums_ref.shape, F32)
    for place, value in enumerate(sums):
        total = jnp.where(line == place, value, total)
    sums_ref[...] = total


def final_kernel(
    all_ref, v_ref, z1_ref, z2_ref, w1_ref, w2_ref, sol_ref, res_ref
):
    every = [all_ref[:, place, :] for place in range(7)]
    top_one = jnp.max(every[5], axis=0, keepdims=True)
    top_two = jnp.max(every[6], axis=0, keepdims=True)
    one = every[5] / top_one
    two = every[6] / top_two

    def add(value):
        return jnp.sum(value, axis=0, keepdims=True)

    g11 = add(every[0] * one * one)
    g12 = add(every[1] * one * two)
    g22 = add(every[2] * two * two)
    r1 = add(every[3] * one)
    r2 = add(every[4] * two)
    det = g11 * g22 - g12 * g12
    y1 = ((g22 * r1 - g12 * r2) / det / top_one)[:, :1]
    y2 = ((g11 * r2 - g12 * r1) / det / top_two)[:, :1]
    sol_ref[...] = y1 * z1_ref[...] + y2 * z2_ref[...]
    res_ref[...] = v_ref[...] - y1 * w1_ref[...] - y2 * w2_ref[...]


def swap(axis, to_even, to_next):
    count = lax.axis_size(axis)
    out = []
    for first, value in ((0, to_even), (1, to_next)):
        pairs = []
        for i in range(first, count - 1, 2):
            pairs += [(i, i + 1), (i + 1, i)]
        if first and count % 2 == 0 and count > 2:
            pairs += [(0, count - 1), (count - 1, 0)]
        taken = [source for source, _ in pairs]
        pairs += [(i, i) for i in range(count) if i not in taken]
        out.append(lax.ppermute(value, axis, pairs))
    return out


def gather_all(value, axis):
    count = lax.axis_size(axis)
    if count & (count - 1):
        return lax.all_gather(value, axis, tiled=True)
    step = 1
    while step < count:
        other = lax.ppermute(value, axis, [(i, i ^ step) for i in range(count)])
        value = jnp.concatenate([value, other], axis=0)
        step *= 2
    return value


def body(
    right_side,
    diag_blocks,
    off_blocks,
    cell_inverse,
    send_cells,
    recv_index,
    seg_count,
    span_inverse,
    span_couple,
):
    _, nx, ny, nz = right_side.shape
    slots = send_cells.shape[1]
    wells, longest = recv_index.shape
    chunks, width, span_all = span_inverse.shape
    span = width // 3
    blocks = slots // LANES
    tile = round_up(3 * blocks, 16)
    rows = round_up(9 * blocks, 16)
    tall = round_up(chunks, 16)
    field = right_side.shape
    (picked,) = call(
        first_kernel,
        [(tile, LANES)],
        [
            (send_cells.shape, jnp.int32),
            (field, F32),
            (diag_blocks.shape, F32),
            pltpu.SemaphoreType.DMA((3,)),
        ],
        flops=10**9,
        space=pltpu.HBM,
        mib=60,
    )(send_cells, right_side, diag_blocks)
    live = jnp.arange(longest)[None, :] < seg_count[:, None]
    index = jnp.where(live, recv_index, -1)
    index = index.reshape(wells, chunks, span).transpose(1, 0, 2).reshape(1, wells * longest)
    couple = jnp.pad(span_couple.transpose(1, 0, 2), ((0, 0), (0, tall - chunks), (0, 0)))
    h, e, apart = call(
        prep_kernel,
        [(3, tall, span_all), (9, tall, wells), (3, chunks, span, span_all)],
        [((chunks, width, LANES), F32)],
    )(span_inverse, couple)

    def precondition(vector, picked):
        column = jnp.concatenate([picked, *swap("gx", picked, picked)], axis=0)
        even, following = swap("gy", column, column)
        keep, even, following = call(
            solve_kernel,
            [(3 * tile, LANES)] * 3,
            [
                ((3, rows, LANES), F32),
                ((3, tall, wells * span), F32),
                ((tall, span_all), F32),
                ((3, tall, wells), F32),
                ((3, tall, wells), F32),
                ((tall, span_all), F32),
                ((rows, slots), BF16),
                ((6 * LANES, slots), BF16),
            ],
            flops=4 * 10**9,
        )(index, column, even, following, apart, h, e)
        even, following = swap("gy", even, following)
        keep, even, following = call(add_kernel, [(tile, LANES)] * 3)(
            keep, even, following
        )
        even, following = swap("gx", even, following)
        z, *faces = call(
            place_kernel,
            [(3, nx, ny, nz)] + [(3, ny, nz)] * 2 + [(3, nx, nz)] * 2,
            [((6 * nx * ny, slots), BF16), ((nz, slots), BF16)],
            flops=10**9,
        )(send_cells, vector, cell_inverse, keep, even, following)
        return z, swap("gx", *faces[:2]) + swap("gy", *faces[2:])

    z1, faces = precondition(right_side, picked)
    w1, turned, picked = call(
        next_kernel, [field, field, (tile, LANES)], flops=10**9
    )(send_cells, z1, *faces, diag_blocks, off_blocks, right_side)
    z2, faces = precondition(turned, picked)
    w2, sums = call(gram_kernel, [field, (8, LANES)])(
        z2, *faces, diag_blocks, off_blocks, right_side, w1
    )
    every = gather_all(gather_all(sums, "gy"), "gx").reshape(-1, 8, LANES)
    return tuple(
        call(final_kernel, [field, field])(every, right_side, z1, z2, w1, w2)
    )


def solution(mesh):
    return jax.shard_map(
        body,
        mesh=mesh,
        in_specs=(
            P(None, "gx", "gy", None),
            P(None, "gx", "gy", None),
            P(None, None, "gx", "gy", None),
            P(None, "gx", "gy", None),
            P(("gx", "gy"), None),
            P(("gx", "gy"), None),
            P(("gx", "gy")),
            P(None, None, ("gx", "gy")),
            P(None, None, ("gx", "gy")),
        ),
        out_specs=(P(None, "gx", "gy", None), P(None, "gx", "gy", None)),
        check_vma=False,
    )
```

```python
import functools

import jax
import jax.numpy as jnp
from jax import lax
from jax.experimental import pallas as pl
from jax.experimental.pallas import tpu as pltpu
from jax.sharding import PartitionSpec as P

LANES = 128
F32 = jnp.float32
BF16 = jnp.bfloat16


def round_up(value, unit):
    return -(-value // unit) * unit


def iota(shape, dim):
    return lax.broadcasted_iota(jnp.int32, shape, dim)


def split(value, pieces):
    out = []
    for _ in range(pieces - 1):
        piece = value.astype(BF16)
        out.append(piece)
        value = value - piece.astype(F32)
    out.append(value.astype(BF16))
    return out


def mm(left, right, trans=False):
    dims = (((1,), (1 if trans else 0,)), ((), ()))
    return lax.dot_general(left, right, dims, preferred_element_type=F32)


def mm_exact(value, choice):
    total = None
    for piece in split(value, 3):
        part = mm(piece, choice)
        total = part if total is None else total + part
    return total


def ones_where(mask):
    return jnp.where(mask, 1.0, 0.0).astype(BF16)


def call(kernel, outs, scratch=(), flops=0, space=pltpu.VMEM, mib=40):
    def run(*args):
        moved = sum(a.size * 4 for a in args) + sum(
            4 * functools.reduce(lambda p, q: p * q, o) for o in outs
        )
        return pl.pallas_call(
            kernel,
            out_shape=[jax.ShapeDtypeStruct(o, F32) for o in outs],
            in_specs=[pl.BlockSpec(memory_space=space)] * len(args),
            out_specs=[pl.BlockSpec(memory_space=pltpu.VMEM)] * len(outs),
            scratch_shapes=[s if hasattr(s, "dtype") else pltpu.VMEM(*s) for s in scratch],
            cost_estimate=pl.CostEstimate(
                flops=flops, bytes_accessed=moved, transcendentals=0
            ),
            compiler_params=pltpu.CompilerParams(vmem_limit_bytes=mib * 2**20),
        )(*args)

    return run


def chunk_of(slots):
    for groups in (5, 4, 3, 2, 1):
        if slots % (groups * LANES) == 0:
            return groups * LANES


def is_odd(axis):
    return lax.rem(lax.axis_index(axis), 2) == 1


def row_and_depth(cells, nz):
    if nz & (nz - 1) == 0:
        return lax.shift_right_logical(cells, nz.bit_length() - 1), cells & (nz - 1)
    return lax.div(cells, jnp.int32(nz)), lax.rem(cells, jnp.int32(nz))


def pick(field, cells_ref, out_ref):
    _, rows, depth = field.shape
    slots = cells_ref.shape[1]
    blocks = slots // LANES
    chunk = chunk_of(slots)
    flat = field.reshape(3 * rows, depth)
    left = jnp.concatenate(split(flat, 2), axis=0)
    for start in range(0, slots, chunk):
        row, deep = row_and_depth(cells_ref[:, start : start + chunk], depth)
        right = ones_where(iota((depth, chunk), 0) == deep)
        found = mm(left, right)
        found = found[: 3 * rows] + found[3 * rows :]
        here = iota((rows, chunk), 0) == row
        for comp in range(3):
            part = jnp.where(here, found[comp * rows : (comp + 1) * rows], 0.0)
            line = jnp.sum(part, axis=0, keepdims=True)
            for piece in range(chunk // LANES):
                at = comp * blocks + start // LANES + piece
                out_ref[at : at + 1, :] = line[:, piece * LANES : (piece + 1) * LANES]
    pad = out_ref.shape[0] - 3 * blocks
    if pad:
        out_ref[3 * blocks :, :] = jnp.zeros((pad, LANES), F32)


def times_diag(d_ref, field):
    nx, ny, nz = d_ref.shape[1:]
    return jnp.stack(
        [
            sum(d_ref[3 * a + b] * field[b] for b in range(3)).reshape(nx * ny, nz)
            for a in range(3)
        ]
    )


def first_kernel(cells_hbm, v_hbm, d_hbm, out_ref, cells_ref, v_ref, d_ref, sem):
    pairs = ((cells_hbm, cells_ref), (v_hbm, v_ref), (d_hbm, d_ref))
    copies = [
        pltpu.make_async_copy(src, dst, sem.at[place])
        for place, (src, dst) in enumerate(pairs)
    ]
    for copy in copies:
        copy.start()
    for copy in copies:
        copy.wait()
    pick(times_diag(d_ref, [v_ref[b] for b in range(3)]), cells_ref, out_ref)


def spread_matrix(wells, width):
    shape = (wells, wells * width)
    gap = iota(shape, 1) - width * iota(shape, 0)
    return ones_where((gap >= 0) & (gap < width))


def last_matrix(wells, width, comp):
    shape = (wells * width, wells)
    return ones_where(iota(shape, 0) == width * iota(shape, 1) + (width - 3 + comp))


def prep_kernel(g_ref, couple_ref, h_ref, e_ref, apart_ref, part_ref):
    chunks, width, span_all = g_ref.shape
    wells = couple_ref.shape[2]
    span = width // 3
    for lane in range(0, span_all, LANES):
        part_ref[...] = g_ref[:, :, lane : lane + LANES]
        for comp in range(3):
            apart_ref[comp, :, :, lane : lane + LANES] = part_ref[
                :, pl.ds(comp, span, stride=3), :
            ]
    spread = spread_matrix(wells, width)
    heads = [g_ref[:, d, :] for d in range(3)]
    for b in range(3):
        total = sum(
            heads[d] * mm_exact(couple_ref[3 * d + b], spread)[:chunks] for d in range(3)
        )
        h_ref[b] = jnp.zeros(h_ref.shape[1:], F32)
        h_ref[b, :chunks, :] = total
        full = h_ref[b]
        for a in range(3):
            e_ref[3 * a + b] = mm_exact(full, last_matrix(wells, width, a))


def solve_kernel(
    idx_ref, own_ref, even_ref, next_ref, g_ref, h_ref, e_ref,
    keep_ref, to_even_ref, to_next_ref,
    pool_ref, r_ref, q_ref, tail_ref, p_ref, y_ref, ohr_ref, w_ref,
):
    _, chunks, span, span_all = g_ref.shape
    width = 3 * span
    wells = span_all // width
    slots = idx_ref.shape[1]
    blocks = slots // LANES
    rows = pool_ref.shape[1]
    tile = own_ref.shape[0] // 3
    group = wells * span
    odd_x, odd_y = is_odd("gx"), is_odd("gy")
    pool_ref[:, 9 * blocks :, :] = jnp.zeros((3, rows - 9 * blocks, LANES), F32)
    own, even, following = own_ref[...], even_ref[...], next_ref[...]
    columns = (
        jnp.where(odd_y, even, following), own, jnp.where(odd_y, following, even)
    )
    for b, column in enumerate(columns):
        own, even, following = column[:tile], column[tile : 2 * tile], column[2 * tile :]
        parts = (jnp.where(odd_x, even, following), own, jnp.where(odd_x, following, even))
        for a, part in enumerate(parts):
            for comp in range(3):
                at = (a * 3 + b) * blocks
                pool_ref[comp, at : at + blocks, :] = part[
                    comp * blocks : (comp + 1) * blocks
                ]
    pooled = pool_ref[...].reshape(3 * rows, LANES)
    left = jnp.concatenate(split(pooled, 2), axis=1)
    size = chunk_of(slots)
    r_ref[...] = jnp.zeros(r_ref.shape, F32)
    for start in range(0, slots, size):
        place = idx_ref[:, start : start + size]
        high = lax.shift_right_arithmetic(place, LANES.bit_length() - 1)
        low = place & (LANES - 1)
        right = ones_where((iota((2 * LANES, size), 0) & (LANES - 1)) == low)
        found = mm(left, right)
        here = iota((rows, size), 0) == high
        ohr_ref[:, start : start + size] = ones_where(here)
        for comp in range(3):
            part = jnp.where(here, found[comp * rows : (comp + 1) * rows], 0.0)
            line = jnp.sum(part, axis=0, keepdims=True)
            for piece in range(size // group):
                at = start // group + piece
                r_ref[comp, at : at + 1, :] = line[:, piece * group : (piece + 1) * group]
    two = (2 * group, span_all)
    well_of = lax.shift_right_logical(iota(two, 0) & (group - 1), (span - 1).bit_length())
    gap = iota(two, 1) - width * well_of
    spread = ones_where((gap >= 0) & (gap < width))
    own = (iota((span, group), 1) & (span - 1)) == iota((span, group), 0)
    total = None
    for comp in range(3):
        values = r_ref[comp][:chunks]
        wide = jnp.where(own[None], values[:, None, :], 0.0).reshape(chunks * span, group)
        lifted = mm(jnp.concatenate(split(wide, 2), axis=1), spread)
        lifted = lifted.reshape(chunks, span, span_all)
        part = g_ref[comp] * lifted
        total = part if total is None else total + part
    q_ref[...] = jnp.zeros(q_ref.shape, F32)
    q_ref[:chunks, :] = jnp.sum(total, axis=1)
    plain = q_ref[...]
    for a in range(3):
        tail_ref[a] = mm_exact(plain, last_matrix(wells, width, a))
    p_ref[...] = jnp.zeros(p_ref.shape, F32)
    state = [jnp.zeros((1, wells), F32)] * 3
    for c in range(chunks - 1):
        state = [
            tail_ref[a, c : c + 1, :]
            - (
                e_ref[3 * a, c : c + 1, :] * state[0]
                + e_ref[3 * a + 1, c : c + 1, :] * state[1]
                + e_ref[3 * a + 2, c : c + 1, :] * state[2]
            )
            for a in range(3)
        ]
        for a in range(3):
            p_ref[a, c + 1 : c + 2, :] = state[a]
    wide_well = spread_matrix(wells, width)
    for b in range(3):
        plain = plain - h_ref[b] * mm_exact(p_ref[b], wide_well)
    square = (span_all, span_all)
    lane = iota((1, span_all), 1)
    comp_of = lax.div(lane, jnp.int32(group))
    rest = lax.rem(lane, jnp.int32(group))
    source = width * lax.div(rest, jnp.int32(span)) + 3 * lax.rem(rest, jnp.int32(span)) + comp_of
    y_ref[...] = mm_exact(plain, ones_where(iota(square, 0) == source))
    for c in range(chunks):
        low = idx_ref[:, c * group : (c + 1) * group] & (LANES - 1)
        match = iota((LANES, group), 0) == low
        for comp in range(3):
            value = y_ref[c : c + 1, comp * group : (comp + 1) * group]
            for place, piece in enumerate(split(value, 2)):
                at = (place * 3 + comp) * LANES
                w_ref[at : at + LANES, c * group : (c + 1) * group] = jnp.where(
                    match, piece.astype(F32), 0.0
                ).astype(BF16)
    spread_out = mm(ohr_ref[...], w_ref[...], trans=True)
    spread_out = spread_out[:, : 3 * LANES] + spread_out[:, 3 * LANES :]
    pool_ref[0] = spread_out[:, :LANES]
    pool_ref[1] = spread_out[:, LANES : 2 * LANES]
    pool_ref[2] = spread_out[:, 2 * LANES :]
    for dst in (keep_ref, to_even_ref, to_next_ref):
        dst[...] = jnp.zeros(dst.shape, F32)
    for a in range(3):
        for comp in range(3):
            parts = []
            for b in range(3):
                at = (a * 3 + b) * blocks
                parts.append(pool_ref[comp, at : at + blocks, :])
            at = slice(a * tile + comp * blocks, a * tile + (comp + 1) * blocks)
            keep_ref[at, :] = parts[1]
            to_even_ref[at, :] = jnp.where(odd_y, parts[0], parts[2])
            to_next_ref[at, :] = jnp.where(odd_y, parts[2], parts[0])


def add_kernel(x_ref, y_ref, z_ref, keep_ref, to_even_ref, to_next_ref):
    tile = keep_ref.shape[0]
    odd_x = is_odd("gx")
    low, mid, high = [
        x_ref[part, :] + y_ref[part, :] + z_ref[part, :]
        for part in [slice(place * tile, (place + 1) * tile) for place in range(3)]
    ]
    keep_ref[...] = mid
    to_even_ref[...] = jnp.where(odd_x, low, high)
    to_next_ref[...] = jnp.where(odd_x, high, low)


def place_kernel(
    cells_ref, v_ref, inv_ref, x_ref, y_ref, z_ref,
    out_ref, x_even_ref, x_next_ref, y_even_ref, y_next_ref,
    left_ref, right_ref,
):
    (first_x, last_x), (first_y, last_y) = [
        (lax.axis_index(axis) == 0, lax.axis_index(axis) == lax.axis_size(axis) - 1)
        for axis in ("gx", "gy")
    ]
    odd_x, odd_y = is_odd("gx"), is_odd("gy")
    nx, ny, nz = v_ref.shape[1:]
    rows = nx * ny
    slots = cells_ref.shape[1]
    blocks = slots // LANES
    back = x_ref[...] + y_ref[...] + z_ref[...]
    pieces = [piece.astype(F32) for piece in split(back, 2)]
    for block in range(blocks):
        lanes = slice(block * LANES, (block + 1) * LANES)
        row, deep = row_and_depth(cells_ref[:, lanes], nz)
        here = iota((rows, LANES), 0) == row
        right_ref[:, lanes] = ones_where(iota((nz, LANES), 0) == deep)
        for place, piece in enumerate(pieces):
            for comp in range(3):
                at = comp * blocks + block
                group = (place * 3 + comp) * rows
                left_ref[group : group + rows, lanes] = jnp.where(
                    here, piece[at : at + 1, :], 0.0
                ).astype(BF16)
    placed = mm(left_ref[...], right_ref[...], trans=True)
    placed = placed[: 3 * rows] + placed[3 * rows :]
    for a in range(3):
        own = sum(inv_ref[3 * a + b] * v_ref[b] for b in range(3))
        out_ref[a] = own + placed[a * rows : (a + 1) * rows].reshape(nx, ny, nz)
        low = jnp.where(first_x, 0.0, out_ref[a, 0])
        high = jnp.where(last_x, 0.0, out_ref[a, nx - 1])
        x_even_ref[a] = jnp.where(odd_x, low, high)
        x_next_ref[a] = jnp.where(odd_x, high, low)
        low = jnp.where(first_y, 0.0, out_ref[a, :, 0, :])
        high = jnp.where(last_y, 0.0, out_ref[a, :, ny - 1, :])
        y_even_ref[a] = jnp.where(odd_y, low, high)
        y_next_ref[a] = jnp.where(odd_y, high, low)


def jacobian(z_ref, faces, d_ref, off_ref, store):
    nx, ny, nz = z_ref.shape[1:]
    odd_x, odd_y = is_odd("gx"), is_odd("gy")
    x_even, x_next, y_even, y_next = [face[...] for face in faces]
    xl, xh = jnp.where(odd_x, x_even, x_next), jnp.where(odd_x, x_next, x_even)
    yl, yh = jnp.where(odd_y, y_even, y_next), jnp.where(odd_y, y_next, y_even)
    row = iota((ny, nz), 0)
    lane = iota((ny, nz), 1)
    for x in range(nx):
        beside = []
        for b in range(3):
            own = z_ref[b, x]
            beside.append(
                [
                    z_ref[b, x - 1] if x else xl[b],
                    z_ref[b, x + 1] if x < nx - 1 else xh[b],
                    jnp.where(row == 0, yl[b, x : x + 1, :], pltpu.roll(own, 1, 0)),
                    jnp.where(row == ny - 1, yh[b, x : x + 1, :], pltpu.roll(own, ny - 1, 0)),
                    jnp.where(lane == 0, 0.0, pltpu.roll(own, 1, 1)),
                    jnp.where(lane == nz - 1, 0.0, pltpu.roll(own, nz - 1, 1)),
                ]
            )
        for a in range(3):
            total = sum(d_ref[3 * a + b, x] * z_ref[b, x] for b in range(3))
            for face in range(6):
                for b in range(3):
                    total = total + off_ref[face, 3 * a + b, x] * beside[b][face]
            store(a, x, total)


def next_kernel(
    cells_ref, z_ref, f0_ref, f1_ref, f2_ref, f3_ref, d_ref, off_ref, v_ref,
    w_ref, t_ref, out_ref,
):
    def store(a, x, value):
        w_ref[a, x] = value
        t_ref[a, x] = value - v_ref[a, x]

    jacobian(z_ref, (f0_ref, f1_ref, f2_ref, f3_ref), d_ref, off_ref, store)
    pick(times_diag(d_ref, [t_ref[b] for b in range(3)]), cells_ref, out_ref)


def gram_kernel(
    z_ref, f0_ref, f1_ref, f2_ref, f3_ref, d_ref, off_ref, v_ref, w1_ref,
    w_ref, sums_ref,
):
    def store(a, x, value):
        w_ref[a, x] = value

    jacobian(z_ref, (f0_ref, f1_ref, f2_ref, f3_ref), d_ref, off_ref, store)
    one, two, rhs = w1_ref[...], w_ref[...], v_ref[...]
    top_one = jnp.maximum(jnp.max(jnp.abs(one)), 1e-30)
    top_two = jnp.maximum(jnp.max(jnp.abs(two)), 1e-30)
    one = one * (1.0 / jnp.full((1, 1), top_one))
    two = two * (1.0 / jnp.full((1, 1), top_two))
    sums = [
        jnp.sum(one * one), jnp.sum(one * two), jnp.sum(two * two),
        jnp.sum(one * rhs), jnp.sum(two * rhs), top_one, top_two,
    ]
    line = iota(sums_ref.shape, 0)
    total = jnp.zeros(sums_ref.shape, F32)
    for place, value in enumerate(sums):
        total = jnp.where(line == place, value, total)
    sums_ref[...] = total


def final_kernel(
    sums_ref, v_ref, z1_ref, z2_ref, w1_ref, w2_ref, sol_ref, res_ref
):
    g11, g12, g22, r1, r2, top_one, top_two = [sums_ref[i : i + 1, :] for i in range(7)]
    det = g11 * g22 - g12 * g12
    y1 = ((g22 * r1 - g12 * r2) / det / top_one)[:, :1]
    y2 = ((g11 * r2 - g12 * r1) / det / top_two)[:, :1]
    sol_ref[...] = y1 * z1_ref[...] + y2 * z2_ref[...]
    res_ref[...] = v_ref[...] - y1 * w1_ref[...] - y2 * w2_ref[...]


def swap(axis, to_even, to_next):
    size = {name: lax.axis_size(name) for name in ("gx", "gy")}
    count, breadth = size[axis], size["gy" if axis == "gx" else "gx"]

    def device(along, across):
        return along * size["gy"] + across if axis == "gx" else across * size["gy"] + along

    out = []
    for first, value in ((0, to_even), (1, to_next)):
        pairs = []
        for across in range(breadth):
            for i in range(count):
                other = i + 1 if i % 2 == first else i - 1
                if 0 <= other < count:
                    pairs.append((device(i, across), device(other, across)))
                elif across ^ 1 < breadth:
                    pairs.append((device(i, across), device(i, across ^ 1)))
                else:
                    pairs.append((device(i, across), device(i, across)))
        out.append(lax.ppermute(value, ("gx", "gy"), pairs))
    return out


def merge_kernel(*refs):
    *parts, out_ref = refs
    parts = [part[...] for part in parts]
    tops = [[part[place : place + 1] for part in parts] for place in (5, 6)]
    top_one, top_two = [functools.reduce(jnp.maximum, top) for top in tops]
    line = iota(out_ref.shape, 0)
    total = None
    for part in parts:
        one, two = part[5:6] / top_one, part[6:7] / top_two
        scale = jnp.where(
            line == 0, one * one, jnp.where(
                line == 1, one * two, jnp.where(
                    line == 2, two * two, jnp.where(line == 3, one, two)
                )
            ),
        )
        part = part * scale
        total = part if total is None else total + part
    total = jnp.where(line == 5, top_one, jnp.where(line == 6, top_two, total))
    out_ref[...] = total


def merge_all(value, axis):
    count = lax.axis_size(axis)
    if count & (count - 1):
        every = lax.all_gather(value, axis)
        return call(merge_kernel, [value.shape])(*[every[i] for i in range(count)])[0]
    step = 1
    while step < count:
        radix = min(4, count // step)
        others = [
            lax.ppermute(value, axis, [(i, i ^ (k * step)) for i in range(count)])
            for k in range(1, radix)
        ]
        (value,) = call(merge_kernel, [value.shape])(value, *others)
        step *= radix
    return value


def body(
    right_side,
    diag_blocks,
    off_blocks,
    cell_inverse,
    send_cells,
    recv_index,
    seg_count,
    span_inverse,
    span_couple,
):
    _, nx, ny, nz = right_side.shape
    slots = send_cells.shape[1]
    wells, longest = recv_index.shape
    chunks, width, span_all = span_inverse.shape
    span = width // 3
    blocks = slots // LANES
    tile = round_up(3 * blocks, 16)
    rows = round_up(9 * blocks, 16)
    tall = round_up(chunks, 16)
    field = right_side.shape
    (picked,) = call(
        first_kernel,
        [(tile, LANES)],
        [
            (send_cells.shape, jnp.int32),
            (field, F32),
            (diag_blocks.shape, F32),
            pltpu.SemaphoreType.DMA((3,)),
        ],
        flops=10**9,
        space=pltpu.HBM,
        mib=60,
    )(send_cells, right_side, diag_blocks)
    live = jnp.arange(longest)[None, :] < seg_count[:, None]
    index = jnp.where(live, recv_index, -1)
    index = index.reshape(wells, chunks, span).transpose(1, 0, 2).reshape(1, wells * longest)
    couple = jnp.pad(span_couple.transpose(1, 0, 2), ((0, 0), (0, tall - chunks), (0, 0)))
    h, e, apart = call(
        prep_kernel,
        [(3, tall, span_all), (9, tall, wells), (3, chunks, span, span_all)],
        [((chunks, width, LANES), F32)],
    )(span_inverse, couple)

    def precondition(vector, picked):
        column = jnp.concatenate([picked, *swap("gx", picked, picked)], axis=0)
        even, following = swap("gy", column, column)
        keep, even, following = call(
            solve_kernel,
            [(3 * tile, LANES)] * 3,
            [
                ((3, rows, LANES), F32),
                ((3, tall, wells * span), F32),
                ((tall, span_all), F32),
                ((3, tall, wells), F32),
                ((3, tall, wells), F32),
                ((tall, span_all), F32),
                ((rows, slots), BF16),
                ((6 * LANES, slots), BF16),
            ],
            flops=4 * 10**9,
        )(index, column, even, following, apart, h, e)
        even, following = swap("gy", even, following)
        keep, even, following = call(add_kernel, [(tile, LANES)] * 3)(
            keep, even, following
        )
        even, following = swap("gx", even, following)
        z, *faces = call(
            place_kernel,
            [(3, nx, ny, nz)] + [(3, ny, nz)] * 2 + [(3, nx, nz)] * 2,
            [((6 * nx * ny, slots), BF16), ((nz, slots), BF16)],
            flops=10**9,
        )(send_cells, vector, cell_inverse, keep, even, following)
        return z, swap("gx", *faces[:2]) + swap("gy", *faces[2:])

    z1, faces = precondition(right_side, picked)
    w1, turned, picked = call(
        next_kernel, [field, field, (tile, LANES)], flops=10**9
    )(send_cells, z1, *faces, diag_blocks, off_blocks, right_side)
    z2, faces = precondition(turned, picked)
    w2, sums = call(gram_kernel, [field, (8, LANES)])(
        z2, *faces, diag_blocks, off_blocks, right_side, w1
    )
    sums = merge_all(merge_all(sums, "gy"), "gx")
    return tuple(
        call(final_kernel, [field, field])(sums, right_side, z1, z2, w1, w2)
    )


def solution(mesh):
    return jax.shard_map(
        body,
        mesh=mesh,
        in_specs=(
            P(None, "gx", "gy", None),
            P(None, "gx", "gy", None),
            P(None, None, "gx", "gy", None),
            P(None, "gx", "gy", None),
            P(("gx", "gy"), None),
            P(("gx", "gy"), None),
            P(("gx", "gy")),
            P(None, None, ("gx", "gy")),
            P(None, None, ("gx", "gy")),
        ),
        out_specs=(P(None, "gx", "gy", None), P(None, "gx", "gy", None)),
        check_vma=False,
    )
```

```python
import functools

import jax
import jax.numpy as jnp
from jax import lax
from jax.experimental import pallas as pl
from jax.experimental.pallas import tpu as pltpu
from jax.sharding import PartitionSpec as P

LANES = 128
F32 = jnp.float32
BF16 = jnp.bfloat16


def round_up(value, unit):
    return -(-value // unit) * unit


def iota(shape, dim):
    return lax.broadcasted_iota(jnp.int32, shape, dim)


def split(value, pieces):
    out = []
    for _ in range(pieces - 1):
        piece = value.astype(BF16)
        out.append(piece)
        value = value - piece.astype(F32)
    out.append(value.astype(BF16))
    return out


def mm(left, right, trans=False):
    dims = (((1,), (1 if trans else 0,)), ((), ()))
    return lax.dot_general(left, right, dims, preferred_element_type=F32)


def mm_exact(value, choice):
    total = None
    for piece in split(value, 3):
        part = mm(piece, choice)
        total = part if total is None else total + part
    return total


def ones_where(mask):
    return jnp.where(mask, 1.0, 0.0).astype(BF16)


def call(kernel, outs, scratch=(), flops=0, space=pltpu.VMEM, mib=40):
    def run(*args):
        shapes = [
            o if hasattr(o, "dtype") else jax.ShapeDtypeStruct(o, F32) for o in outs
        ]
        moved = sum(a.size * a.dtype.itemsize for a in (*args, *shapes))
        return pl.pallas_call(
            kernel,
            out_shape=shapes,
            in_specs=[pl.BlockSpec(memory_space=space)] * len(args),
            out_specs=[pl.BlockSpec(memory_space=pltpu.VMEM)] * len(outs),
            scratch_shapes=[s if hasattr(s, "dtype") else pltpu.VMEM(*s) for s in scratch],
            cost_estimate=pl.CostEstimate(
                flops=flops, bytes_accessed=moved, transcendentals=0
            ),
            compiler_params=pltpu.CompilerParams(vmem_limit_bytes=mib * 2**20),
        )(*args)

    return run


def chunk_of(slots):
    for groups in (5, 4, 3, 2, 1):
        if slots % (groups * LANES) == 0:
            return groups * LANES


def is_odd(axis):
    return lax.rem(lax.axis_index(axis), 2) == 1


def row_and_depth(cells, nz):
    if nz & (nz - 1) == 0:
        return lax.shift_right_logical(cells, nz.bit_length() - 1), cells & (nz - 1)
    return lax.div(cells, jnp.int32(nz)), lax.rem(cells, jnp.int32(nz))


def pick(field, cells_ref, deep_ref, out_ref):
    _, rows, depth = field.shape
    slots = cells_ref.shape[1]
    blocks = slots // LANES
    chunk = chunk_of(slots)
    left = jnp.concatenate(split(field.reshape(3 * rows, depth), 2), axis=1)
    for start in range(0, slots, chunk):
        row, _ = row_and_depth(cells_ref[:, start : start + chunk], depth)
        right = deep_ref[:, start : start + chunk]
        found = mm(left, jnp.concatenate([right, right], axis=0))
        here = iota((rows, chunk), 0) == row
        for comp in range(3):
            part = jnp.where(here, found[comp * rows : (comp + 1) * rows], 0.0)
            line = jnp.sum(part, axis=0, keepdims=True)
            for piece in range(chunk // LANES):
                at = comp * blocks + start // LANES + piece
                out_ref[at : at + 1, :] = line[:, piece * LANES : (piece + 1) * LANES]
    pad = out_ref.shape[0] - 3 * blocks
    if pad:
        out_ref[3 * blocks :, :] = jnp.zeros((pad, LANES), F32)


def one_hot(out_ref, values):
    chunk = chunk_of(out_ref.shape[1])
    for start in range(0, out_ref.shape[1], chunk):
        lanes = slice(start, start + chunk)
        out_ref[:, lanes] = ones_where(
            iota((out_ref.shape[0], chunk), 0) == values(lanes)
        )


def scaled(hot, lines):
    rows = hot.shape[0]
    out = []
    for place in range(2):
        for line in lines:
            piece = split(line, 2)[place].astype(F32)
            few = jnp.broadcast_to(piece, (16, piece.shape[1])).astype(BF16)
            out += [few * hot[at : at + 16] for at in range(0, rows, 16)]
    return jnp.concatenate(out, axis=0)


def times_diag(d_ref, field):
    nx, ny, nz = d_ref.shape[1:]
    return jnp.stack(
        [
            sum(d_ref[3 * a + b] * field[b] for b in range(3)).reshape(nx * ny, nz)
            for a in range(3)
        ]
    )


def first_kernel(
    cells_hbm, v_hbm, d_hbm, out_ref, cells_ref, v_ref, d_ref, deep_ref, sem
):
    pairs = ((cells_hbm, cells_ref), (v_hbm, v_ref), (d_hbm, d_ref))
    copies = [
        pltpu.make_async_copy(src, dst, sem.at[place])
        for place, (src, dst) in enumerate(pairs)
    ]
    for copy in copies:
        copy.start()
    copies[0].wait()
    depth = v_ref.shape[3]
    one_hot(deep_ref, lambda lanes: row_and_depth(cells_ref[:, lanes], depth)[1])
    copies[1].wait()
    copies[2].wait()
    pick(times_diag(d_ref, [v_ref[b] for b in range(3)]), cells_ref, deep_ref, out_ref)


def spread_matrix(wells, width):
    shape = (wells, wells * width)
    gap = iota(shape, 1) - width * iota(shape, 0)
    return ones_where((gap >= 0) & (gap < width))


def last_matrix(wells, width, comp):
    shape = (wells * width, wells)
    return ones_where(iota(shape, 0) == width * iota(shape, 1) + (width - 3 + comp))


def prep_kernel(
    idx_ref, cells_ref, g_ref, couple_ref,
    h_ref, e_ref, apart_ref, low_ref, high_ref, deep_ref, row_ref,
    part_ref,
):
    wide = low_ref.shape[0]
    depth = deep_ref.shape[0]
    one_hot(low_ref, lambda lanes: idx_ref[:, lanes] & (wide - 1))
    one_hot(
        high_ref,
        lambda lanes: lax.shift_right_arithmetic(idx_ref[:, lanes], wide.bit_length() - 1),
    )
    one_hot(row_ref, lambda lanes: row_and_depth(cells_ref[:, lanes], depth)[0])
    one_hot(deep_ref, lambda lanes: row_and_depth(cells_ref[:, lanes], depth)[1])
    chunks, width, span_all = g_ref.shape
    wells = couple_ref.shape[2]
    span = width // 3
    for lane in range(0, span_all, LANES):
        part_ref[...] = g_ref[:, :, lane : lane + LANES]
        for comp in range(3):
            apart_ref[comp, :, :, lane : lane + LANES] = part_ref[
                :, pl.ds(comp, span, stride=3), :
            ]
    spread = spread_matrix(wells, width)
    heads = [g_ref[:, d, :] for d in range(3)]
    for b in range(3):
        total = sum(
            heads[d] * mm_exact(couple_ref[3 * d + b], spread)[:chunks] for d in range(3)
        )
        h_ref[b] = jnp.zeros(h_ref.shape[1:], F32)
        h_ref[b, :chunks, :] = total
        full = h_ref[b]
        for a in range(3):
            e_ref[3 * a + b] = mm_exact(full, last_matrix(wells, width, a))


def solve_kernel(
    idx_ref, own_ref, even_ref, next_ref, g_ref, h_ref, e_ref, low_ref, high_ref,
    keep_ref, to_even_ref, to_next_ref,
    pool_ref, r_ref, q_ref, tail_ref, p_ref, y_ref,
):
    _, chunks, span, span_all = g_ref.shape
    width = 3 * span
    wells = span_all // width
    slots = idx_ref.shape[1]
    blocks = slots // LANES
    rows = pool_ref.shape[1]
    tile = own_ref.shape[0] // 3
    group = wells * span
    odd_x, odd_y = is_odd("gx"), is_odd("gy")
    pool_ref[:, 9 * blocks :, :] = jnp.zeros((3, rows - 9 * blocks, LANES), F32)
    own, even, following = own_ref[...], even_ref[...], next_ref[...]
    columns = (
        jnp.where(odd_y, even, following), own, jnp.where(odd_y, following, even)
    )
    for b, column in enumerate(columns):
        own, even, following = column[:tile], column[tile : 2 * tile], column[2 * tile :]
        parts = (jnp.where(odd_x, even, following), own, jnp.where(odd_x, following, even))
        for a, part in enumerate(parts):
            for comp in range(3):
                at = (a * 3 + b) * blocks
                pool_ref[comp, at : at + blocks, :] = part[
                    comp * blocks : (comp + 1) * blocks
                ]
    half = rows // 2
    wide = 2 * LANES
    pooled = jnp.concatenate(
        [
            jnp.concatenate(
                [pool_ref[comp, pl.ds(odd, half, stride=2), :] for odd in range(2)], axis=1
            )
            for comp in range(3)
        ],
        axis=0,
    )
    left = jnp.concatenate(split(pooled, 2), axis=1)
    size = chunk_of(slots)
    r_ref[...] = jnp.zeros(r_ref.shape, F32)
    for start in range(0, slots, size):
        place = idx_ref[:, start : start + size]
        right = low_ref[:, start : start + size]
        found = mm(left, jnp.concatenate([right, right], axis=0))
        here = iota((half, size), 0) == lax.shift_right_arithmetic(place, wide.bit_length() - 1)
        for comp in range(3):
            part = jnp.where(here, found[comp * half : (comp + 1) * half], 0.0)
            line = jnp.sum(part, axis=0, keepdims=True)
            for piece in range(size // group):
                at = start // group + piece
                r_ref[comp, at : at + 1, :] = line[:, piece * group : (piece + 1) * group]
    two = (2 * group, span_all)
    well_of = lax.shift_right_logical(iota(two, 0) & (group - 1), (span - 1).bit_length())
    gap = iota(two, 1) - width * well_of
    spread = ones_where((gap >= 0) & (gap < width))
    own = (iota((span, group), 1) & (span - 1)) == iota((span, group), 0)
    total = None
    for comp in range(3):
        values = r_ref[comp][:chunks]
        wide = jnp.where(own[None], values[:, None, :], 0.0).reshape(chunks * span, group)
        lifted = mm(jnp.concatenate(split(wide, 2), axis=1), spread)
        lifted = lifted.reshape(chunks, span, span_all)
        part = g_ref[comp] * lifted
        total = part if total is None else total + part
    q_ref[...] = jnp.zeros(q_ref.shape, F32)
    q_ref[:chunks, :] = jnp.sum(total, axis=1)
    plain = q_ref[...]
    for a in range(3):
        tail_ref[a] = mm_exact(plain, last_matrix(wells, width, a))
    p_ref[...] = jnp.zeros(p_ref.shape, F32)
    state = [jnp.zeros((1, wells), F32)] * 3
    for c in range(chunks - 1):
        state = [
            tail_ref[a, c : c + 1, :]
            - (
                e_ref[3 * a, c : c + 1, :] * state[0]
                + e_ref[3 * a + 1, c : c + 1, :] * state[1]
                + e_ref[3 * a + 2, c : c + 1, :] * state[2]
            )
            for a in range(3)
        ]
        for a in range(3):
            p_ref[a, c + 1 : c + 2, :] = state[a]
    wide_well = spread_matrix(wells, width)
    for b in range(3):
        plain = plain - h_ref[b] * mm_exact(p_ref[b], wide_well)
    square = (span_all, span_all)
    lane = iota((1, span_all), 1)
    comp_of = lax.div(lane, jnp.int32(group))
    rest = lax.rem(lane, jnp.int32(group))
    source = width * lax.div(rest, jnp.int32(span)) + 3 * lax.rem(rest, jnp.int32(span)) + comp_of
    y_ref[...] = mm_exact(plain, ones_where(iota(square, 0) == source))
    spread_out = None
    for start in range(0, slots, size):
        lanes = slice(start, start + size)
        steps = range(start // group, (start + size) // group)
        lines = [
            jnp.concatenate(
                [y_ref[c : c + 1, comp * group : (comp + 1) * group] for c in steps], axis=1
            )
            for comp in range(3)
        ]
        part = mm(scaled(high_ref[:, lanes], lines), low_ref[:, lanes], trans=True)
        spread_out = part if spread_out is None else spread_out + part
    spread_out = spread_out[: 3 * half] + spread_out[3 * half :]
    for comp in range(3):
        block = spread_out[comp * half : (comp + 1) * half]
        for odd in range(2):
            pool_ref[comp, pl.ds(odd, half, stride=2), :] = block[
                :, odd * LANES : (odd + 1) * LANES
            ]
    for dst in (keep_ref, to_even_ref, to_next_ref):
        dst[...] = jnp.zeros(dst.shape, F32)
    for a in range(3):
        for comp in range(3):
            parts = []
            for b in range(3):
                at = (a * 3 + b) * blocks
                parts.append(pool_ref[comp, at : at + blocks, :])
            at = slice(a * tile + comp * blocks, a * tile + (comp + 1) * blocks)
            keep_ref[at, :] = parts[1]
            to_even_ref[at, :] = jnp.where(odd_y, parts[0], parts[2])
            to_next_ref[at, :] = jnp.where(odd_y, parts[2], parts[0])


def add_kernel(x_ref, y_ref, z_ref, keep_ref, to_even_ref, to_next_ref):
    tile = keep_ref.shape[0]
    odd_x = is_odd("gx")
    low, mid, high = [
        x_ref[part, :] + y_ref[part, :] + z_ref[part, :]
        for part in [slice(place * tile, (place + 1) * tile) for place in range(3)]
    ]
    keep_ref[...] = mid
    to_even_ref[...] = jnp.where(odd_x, low, high)
    to_next_ref[...] = jnp.where(odd_x, high, low)


def place_kernel(
    row_ref, deep_ref, v_ref, inv_ref, x_ref, y_ref, z_ref,
    out_ref, x_even_ref, x_next_ref, y_even_ref, y_next_ref,
):
    (first_x, last_x), (first_y, last_y) = [
        (lax.axis_index(axis) == 0, lax.axis_index(axis) == lax.axis_size(axis) - 1)
        for axis in ("gx", "gy")
    ]
    odd_x, odd_y = is_odd("gx"), is_odd("gy")
    nx, ny, nz = v_ref.shape[1:]
    rows = nx * ny
    slots = row_ref.shape[1]
    blocks = slots // LANES
    back = x_ref[...] + y_ref[...] + z_ref[...]
    size = chunk_of(slots)
    placed = None
    for start in range(0, slots, size):
        lanes = slice(start, start + size)
        steps = range(start // LANES, (start + size) // LANES)
        lines = [
            jnp.concatenate(
                [back[comp * blocks + at : comp * blocks + at + 1] for at in steps], axis=1
            )
            for comp in range(3)
        ]
        part = mm(scaled(row_ref[:, lanes], lines), deep_ref[:, lanes], trans=True)
        placed = part if placed is None else placed + part
    placed = placed[: 3 * rows] + placed[3 * rows :]
    for a in range(3):
        own = sum(inv_ref[3 * a + b] * v_ref[b] for b in range(3))
        out_ref[a] = own + placed[a * rows : (a + 1) * rows].reshape(nx, ny, nz)
        low = jnp.where(first_x, 0.0, out_ref[a, 0])
        high = jnp.where(last_x, 0.0, out_ref[a, nx - 1])
        x_even_ref[a] = jnp.where(odd_x, low, high)
        x_next_ref[a] = jnp.where(odd_x, high, low)
        low = jnp.where(first_y, 0.0, out_ref[a, :, 0, :])
        high = jnp.where(last_y, 0.0, out_ref[a, :, ny - 1, :])
        y_even_ref[a] = jnp.where(odd_y, low, high)
        y_next_ref[a] = jnp.where(odd_y, high, low)


def inner_kernel(z_ref, d_ref, off_ref, w_ref):
    nx, ny, nz = z_ref.shape[1:]
    row = iota((ny, nz), 0)
    lane = iota((ny, nz), 1)
    for x in range(nx):
        beside = []
        for b in range(3):
            own = z_ref[b, x]
            beside.append(
                [
                    z_ref[b, x - 1] if x else None,
                    z_ref[b, x + 1] if x < nx - 1 else None,
                    jnp.where(row == 0, 0.0, pltpu.roll(own, 1, 0)),
                    jnp.where(row == ny - 1, 0.0, pltpu.roll(own, ny - 1, 0)),
                    jnp.where(lane == 0, 0.0, pltpu.roll(own, 1, 1)),
                    jnp.where(lane == nz - 1, 0.0, pltpu.roll(own, nz - 1, 1)),
                ]
            )
        for a in range(3):
            total = sum(d_ref[3 * a + b, x] * z_ref[b, x] for b in range(3))
            for face in range(6):
                for b in range(3):
                    if beside[b][face] is not None:
                        total = total + off_ref[face, 3 * a + b, x] * beside[b][face]
            w_ref[a, x] = total


def add_faces(part_ref, faces, off_ref, w_ref):
    nx, ny, nz = part_ref.shape[1:]
    odd_x, odd_y = is_odd("gx"), is_odd("gy")
    x_even, x_next, y_even, y_next = [face[...] for face in faces]
    xl, xh = jnp.where(odd_x, x_even, x_next), jnp.where(odd_x, x_next, x_even)
    yl, yh = jnp.where(odd_y, y_even, y_next), jnp.where(odd_y, y_next, y_even)
    for a in range(3):
        w_ref[a] = part_ref[a]
        for x, face, beside in ((0, 0, xl), (nx - 1, 1, xh)):
            w_ref[a, x] += sum(off_ref[face, 3 * a + b, x] * beside[b] for b in range(3))
        for y, face, beside in ((0, 2, yl), (ny - 1, 3, yh)):
            w_ref[a, :, y, :] += sum(
                off_ref[face, 3 * a + b, :, y, :] * beside[b] for b in range(3)
            )


def next_kernel(
    cells_ref, deep_ref, part_ref, f0_ref, f1_ref, f2_ref, f3_ref, d_ref, off_ref, v_ref,
    w_ref, t_ref, out_ref,
):
    add_faces(part_ref, (f0_ref, f1_ref, f2_ref, f3_ref), off_ref, w_ref)
    t_ref[...] = w_ref[...] - v_ref[...]
    pick(times_diag(d_ref, [t_ref[b] for b in range(3)]), cells_ref, deep_ref, out_ref)


def gram_kernel(
    part_ref, f0_ref, f1_ref, f2_ref, f3_ref, off_ref, v_ref, w1_ref,
    w_ref, sums_ref,
):
    add_faces(part_ref, (f0_ref, f1_ref, f2_ref, f3_ref), off_ref, w_ref)
    one, two, rhs = w1_ref[...], w_ref[...], v_ref[...]
    top_one = jnp.maximum(jnp.max(jnp.abs(one)), 1e-30)
    top_two = jnp.maximum(jnp.max(jnp.abs(two)), 1e-30)
    one = one * (1.0 / jnp.full((1, 1), top_one))
    two = two * (1.0 / jnp.full((1, 1), top_two))
    sums = [
        jnp.sum(one * one), jnp.sum(one * two), jnp.sum(two * two),
        jnp.sum(one * rhs), jnp.sum(two * rhs), top_one, top_two,
    ]
    line = iota(sums_ref.shape, 0)
    total = jnp.zeros(sums_ref.shape, F32)
    for place, value in enumerate(sums):
        total = jnp.where(line == place, value, total)
    sums_ref[...] = total


def final_kernel(
    sums_ref, v_ref, z1_ref, z2_ref, w1_ref, w2_ref, sol_ref, res_ref
):
    g11, g12, g22, r1, r2, top_one, top_two = [sums_ref[i : i + 1, :] for i in range(7)]
    det = g11 * g22 - g12 * g12
    y1 = ((g22 * r1 - g12 * r2) / det / top_one)[:, :1]
    y2 = ((g11 * r2 - g12 * r1) / det / top_two)[:, :1]
    sol_ref[...] = y1 * z1_ref[...] + y2 * z2_ref[...]
    res_ref[...] = v_ref[...] - y1 * w1_ref[...] - y2 * w2_ref[...]


def swap(axis, to_even, to_next):
    size = {name: lax.axis_size(name) for name in ("gx", "gy")}
    count, breadth = size[axis], size["gy" if axis == "gx" else "gx"]

    def device(along, across):
        return along * size["gy"] + across if axis == "gx" else across * size["gy"] + along

    out = []
    order = [(0, to_even), (1, to_next)]
    same = to_even is to_next
    for first, value in order if same else order[::-1]:
        pairs = []
        for across in range(breadth):
            for i in range(count):
                other = i + 1 if i % 2 == first else i - 1
                if 0 <= other < count:
                    pairs.append((device(i, across), device(other, across)))
                elif across ^ 1 < breadth:
                    pairs.append((device(i, across), device(i, across ^ 1)))
                else:
                    pairs.append((device(i, across), device(i, across)))
        out.append(lax.ppermute(value, ("gx", "gy"), pairs))
    return out if same else out[::-1]


def merge_kernel(*refs):
    *parts, out_ref = refs
    parts = [part[...] for part in parts]
    tops = [[part[place : place + 1] for part in parts] for place in (5, 6)]
    top_one, top_two = [functools.reduce(jnp.maximum, top) for top in tops]
    line = iota(out_ref.shape, 0)
    total = None
    for part in parts:
        one, two = part[5:6] / top_one, part[6:7] / top_two
        scale = jnp.where(
            line == 0, one * one, jnp.where(
                line == 1, one * two, jnp.where(
                    line == 2, two * two, jnp.where(line == 3, one, two)
                )
            ),
        )
        part = part * scale
        total = part if total is None else total + part
    total = jnp.where(line == 5, top_one, jnp.where(line == 6, top_two, total))
    out_ref[...] = total


def merge_all(value, axis):
    count = lax.axis_size(axis)
    if count & (count - 1):
        every = lax.all_gather(value, axis)
        return call(merge_kernel, [value.shape])(*[every[i] for i in range(count)])[0]
    step = 1
    while step < count:
        radix = min(4, count // step)
        others = [
            lax.ppermute(value, axis, [(i, i ^ (k * step)) for i in range(count)])
            for k in range(1, radix)
        ]
        (value,) = call(merge_kernel, [value.shape])(value, *others)
        step *= radix
    return value


def body(
    right_side,
    diag_blocks,
    off_blocks,
    cell_inverse,
    send_cells,
    recv_index,
    seg_count,
    span_inverse,
    span_couple,
):
    _, nx, ny, nz = right_side.shape
    slots = send_cells.shape[1]
    wells, longest = recv_index.shape
    chunks, width, span_all = span_inverse.shape
    span = width // 3
    blocks = slots // LANES
    tile = round_up(3 * blocks, 16)
    rows = round_up(9 * blocks, 32)
    tall = round_up(chunks, 16)
    field = right_side.shape
    (picked,) = call(
        first_kernel,
        [(tile, LANES)],
        [
            (send_cells.shape, jnp.int32),
            (field, F32),
            (diag_blocks.shape, F32),
            ((nz, slots), BF16),
            pltpu.SemaphoreType.DMA((3,)),
        ],
        flops=10**9,
        space=pltpu.HBM,
        mib=60,
    )(send_cells, right_side, diag_blocks)
    live = jnp.arange(longest)[None, :] < seg_count[:, None]
    index = jnp.where(live, recv_index, -1)
    index = index.reshape(wells, chunks, span).transpose(1, 0, 2).reshape(1, wells * longest)
    couple = jnp.pad(span_couple.transpose(1, 0, 2), ((0, 0), (0, tall - chunks), (0, 0)))
    h, e, apart, low, high, deep, row = call(
        prep_kernel,
        [(3, tall, span_all), (9, tall, wells), (3, chunks, span, span_all)]
        + [
            jax.ShapeDtypeStruct((height, slots), BF16)
            for height in (2 * LANES, rows // 2, nz, nx * ny)
        ],
        [((chunks, width, LANES), F32)],
    )(index, send_cells, span_inverse, couple)

    def precondition(vector, picked):
        column = jnp.concatenate([picked, *swap("gx", picked, picked)], axis=0)
        even, following = swap("gy", column, column)
        keep, even, following = call(
            solve_kernel,
            [(3 * tile, LANES)] * 3,
            [
                ((3, rows, LANES), F32),
                ((3, tall, wells * span), F32),
                ((tall, span_all), F32),
                ((3, tall, wells), F32),
                ((3, tall, wells), F32),
                ((tall, span_all), F32),
            ],
            flops=4 * 10**9,
        )(index, column, even, following, apart, h, e, low, high)
        even, following = swap("gy", even, following)
        keep, even, following = call(add_kernel, [(tile, LANES)] * 3)(
            keep, even, following
        )
        even, following = swap("gx", even, following)
        z, *faces = call(
            place_kernel,
            [(3, nx, ny, nz)] + [(3, ny, nz)] * 2 + [(3, nx, nz)] * 2,
            flops=10**9,
        )(row, deep, vector, cell_inverse, keep, even, following)
        faces = swap("gx", *faces[:2]) + swap("gy", *faces[2:])
        (part,) = call(inner_kernel, [field], flops=10**7)(z, diag_blocks, off_blocks)
        return z, part, faces

    z1, part, faces = precondition(right_side, picked)
    w1, turned, picked = call(
        next_kernel, [field, field, (tile, LANES)], flops=10**9
    )(send_cells, deep, part, *faces, diag_blocks, off_blocks, right_side)
    z2, part, faces = precondition(turned, picked)
    w2, sums = call(gram_kernel, [field, (8, LANES)])(
        part, *faces, off_blocks, right_side, w1
    )
    sums = merge_all(merge_all(sums, "gy"), "gx")
    return tuple(
        call(final_kernel, [field, field])(sums, right_side, z1, z2, w1, w2)
    )


def solution(mesh):
    return jax.shard_map(
        body,
        mesh=mesh,
        in_specs=(
            P(None, "gx", "gy", None),
            P(None, "gx", "gy", None),
            P(None, None, "gx", "gy", None),
            P(None, "gx", "gy", None),
            P(("gx", "gy"), None),
            P(("gx", "gy"), None),
            P(("gx", "gy")),
            P(None, None, ("gx", "gy")),
            P(None, None, ("gx", "gy")),
        ),
        out_specs=(P(None, "gx", "gy", None), P(None, "gx", "gy", None)),
        check_vma=False,
    )
```

```python
import functools

import jax
import jax.numpy as jnp
from jax import lax
from jax.experimental import pallas as pl
from jax.experimental.pallas import tpu as pltpu
from jax.sharding import PartitionSpec as P

LANES = 128
F32 = jnp.float32
BF16 = jnp.bfloat16


def round_up(value, unit):
    return -(-value // unit) * unit


def iota(shape, dim):
    return lax.broadcasted_iota(jnp.int32, shape, dim)


def split(value, pieces):
    out = []
    for _ in range(pieces - 1):
        piece = value.astype(BF16)
        out.append(piece)
        value = value - piece.astype(F32)
    out.append(value.astype(BF16))
    return out


def mm(left, right, trans=False):
    dims = (((1,), (1 if trans else 0,)), ((), ()))
    return lax.dot_general(left, right, dims, preferred_element_type=F32)


def mm_exact(value, choice):
    total = None
    for piece in split(value, 3):
        part = mm(piece, choice)
        total = part if total is None else total + part
    return total


def ones_where(mask):
    return jnp.where(mask, 1.0, 0.0).astype(BF16)


def call(kernel, outs, scratch=(), flops=0, space=pltpu.VMEM, mib=40):
    def run(*args):
        shapes = [
            o if hasattr(o, "dtype") else jax.ShapeDtypeStruct(o, F32) for o in outs
        ]
        moved = sum(a.size * a.dtype.itemsize for a in (*args, *shapes))
        return pl.pallas_call(
            kernel,
            out_shape=shapes,
            in_specs=[pl.BlockSpec(memory_space=space)] * len(args),
            out_specs=[pl.BlockSpec(memory_space=pltpu.VMEM)] * len(outs),
            scratch_shapes=[s if hasattr(s, "dtype") else pltpu.VMEM(*s) for s in scratch],
            cost_estimate=pl.CostEstimate(
                flops=flops, bytes_accessed=moved, transcendentals=0
            ),
            compiler_params=pltpu.CompilerParams(vmem_limit_bytes=mib * 2**20),
        )(*args)

    return run


def chunk_of(slots):
    for groups in (5, 4, 3, 2, 1):
        if slots % (groups * LANES) == 0:
            return groups * LANES


def is_odd(axis):
    return lax.rem(lax.axis_index(axis), 2) == 1


def row_and_depth(cells, nz):
    if nz & (nz - 1) == 0:
        return lax.shift_right_logical(cells, nz.bit_length() - 1), cells & (nz - 1)
    return lax.div(cells, jnp.int32(nz)), lax.rem(cells, jnp.int32(nz))


def pick(field, cells_ref, deep_ref, out_ref):
    _, rows, depth = field.shape
    slots = cells_ref.shape[1]
    blocks = slots // LANES
    chunk = chunk_of(slots)
    left = jnp.concatenate(split(field.reshape(3 * rows, depth), 2), axis=1)
    for start in range(0, slots, chunk):
        row, _ = row_and_depth(cells_ref[:, start : start + chunk], depth)
        right = deep_ref[:, start : start + chunk]
        found = mm(left, jnp.concatenate([right, right], axis=0))
        here = iota((rows, chunk), 0) == row
        for comp in range(3):
            part = jnp.where(here, found[comp * rows : (comp + 1) * rows], 0.0)
            line = jnp.sum(part, axis=0, keepdims=True)
            for piece in range(chunk // LANES):
                at = comp * blocks + start // LANES + piece
                out_ref[at : at + 1, :] = line[:, piece * LANES : (piece + 1) * LANES]
    pad = out_ref.shape[0] - 3 * blocks
    if pad:
        out_ref[3 * blocks :, :] = jnp.zeros((pad, LANES), F32)


def one_hot(out_ref, values):
    chunk = chunk_of(out_ref.shape[1])
    for start in range(0, out_ref.shape[1], chunk):
        lanes = slice(start, start + chunk)
        out_ref[:, lanes] = ones_where(
            iota((out_ref.shape[0], chunk), 0) == values(lanes)
        )


def scaled(hot, lines):
    rows = hot.shape[0]
    out = []
    for place in range(2):
        for line in lines:
            piece = split(line, 2)[place].astype(F32)
            few = jnp.broadcast_to(piece, (16, piece.shape[1])).astype(BF16)
            out += [few * hot[at : at + 16] for at in range(0, rows, 16)]
    return jnp.concatenate(out, axis=0)


def times_diag(d_ref, field):
    nx, ny, nz = d_ref.shape[1:]
    return jnp.stack(
        [
            sum(d_ref[3 * a + b] * field[b] for b in range(3)).reshape(nx * ny, nz)
            for a in range(3)
        ]
    )


def first_kernel(
    cells_hbm, v_hbm, d_hbm, out_ref, cells_ref, v_ref, d_ref, deep_ref, sem
):
    pairs = [(cells_hbm, cells_ref), (v_hbm, v_ref)]
    pairs += [(d_hbm.at[entry], d_ref.at[entry]) for entry in range(9)]
    copies = [
        pltpu.make_async_copy(src, dst, sem.at[place])
        for place, (src, dst) in enumerate(pairs)
    ]
    for copy in copies:
        copy.start()
    copies[0].wait()
    depth = v_ref.shape[3]
    one_hot(deep_ref, lambda lanes: row_and_depth(cells_ref[:, lanes], depth)[1])
    for copy in copies[1:]:
        copy.wait()
    pick(times_diag(d_ref, [v_ref[b] for b in range(3)]), cells_ref, deep_ref, out_ref)


def hold_kernel(value_ref, out_ref):
    out_ref[...] = value_ref[...]


def spread_matrix(wells, width):
    shape = (wells, wells * width)
    gap = iota(shape, 1) - width * iota(shape, 0)
    return ones_where((gap >= 0) & (gap < width))


def last_matrix(wells, width, comp):
    shape = (wells * width, wells)
    return ones_where(iota(shape, 0) == width * iota(shape, 1) + (width - 3 + comp))


def prep_kernel(
    idx_ref, cells_ref, g_ref, couple_ref,
    h_ref, e_ref, apart_ref, low_ref, high_ref, deep_ref, row_ref,
    part_ref,
):
    wide = low_ref.shape[0]
    depth = deep_ref.shape[0]
    one_hot(low_ref, lambda lanes: idx_ref[:, lanes] & (wide - 1))
    one_hot(
        high_ref,
        lambda lanes: lax.shift_right_arithmetic(idx_ref[:, lanes], wide.bit_length() - 1),
    )
    one_hot(row_ref, lambda lanes: row_and_depth(cells_ref[:, lanes], depth)[0])
    one_hot(deep_ref, lambda lanes: row_and_depth(cells_ref[:, lanes], depth)[1])
    chunks, width, span_all = g_ref.shape
    wells = couple_ref.shape[2]
    span = width // 3
    for lane in range(0, span_all, LANES):
        part_ref[...] = g_ref[:, :, lane : lane + LANES]
        for comp in range(3):
            apart_ref[comp, :, :, lane : lane + LANES] = part_ref[
                :, pl.ds(comp, span, stride=3), :
            ]
    spread = spread_matrix(wells, width)
    heads = [g_ref[:, d, :] for d in range(3)]
    for b in range(3):
        total = sum(
            heads[d] * mm_exact(couple_ref[3 * d + b], spread)[:chunks] for d in range(3)
        )
        h_ref[b] = jnp.zeros(h_ref.shape[1:], F32)
        h_ref[b, :chunks, :] = total
        full = h_ref[b]
        for a in range(3):
            e_ref[3 * a + b] = mm_exact(full, last_matrix(wells, width, a))


def solve_kernel(
    idx_ref, own_ref, even_ref, next_ref, g_ref, h_ref, e_ref, low_ref, high_ref,
    keep_ref, to_next_ref, to_even_ref,
    pool_ref, r_ref, q_ref, tail_ref, p_ref, y_ref,
):
    _, chunks, span, span_all = g_ref.shape
    width = 3 * span
    wells = span_all // width
    slots = idx_ref.shape[1]
    blocks = slots // LANES
    rows = pool_ref.shape[1]
    tile = own_ref.shape[0] // 3
    group = wells * span
    odd_x, odd_y = is_odd("gx"), is_odd("gy")
    pool_ref[:, 9 * blocks :, :] = jnp.zeros((3, rows - 9 * blocks, LANES), F32)
    own, even, following = own_ref[...], even_ref[...], next_ref[...]
    columns = (
        jnp.where(odd_y, even, following), own, jnp.where(odd_y, following, even)
    )
    for b, column in enumerate(columns):
        own, even, following = column[:tile], column[tile : 2 * tile], column[2 * tile :]
        parts = (jnp.where(odd_x, even, following), own, jnp.where(odd_x, following, even))
        for a, part in enumerate(parts):
            for comp in range(3):
                at = (a * 3 + b) * blocks
                pool_ref[comp, at : at + blocks, :] = part[
                    comp * blocks : (comp + 1) * blocks
                ]
    half = rows // 2
    wide = 2 * LANES
    pooled = jnp.concatenate(
        [
            jnp.concatenate(
                [pool_ref[comp, pl.ds(odd, half, stride=2), :] for odd in range(2)], axis=1
            )
            for comp in range(3)
        ],
        axis=0,
    )
    left = jnp.concatenate(split(pooled, 2), axis=1)
    size = chunk_of(slots)
    r_ref[...] = jnp.zeros(r_ref.shape, F32)
    for start in range(0, slots, size):
        place = idx_ref[:, start : start + size]
        right = low_ref[:, start : start + size]
        found = mm(left, jnp.concatenate([right, right], axis=0))
        here = iota((half, size), 0) == lax.shift_right_arithmetic(place, wide.bit_length() - 1)
        for comp in range(3):
            part = jnp.where(here, found[comp * half : (comp + 1) * half], 0.0)
            line = jnp.sum(part, axis=0, keepdims=True)
            for piece in range(size // group):
                at = start // group + piece
                r_ref[comp, at : at + 1, :] = line[:, piece * group : (piece + 1) * group]
    two = (2 * group, span_all)
    well_of = lax.shift_right_logical(iota(two, 0) & (group - 1), (span - 1).bit_length())
    gap = iota(two, 1) - width * well_of
    spread = ones_where((gap >= 0) & (gap < width))
    own = (iota((span, group), 1) & (span - 1)) == iota((span, group), 0)
    total = None
    for comp in range(3):
        values = r_ref[comp][:chunks]
        wide = jnp.where(own[None], values[:, None, :], 0.0).reshape(chunks * span, group)
        lifted = mm(jnp.concatenate(split(wide, 2), axis=1), spread)
        lifted = lifted.reshape(chunks, span, span_all)
        part = g_ref[comp] * lifted
        total = part if total is None else total + part
    q_ref[...] = jnp.zeros(q_ref.shape, F32)
    q_ref[:chunks, :] = jnp.sum(total, axis=1)
    plain = q_ref[...]
    for a in range(3):
        tail_ref[a] = mm_exact(plain, last_matrix(wells, width, a))
    p_ref[...] = jnp.zeros(p_ref.shape, F32)
    state = [jnp.zeros((1, wells), F32)] * 3
    for c in range(chunks - 1):
        state = [
            tail_ref[a, c : c + 1, :]
            - (
                e_ref[3 * a, c : c + 1, :] * state[0]
                + e_ref[3 * a + 1, c : c + 1, :] * state[1]
                + e_ref[3 * a + 2, c : c + 1, :] * state[2]
            )
            for a in range(3)
        ]
        for a in range(3):
            p_ref[a, c + 1 : c + 2, :] = state[a]
    wide_well = spread_matrix(wells, width)
    for b in range(3):
        plain = plain - h_ref[b] * mm_exact(p_ref[b], wide_well)
    square = (span_all, span_all)
    lane = iota((1, span_all), 1)
    comp_of = lax.div(lane, jnp.int32(group))
    rest = lax.rem(lane, jnp.int32(group))
    source = width * lax.div(rest, jnp.int32(span)) + 3 * lax.rem(rest, jnp.int32(span)) + comp_of
    y_ref[...] = mm_exact(plain, ones_where(iota(square, 0) == source))
    spread_out = None
    for start in range(0, slots, size):
        lanes = slice(start, start + size)
        steps = range(start // group, (start + size) // group)
        lines = [
            jnp.concatenate(
                [y_ref[c : c + 1, comp * group : (comp + 1) * group] for c in steps], axis=1
            )
            for comp in range(3)
        ]
        part = mm(scaled(high_ref[:, lanes], lines), low_ref[:, lanes], trans=True)
        spread_out = part if spread_out is None else spread_out + part
    spread_out = spread_out[: 3 * half] + spread_out[3 * half :]
    for comp in range(3):
        block = spread_out[comp * half : (comp + 1) * half]
        for odd in range(2):
            pool_ref[comp, pl.ds(odd, half, stride=2), :] = block[
                :, odd * LANES : (odd + 1) * LANES
            ]
    for dst in (keep_ref, to_even_ref, to_next_ref):
        dst[...] = jnp.zeros(dst.shape, F32)
    for a in range(3):
        for comp in range(3):
            parts = []
            for b in range(3):
                at = (a * 3 + b) * blocks
                parts.append(pool_ref[comp, at : at + blocks, :])
            at = slice(a * tile + comp * blocks, a * tile + (comp + 1) * blocks)
            keep_ref[at, :] = parts[1]
            to_even_ref[at, :] = jnp.where(odd_y, parts[0], parts[2])
            to_next_ref[at, :] = jnp.where(odd_y, parts[2], parts[0])


def add_kernel(x_ref, y_ref, z_ref, keep_ref, to_next_ref, to_even_ref):
    tile = keep_ref.shape[0]
    odd_x = is_odd("gx")
    low, mid, high = [
        x_ref[part, :] + y_ref[part, :] + z_ref[part, :]
        for part in [slice(place * tile, (place + 1) * tile) for place in range(3)]
    ]
    keep_ref[...] = mid
    to_even_ref[...] = jnp.where(odd_x, low, high)
    to_next_ref[...] = jnp.where(odd_x, high, low)


def place_kernel(
    row_ref, deep_ref, v_ref, inv_ref, x_ref, y_ref, z_ref,
    out_ref, x_next_ref, x_even_ref, y_next_ref, y_even_ref,
):
    (first_x, last_x), (first_y, last_y) = [
        (lax.axis_index(axis) == 0, lax.axis_index(axis) == lax.axis_size(axis) - 1)
        for axis in ("gx", "gy")
    ]
    odd_x, odd_y = is_odd("gx"), is_odd("gy")
    nx, ny, nz = v_ref.shape[1:]
    rows = nx * ny
    slots = row_ref.shape[1]
    blocks = slots // LANES
    back = x_ref[...] + y_ref[...] + z_ref[...]
    size = chunk_of(slots)
    placed = None
    for start in range(0, slots, size):
        lanes = slice(start, start + size)
        steps = range(start // LANES, (start + size) // LANES)
        lines = [
            jnp.concatenate(
                [back[comp * blocks + at : comp * blocks + at + 1] for at in steps], axis=1
            )
            for comp in range(3)
        ]
        part = mm(scaled(row_ref[:, lanes], lines), deep_ref[:, lanes], trans=True)
        placed = part if placed is None else placed + part
    placed = placed[: 3 * rows] + placed[3 * rows :]
    for a in range(3):
        own = sum(inv_ref[3 * a + b] * v_ref[b] for b in range(3))
        out_ref[a] = own + placed[a * rows : (a + 1) * rows].reshape(nx, ny, nz)
        low = jnp.where(first_x, 0.0, out_ref[a, 0])
        high = jnp.where(last_x, 0.0, out_ref[a, nx - 1])
        x_even_ref[a] = jnp.where(odd_x, low, high)
        x_next_ref[a] = jnp.where(odd_x, high, low)
        low = jnp.where(first_y, 0.0, out_ref[a, :, 0, :])
        high = jnp.where(last_y, 0.0, out_ref[a, :, ny - 1, :])
        y_even_ref[a] = jnp.where(odd_y, low, high)
        y_next_ref[a] = jnp.where(odd_y, high, low)


def inner_kernel(z_ref, d_ref, off_ref, w_ref):
    nx, ny, nz = z_ref.shape[1:]
    row = iota((ny, nz), 0)
    lane = iota((ny, nz), 1)
    for x in range(nx):
        beside = []
        for b in range(3):
            own = z_ref[b, x]
            beside.append(
                [
                    z_ref[b, x - 1] if x else None,
                    z_ref[b, x + 1] if x < nx - 1 else None,
                    jnp.where(row == 0, 0.0, pltpu.roll(own, 1, 0)),
                    jnp.where(row == ny - 1, 0.0, pltpu.roll(own, ny - 1, 0)),
                    jnp.where(lane == 0, 0.0, pltpu.roll(own, 1, 1)),
                    jnp.where(lane == nz - 1, 0.0, pltpu.roll(own, nz - 1, 1)),
                ]
            )
        for a in range(3):
            total = sum(d_ref[3 * a + b, x] * z_ref[b, x] for b in range(3))
            for face in range(6):
                for b in range(3):
                    if beside[b][face] is not None:
                        total = total + off_ref[face, 3 * a + b, x] * beside[b][face]
            w_ref[a, x] = total


def add_faces(part_ref, faces, off_ref, w_ref):
    nx, ny, nz = part_ref.shape[1:]
    odd_x, odd_y = is_odd("gx"), is_odd("gy")
    x_next, x_even, y_next, y_even = [face[...] for face in faces]
    xl, xh = jnp.where(odd_x, x_even, x_next), jnp.where(odd_x, x_next, x_even)
    yl, yh = jnp.where(odd_y, y_even, y_next), jnp.where(odd_y, y_next, y_even)
    for a in range(3):
        w_ref[a] = part_ref[a]
        for x, face, beside in ((0, 0, xl), (nx - 1, 1, xh)):
            w_ref[a, x] += sum(off_ref[face, 3 * a + b, x] * beside[b] for b in range(3))
        for y, face, beside in ((0, 2, yl), (ny - 1, 3, yh)):
            w_ref[a, :, y, :] += sum(
                off_ref[face, 3 * a + b, :, y, :] * beside[b] for b in range(3)
            )


def next_kernel(
    cells_ref, deep_ref, part_ref, f0_ref, f1_ref, f2_ref, f3_ref, d_ref, off_ref, v_ref,
    w_ref, t_ref, out_ref,
):
    add_faces(part_ref, (f0_ref, f1_ref, f2_ref, f3_ref), off_ref, w_ref)
    t_ref[...] = w_ref[...] - v_ref[...]
    pick(times_diag(d_ref, [t_ref[b] for b in range(3)]), cells_ref, deep_ref, out_ref)


def gram_kernel(
    part_ref, f0_ref, f1_ref, f2_ref, f3_ref, off_ref, v_ref, w1_ref,
    w_ref, sums_ref,
):
    add_faces(part_ref, (f0_ref, f1_ref, f2_ref, f3_ref), off_ref, w_ref)
    one, two, rhs = w1_ref[...], w_ref[...], v_ref[...]
    top_one = jnp.maximum(jnp.max(jnp.abs(one)), 1e-30)
    top_two = jnp.maximum(jnp.max(jnp.abs(two)), 1e-30)
    one = one * (1.0 / jnp.full((1, 1), top_one))
    two = two * (1.0 / jnp.full((1, 1), top_two))
    sums = [
        jnp.sum(one * one), jnp.sum(one * two), jnp.sum(two * two),
        jnp.sum(one * rhs), jnp.sum(two * rhs), top_one, top_two,
    ]
    line = iota(sums_ref.shape, 0)
    total = jnp.zeros(sums_ref.shape, F32)
    for place, value in enumerate(sums):
        total = jnp.where(line == place, value, total)
    sums_ref[...] = total


def final_kernel(
    sums_ref, v_ref, z1_ref, z2_ref, w1_ref, w2_ref, sol_ref, res_ref
):
    g11, g12, g22, r1, r2, top_one, top_two = [sums_ref[i : i + 1, :] for i in range(7)]
    det = g11 * g22 - g12 * g12
    y1 = ((g22 * r1 - g12 * r2) / det / top_one)[:, :1]
    y2 = ((g11 * r2 - g12 * r1) / det / top_two)[:, :1]
    sol_ref[...] = y1 * z1_ref[...] + y2 * z2_ref[...]
    res_ref[...] = v_ref[...] - y1 * w1_ref[...] - y2 * w2_ref[...]


def swap(axis, to_even, to_next):
    size = {name: lax.axis_size(name) for name in ("gx", "gy")}
    count, breadth = size[axis], size["gy" if axis == "gx" else "gx"]

    def device(along, across):
        return along * size["gy"] + across if axis == "gx" else across * size["gy"] + along

    out = []
    order = [(1, to_next), (0, to_even)]
    same = to_even is to_next
    for first, value in order:
        pairs = []
        for across in range(breadth):
            for i in range(count):
                other = i + 1 if i % 2 == first else i - 1
                if 0 <= other < count:
                    pairs.append((device(i, across), device(other, across)))
                elif across ^ 1 < breadth:
                    pairs.append((device(i, across), device(i, across ^ 1)))
                else:
                    pairs.append((device(i, across), device(i, across)))
        out.append(lax.ppermute(value, ("gx", "gy"), pairs))
    return out[::-1]


def merge_kernel(*refs):
    *parts, out_ref = refs
    parts = [part[...] for part in parts]
    tops = [[part[place : place + 1] for part in parts] for place in (5, 6)]
    top_one, top_two = [functools.reduce(jnp.maximum, top) for top in tops]
    line = iota(out_ref.shape, 0)
    total = None
    for part in parts:
        one, two = part[5:6] / top_one, part[6:7] / top_two
        scale = jnp.where(
            line == 0, one * one, jnp.where(
                line == 1, one * two, jnp.where(
                    line == 2, two * two, jnp.where(line == 3, one, two)
                )
            ),
        )
        part = part * scale
        total = part if total is None else total + part
    total = jnp.where(line == 5, top_one, jnp.where(line == 6, top_two, total))
    out_ref[...] = total


def merge_all(value):
    axes = ("gx", "gy")
    count = lax.axis_size(axes)
    if count & (count - 1):
        every = lax.all_gather(value, axes)
        return call(merge_kernel, [value.shape])(*[every[i] for i in range(count)])[0]
    step, radix = 1, 2 if count.bit_length() % 2 == 0 else 4
    while step < count:
        others = [
            lax.ppermute(value, axes, [(i, i ^ (k * step)) for i in range(count)])
            for k in range(1, radix)
        ]
        (value,) = call(merge_kernel, [value.shape])(value, *others)
        step, radix = step * radix, 4
    return value


def body(
    right_side,
    diag_blocks,
    off_blocks,
    cell_inverse,
    send_cells,
    recv_index,
    seg_count,
    span_inverse,
    span_couple,
):
    _, nx, ny, nz = right_side.shape
    slots = send_cells.shape[1]
    wells, longest = recv_index.shape
    chunks, width, span_all = span_inverse.shape
    span = width // 3
    blocks = slots // LANES
    tile = round_up(3 * blocks, 16)
    rows = round_up(9 * blocks, 32)
    tall = round_up(chunks, 16)
    field = right_side.shape
    (picked,) = call(
        first_kernel,
        [(tile, LANES)],
        [
            (send_cells.shape, jnp.int32),
            (field, F32),
            (diag_blocks.shape, F32),
            ((nz, slots), BF16),
            pltpu.SemaphoreType.DMA((11,)),
        ],
        flops=10**9,
        space=pltpu.HBM,
        mib=60,
    )(send_cells, right_side, diag_blocks)
    live = jnp.arange(longest)[None, :] < seg_count[:, None]
    index = jnp.where(live, recv_index, -1)
    index = index.reshape(wells, chunks, span).transpose(1, 0, 2).reshape(1, wells * longest)
    couple = jnp.pad(span_couple.transpose(1, 0, 2), ((0, 0), (0, tall - chunks), (0, 0)))
    h, e, apart, low, high, deep, row = call(
        prep_kernel,
        [(3, tall, span_all), (9, tall, wells), (3, chunks, span, span_all)]
        + [
            jax.ShapeDtypeStruct((height, slots), BF16)
            for height in (2 * LANES, rows // 2, nz, nx * ny)
        ],
        [((chunks, width, LANES), F32)],
    )(index, send_cells, span_inverse, couple)

    def precondition(vector, picked):
        beside = swap("gx", picked, picked)
        if vector is right_side:
            (picked,) = call(hold_kernel, [picked.shape])(picked)
        column = jnp.concatenate([picked, *beside], axis=0)
        even, following = swap("gy", column, column)
        keep, following, even = call(
            solve_kernel,
            [(3 * tile, LANES)] * 3,
            [
                ((3, rows, LANES), F32),
                ((3, tall, wells * span), F32),
                ((tall, span_all), F32),
                ((3, tall, wells), F32),
                ((3, tall, wells), F32),
                ((tall, span_all), F32),
            ],
            flops=4 * 10**9,
        )(index, column, even, following, apart, h, e, low, high)
        even, following = swap("gy", even, following)
        keep, following, even = call(add_kernel, [(tile, LANES)] * 3)(
            keep, following, even
        )
        even, following = swap("gx", even, following)
        z, *faces = call(
            place_kernel,
            [(3, nx, ny, nz)] + [(3, ny, nz)] * 2 + [(3, nx, nz)] * 2,
            flops=10**9,
        )(row, deep, vector, cell_inverse, keep, following, even)
        faces = swap("gx", *faces[1::-1])[::-1] + swap("gy", *faces[:1:-1])[::-1]
        (part,) = call(inner_kernel, [field], flops=10**7)(z, diag_blocks, off_blocks)
        return z, part, faces

    z1, part, faces = precondition(right_side, picked)
    w1, turned, picked = call(
        next_kernel, [field, field, (tile, LANES)], flops=10**9
    )(send_cells, deep, part, *faces, diag_blocks, off_blocks, right_side)
    z2, part, faces = precondition(turned, picked)
    w2, sums = call(gram_kernel, [field, (8, LANES)])(
        part, *faces, off_blocks, right_side, w1
    )
    sums = merge_all(sums)
    return tuple(
        call(final_kernel, [field, field])(sums, right_side, z1, z2, w1, w2)
    )


def solution(mesh):
    return jax.shard_map(
        body,
        mesh=mesh,
        in_specs=(
            P(None, "gx", "gy", None),
            P(None, "gx", "gy", None),
            P(None, None, "gx", "gy", None),
            P(None, "gx", "gy", None),
            P(("gx", "gy"), None),
            P(("gx", "gy"), None),
            P(("gx", "gy")),
            P(None, None, ("gx", "gy")),
            P(None, None, ("gx", "gy")),
        ),
        out_specs=(P(None, "gx", "gy", None), P(None, "gx", "gy", None)),
        check_vma=False,
    )
```

```python
import functools

import jax
import jax.numpy as jnp
from jax import lax
from jax.experimental import pallas as pl
from jax.experimental.pallas import tpu as pltpu
from jax.sharding import PartitionSpec as P

LANES = 128
F32 = jnp.float32
BF16 = jnp.bfloat16


def round_up(value, unit):
    return -(-value // unit) * unit


def iota(shape, dim):
    return lax.broadcasted_iota(jnp.int32, shape, dim)


def split(value, pieces):
    out = []
    for _ in range(pieces - 1):
        piece = value.astype(BF16)
        out.append(piece)
        value = value - piece.astype(F32)
    out.append(value.astype(BF16))
    return out


def mm(left, right, trans=False):
    dims = (((1,), (1 if trans else 0,)), ((), ()))
    return lax.dot_general(left, right, dims, preferred_element_type=F32)


def mm_exact(value, choice):
    total = None
    for piece in split(value, 3):
        part = mm(piece, choice)
        total = part if total is None else total + part
    return total


def ones_where(mask):
    return jnp.where(mask, 1.0, 0.0).astype(BF16)


def call(kernel, outs, scratch=(), flops=0, space=pltpu.VMEM, mib=40):
    def run(*args):
        shapes = [
            o if hasattr(o, "dtype") else jax.ShapeDtypeStruct(o, F32) for o in outs
        ]
        moved = sum(a.size * a.dtype.itemsize for a in (*args, *shapes))
        return pl.pallas_call(
            kernel,
            out_shape=shapes,
            in_specs=[pl.BlockSpec(memory_space=space)] * len(args),
            out_specs=[pl.BlockSpec(memory_space=pltpu.VMEM)] * len(outs),
            scratch_shapes=[s if hasattr(s, "dtype") else pltpu.VMEM(*s) for s in scratch],
            cost_estimate=pl.CostEstimate(
                flops=flops, bytes_accessed=moved, transcendentals=0
            ),
            compiler_params=pltpu.CompilerParams(vmem_limit_bytes=mib * 2**20),
        )(*args)

    return run


def chunk_of(slots):
    for groups in (5, 4, 3, 2, 1):
        if slots % (groups * LANES) == 0:
            return groups * LANES


def is_odd(axis):
    return lax.rem(lax.axis_index(axis), 2) == 1


def row_and_depth(cells, nz):
    if nz & (nz - 1) == 0:
        return lax.shift_right_logical(cells, nz.bit_length() - 1), cells & (nz - 1)
    return lax.div(cells, jnp.int32(nz)), lax.rem(cells, jnp.int32(nz))


def pick(field, cells_ref, deep_ref, out_ref):
    _, rows, depth = field.shape
    slots = cells_ref.shape[1]
    blocks = slots // LANES
    chunk = chunk_of(slots)
    left = jnp.concatenate(split(field.reshape(3 * rows, depth), 2), axis=1)
    for start in range(0, slots, chunk):
        row, _ = row_and_depth(cells_ref[:, start : start + chunk], depth)
        right = deep_ref[:, start : start + chunk]
        found = mm(left, jnp.concatenate([right, right], axis=0))
        here = iota((rows, chunk), 0) == row
        for comp in range(3):
            part = jnp.where(here, found[comp * rows : (comp + 1) * rows], 0.0)
            line = jnp.sum(part, axis=0, keepdims=True)
            for piece in range(chunk // LANES):
                at = comp * blocks + start // LANES + piece
                out_ref[at : at + 1, :] = line[:, piece * LANES : (piece + 1) * LANES]
    pad = out_ref.shape[0] - 3 * blocks
    if pad:
        out_ref[3 * blocks :, :] = jnp.zeros((pad, LANES), F32)


def one_hot(out_ref, values):
    chunk = chunk_of(out_ref.shape[1])
    for start in range(0, out_ref.shape[1], chunk):
        lanes = slice(start, start + chunk)
        out_ref[:, lanes] = ones_where(
            iota((out_ref.shape[0], chunk), 0) == values(lanes)
        )


def scaled(hot, lines):
    rows = hot.shape[0]
    out = []
    for place in range(2):
        for line in lines:
            piece = split(line, 2)[place].astype(F32)
            few = jnp.broadcast_to(piece, (16, piece.shape[1])).astype(BF16)
            out += [few * hot[at : at + 16] for at in range(0, rows, 16)]
    return jnp.concatenate(out, axis=0)


def times_diag(d_ref, field):
    nx, ny, nz = d_ref.shape[1:]
    return jnp.stack(
        [
            sum(d_ref[3 * a + b] * field[b] for b in range(3)).reshape(nx * ny, nz)
            for a in range(3)
        ]
    )


def first_kernel(
    cells_hbm, v_hbm, d_hbm, out_ref, cells_ref, v_ref, d_ref, deep_ref, sem
):
    pairs = [(cells_hbm, cells_ref), (v_hbm, v_ref)]
    pairs += [(d_hbm.at[entry], d_ref.at[entry]) for entry in range(9)]
    copies = [
        pltpu.make_async_copy(src, dst, sem.at[place])
        for place, (src, dst) in enumerate(pairs)
    ]
    for copy in copies:
        copy.start()
    copies[0].wait()
    depth = v_ref.shape[3]
    one_hot(deep_ref, lambda lanes: row_and_depth(cells_ref[:, lanes], depth)[1])
    for copy in copies[1:]:
        copy.wait()
    pick(times_diag(d_ref, [v_ref[b] for b in range(3)]), cells_ref, deep_ref, out_ref)


def hold_kernel(value_ref, out_ref):
    out_ref[...] = value_ref[...]


def spread_matrix(wells, width):
    shape = (wells, wells * width)
    gap = iota(shape, 1) - width * iota(shape, 0)
    return ones_where((gap >= 0) & (gap < width))


def last_matrix(wells, width, comp):
    shape = (wells * width, wells)
    return ones_where(iota(shape, 0) == width * iota(shape, 1) + (width - 3 + comp))


def prep_kernel(
    idx_ref, cells_ref, g_ref, couple_ref,
    h_ref, e_ref, apart_ref, low_ref, high_ref, deep_ref, row_ref,
    part_ref,
):
    wide = low_ref.shape[0]
    depth = deep_ref.shape[0]
    one_hot(low_ref, lambda lanes: idx_ref[:, lanes] & (wide - 1))
    one_hot(
        high_ref,
        lambda lanes: lax.shift_right_arithmetic(idx_ref[:, lanes], wide.bit_length() - 1),
    )
    one_hot(row_ref, lambda lanes: row_and_depth(cells_ref[:, lanes], depth)[0])
    one_hot(deep_ref, lambda lanes: row_and_depth(cells_ref[:, lanes], depth)[1])
    chunks, width, span_all = g_ref.shape
    wells = couple_ref.shape[2]
    span = width // 3
    for lane in range(0, span_all, LANES):
        part_ref[...] = g_ref[:, :, lane : lane + LANES]
        for comp in range(3):
            apart_ref[comp, :, :, lane : lane + LANES] = part_ref[
                :, pl.ds(comp, span, stride=3), :
            ]
    spread = spread_matrix(wells, width)
    heads = [g_ref[:, d, :] for d in range(3)]
    for b in range(3):
        total = sum(
            heads[d] * mm_exact(couple_ref[3 * d + b], spread)[:chunks] for d in range(3)
        )
        h_ref[b] = jnp.zeros(h_ref.shape[1:], F32)
        h_ref[b, :chunks, :] = total
        full = h_ref[b]
        for a in range(3):
            e_ref[3 * a + b] = mm_exact(full, last_matrix(wells, width, a))


def pool_column(pool_ref, column, first, blocks):
    odd_x = is_odd("gx")
    tile = column.shape[0] // 3
    own, even, following = column[:tile], column[tile : 2 * tile], column[2 * tile :]
    parts = (jnp.where(odd_x, even, following), own, jnp.where(odd_x, following, even))
    for a, part in enumerate(parts):
        for comp in range(3):
            at = (first + a) * blocks
            pool_ref[comp, at : at + blocks, :] = part[comp * blocks : (comp + 1) * blocks]


def clear_tail(pool_ref, used):
    pool_ref[:, used:, :] = jnp.zeros((3, pool_ref.shape[1] - used, LANES), F32)


def gather_lines(pool_ref, idx_ref, low_ref, first_row):
    half = pool_ref.shape[1] // 2
    wide = 2 * LANES
    pooled = jnp.concatenate(
        [
            jnp.concatenate(
                [pool_ref[comp, pl.ds(odd, half, stride=2), :] for odd in range(2)], axis=1
            )
            for comp in range(3)
        ],
        axis=0,
    )
    left = jnp.concatenate(split(pooled, 2), axis=1)
    slots = idx_ref.shape[1]
    size = chunk_of(slots)
    for start in range(0, slots, size):
        place = idx_ref[:, start : start + size]
        right = low_ref[:, start : start + size]
        found = mm(left, jnp.concatenate([right, right], axis=0))
        block = lax.shift_right_arithmetic(place, wide.bit_length() - 1) - first_row
        here = iota((half, size), 0) == block
        for comp in range(3):
            part = jnp.where(here, found[comp * half : (comp + 1) * half], 0.0)
            yield start, comp, jnp.sum(part, axis=0, keepdims=True)


def scatter_lines(pool_ref, y_ref, low_ref, high_ref, first_row, group):
    half = pool_ref.shape[1] // 2
    slots = low_ref.shape[1]
    size = chunk_of(slots)
    spread_out = None
    for start in range(0, slots, size):
        lanes = slice(start, start + size)
        steps = range(start // group, (start + size) // group)
        lines = [
            jnp.concatenate(
                [y_ref[c : c + 1, comp * group : (comp + 1) * group] for c in steps], axis=1
            )
            for comp in range(3)
        ]
        hot = high_ref[first_row : first_row + half, lanes]
        part = mm(scaled(hot, lines), low_ref[:, lanes], trans=True)
        spread_out = part if spread_out is None else spread_out + part
    spread_out = spread_out[: 3 * half] + spread_out[3 * half :]
    for comp in range(3):
        block = spread_out[comp * half : (comp + 1) * half]
        for odd in range(2):
            pool_ref[comp, pl.ds(odd, half, stride=2), :] = block[
                :, odd * LANES : (odd + 1) * LANES
            ]


def own_gather_kernel(idx_ref, own_ref, low_ref, r_ref, pool_ref):
    group = r_ref.shape[2]
    blocks = idx_ref.shape[1] // LANES
    clear_tail(pool_ref, 3 * blocks)
    pool_column(pool_ref, own_ref[...], 0, blocks)
    r_ref[...] = jnp.zeros(r_ref.shape, F32)
    first_row = round_up(3 * blocks, 16)
    for start, comp, line in gather_lines(pool_ref, idx_ref, low_ref, first_row):
        for piece in range(line.shape[1] // group):
            at = start // group + piece
            r_ref[comp, at : at + 1, :] = line[:, piece * group : (piece + 1) * group]


def own_scatter_kernel(y_ref, low_ref, high_ref, keep_ref, pool_ref):
    blocks = low_ref.shape[1] // LANES
    tile = keep_ref.shape[0] // 3
    first_row = round_up(3 * blocks, 16)
    scatter_lines(pool_ref, y_ref, low_ref, high_ref, first_row, y_ref.shape[1] // 3)
    keep_ref[...] = jnp.zeros(keep_ref.shape, F32)
    for a in range(3):
        for comp in range(3):
            at = slice(a * tile + comp * blocks, a * tile + (comp + 1) * blocks)
            keep_ref[at, :] = pool_ref[comp, a * blocks : (a + 1) * blocks, :]


def solve_kernel(
    idx_ref, even_ref, next_ref, part_ref, g_ref, h_ref, e_ref, low_ref, high_ref,
    y_ref, to_next_ref, to_even_ref,
    pool_ref, r_ref, q_ref, tail_ref, p_ref,
):
    _, chunks, span, span_all = g_ref.shape
    width = 3 * span
    wells = span_all // width
    blocks = idx_ref.shape[1] // LANES
    tile = even_ref.shape[0] // 3
    group = wells * span
    odd_y = is_odd("gy")
    clear_tail(pool_ref, 6 * blocks)
    even, following = even_ref[...], next_ref[...]
    pool_column(pool_ref, jnp.where(odd_y, even, following), 0, blocks)
    pool_column(pool_ref, jnp.where(odd_y, following, even), 3, blocks)
    r_ref[...] = jnp.zeros(r_ref.shape, F32)
    for start, comp, line in gather_lines(pool_ref, idx_ref, low_ref, 0):
        for piece in range(line.shape[1] // group):
            at = start // group + piece
            r_ref[comp, at : at + 1, :] = (
                line[:, piece * group : (piece + 1) * group] + part_ref[comp, at : at + 1, :]
            )
    two = (2 * group, span_all)
    well_of = lax.shift_right_logical(iota(two, 0) & (group - 1), (span - 1).bit_length())
    gap = iota(two, 1) - width * well_of
    spread = ones_where((gap >= 0) & (gap < width))
    own = (iota((span, group), 1) & (span - 1)) == iota((span, group), 0)
    total = None
    for comp in range(3):
        values = r_ref[comp][:chunks]
        wide = jnp.where(own[None], values[:, None, :], 0.0).reshape(chunks * span, group)
        lifted = mm(jnp.concatenate(split(wide, 2), axis=1), spread)
        lifted = lifted.reshape(chunks, span, span_all)
        part = g_ref[comp] * lifted
        total = part if total is None else total + part
    q_ref[...] = jnp.zeros(q_ref.shape, F32)
    q_ref[:chunks, :] = jnp.sum(total, axis=1)
    plain = q_ref[...]
    for a in range(3):
        tail_ref[a] = mm_exact(plain, last_matrix(wells, width, a))
    p_ref[...] = jnp.zeros(p_ref.shape, F32)
    state = [jnp.zeros((1, wells), F32)] * 3
    for c in range(chunks - 1):
        state = [
            tail_ref[a, c : c + 1, :]
            - (
                e_ref[3 * a, c : c + 1, :] * state[0]
                + e_ref[3 * a + 1, c : c + 1, :] * state[1]
                + e_ref[3 * a + 2, c : c + 1, :] * state[2]
            )
            for a in range(3)
        ]
        for a in range(3):
            p_ref[a, c + 1 : c + 2, :] = state[a]
    wide_well = spread_matrix(wells, width)
    for b in range(3):
        plain = plain - h_ref[b] * mm_exact(p_ref[b], wide_well)
    square = (span_all, span_all)
    lane = iota((1, span_all), 1)
    comp_of = lax.div(lane, jnp.int32(group))
    rest = lax.rem(lane, jnp.int32(group))
    source = width * lax.div(rest, jnp.int32(span)) + 3 * lax.rem(rest, jnp.int32(span)) + comp_of
    y_ref[...] = mm_exact(plain, ones_where(iota(square, 0) == source))
    scatter_lines(pool_ref, y_ref, low_ref, high_ref, 0, group)
    for dst in (to_even_ref, to_next_ref):
        dst[...] = jnp.zeros(dst.shape, F32)
    for a in range(3):
        for comp in range(3):
            before, after = [
                pool_ref[comp, (b + a) * blocks : (b + a + 1) * blocks, :] for b in (0, 3)
            ]
            at = slice(a * tile + comp * blocks, a * tile + (comp + 1) * blocks)
            to_even_ref[at, :] = jnp.where(odd_y, before, after)
            to_next_ref[at, :] = jnp.where(odd_y, after, before)


def add_kernel(x_ref, y_ref, z_ref, keep_ref, to_next_ref, to_even_ref):
    tile = keep_ref.shape[0]
    odd_x = is_odd("gx")
    low, mid, high = [
        x_ref[part, :] + y_ref[part, :] + z_ref[part, :]
        for part in [slice(place * tile, (place + 1) * tile) for place in range(3)]
    ]
    keep_ref[...] = mid
    to_even_ref[...] = jnp.where(odd_x, low, high)
    to_next_ref[...] = jnp.where(odd_x, high, low)


def place_kernel(
    row_ref, deep_ref, v_ref, inv_ref, x_ref, y_ref, z_ref,
    out_ref, x_next_ref, x_even_ref, y_next_ref, y_even_ref,
):
    (first_x, last_x), (first_y, last_y) = [
        (lax.axis_index(axis) == 0, lax.axis_index(axis) == lax.axis_size(axis) - 1)
        for axis in ("gx", "gy")
    ]
    odd_x, odd_y = is_odd("gx"), is_odd("gy")
    nx, ny, nz = v_ref.shape[1:]
    rows = nx * ny
    slots = row_ref.shape[1]
    blocks = slots // LANES
    back = x_ref[...] + y_ref[...] + z_ref[...]
    size = chunk_of(slots)
    placed = None
    for start in range(0, slots, size):
        lanes = slice(start, start + size)
        steps = range(start // LANES, (start + size) // LANES)
        lines = [
            jnp.concatenate(
                [back[comp * blocks + at : comp * blocks + at + 1] for at in steps], axis=1
            )
            for comp in range(3)
        ]
        part = mm(scaled(row_ref[:, lanes], lines), deep_ref[:, lanes], trans=True)
        placed = part if placed is None else placed + part
    placed = placed[: 3 * rows] + placed[3 * rows :]
    for a in range(3):
        own = sum(inv_ref[3 * a + b] * v_ref[b] for b in range(3))
        out_ref[a] = own + placed[a * rows : (a + 1) * rows].reshape(nx, ny, nz)
        low = jnp.where(first_x, 0.0, out_ref[a, 0])
        high = jnp.where(last_x, 0.0, out_ref[a, nx - 1])
        x_even_ref[a] = jnp.where(odd_x, low, high)
        x_next_ref[a] = jnp.where(odd_x, high, low)
        low = jnp.where(first_y, 0.0, out_ref[a, :, 0, :])
        high = jnp.where(last_y, 0.0, out_ref[a, :, ny - 1, :])
        y_even_ref[a] = jnp.where(odd_y, low, high)
        y_next_ref[a] = jnp.where(odd_y, high, low)


def inner_kernel(z_ref, d_ref, off_ref, w_ref):
    nx, ny, nz = z_ref.shape[1:]
    row = iota((ny, nz), 0)
    lane = iota((ny, nz), 1)
    for x in range(nx):
        beside = []
        for b in range(3):
            own = z_ref[b, x]
            beside.append(
                [
                    z_ref[b, x - 1] if x else None,
                    z_ref[b, x + 1] if x < nx - 1 else None,
                    jnp.where(row == 0, 0.0, pltpu.roll(own, 1, 0)),
                    jnp.where(row == ny - 1, 0.0, pltpu.roll(own, ny - 1, 0)),
                    jnp.where(lane == 0, 0.0, pltpu.roll(own, 1, 1)),
                    jnp.where(lane == nz - 1, 0.0, pltpu.roll(own, nz - 1, 1)),
                ]
            )
        for a in range(3):
            total = sum(d_ref[3 * a + b, x] * z_ref[b, x] for b in range(3))
            for face in range(6):
                for b in range(3):
                    if beside[b][face] is not None:
                        total = total + off_ref[face, 3 * a + b, x] * beside[b][face]
            w_ref[a, x] = total


def add_faces(part_ref, faces, off_ref, w_ref):
    nx, ny, nz = part_ref.shape[1:]
    odd_x, odd_y = is_odd("gx"), is_odd("gy")
    x_next, x_even, y_next, y_even = [face[...] for face in faces]
    xl, xh = jnp.where(odd_x, x_even, x_next), jnp.where(odd_x, x_next, x_even)
    yl, yh = jnp.where(odd_y, y_even, y_next), jnp.where(odd_y, y_next, y_even)
    for a in range(3):
        w_ref[a] = part_ref[a]
        for x, face, beside in ((0, 0, xl), (nx - 1, 1, xh)):
            w_ref[a, x] += sum(off_ref[face, 3 * a + b, x] * beside[b] for b in range(3))
        for y, face, beside in ((0, 2, yl), (ny - 1, 3, yh)):
            w_ref[a, :, y, :] += sum(
                off_ref[face, 3 * a + b, :, y, :] * beside[b] for b in range(3)
            )


def next_kernel(
    cells_ref, deep_ref, part_ref, f0_ref, f1_ref, f2_ref, f3_ref, d_ref, off_ref, v_ref,
    w_ref, t_ref, out_ref,
):
    add_faces(part_ref, (f0_ref, f1_ref, f2_ref, f3_ref), off_ref, w_ref)
    t_ref[...] = w_ref[...] - v_ref[...]
    pick(times_diag(d_ref, [t_ref[b] for b in range(3)]), cells_ref, deep_ref, out_ref)


def gram_kernel(
    part_ref, f0_ref, f1_ref, f2_ref, f3_ref, off_ref, v_ref, w1_ref,
    w_ref, sums_ref,
):
    add_faces(part_ref, (f0_ref, f1_ref, f2_ref, f3_ref), off_ref, w_ref)
    one, two, rhs = w1_ref[...], w_ref[...], v_ref[...]
    top_one = jnp.maximum(jnp.max(jnp.abs(one)), 1e-30)
    top_two = jnp.maximum(jnp.max(jnp.abs(two)), 1e-30)
    one = one * (1.0 / jnp.full((1, 1), top_one))
    two = two * (1.0 / jnp.full((1, 1), top_two))
    sums = [
        jnp.sum(one * one), jnp.sum(one * two), jnp.sum(two * two),
        jnp.sum(one * rhs), jnp.sum(two * rhs), top_one, top_two,
    ]
    line = iota(sums_ref.shape, 0)
    total = jnp.zeros(sums_ref.shape, F32)
    for place, value in enumerate(sums):
        total = jnp.where(line == place, value, total)
    sums_ref[...] = total


def final_kernel(
    sums_ref, v_ref, z1_ref, z2_ref, w1_ref, w2_ref, sol_ref, res_ref
):
    g11, g12, g22, r1, r2, top_one, top_two = [sums_ref[i : i + 1, :] for i in range(7)]
    det = g11 * g22 - g12 * g12
    y1 = ((g22 * r1 - g12 * r2) / det / top_one)[:, :1]
    y2 = ((g11 * r2 - g12 * r1) / det / top_two)[:, :1]
    sol_ref[...] = y1 * z1_ref[...] + y2 * z2_ref[...]
    res_ref[...] = v_ref[...] - y1 * w1_ref[...] - y2 * w2_ref[...]


def swap(axis, to_even, to_next):
    size = {name: lax.axis_size(name) for name in ("gx", "gy")}
    count, breadth = size[axis], size["gy" if axis == "gx" else "gx"]

    def device(along, across):
        return along * size["gy"] + across if axis == "gx" else across * size["gy"] + along

    out = []
    order = [(1, to_next), (0, to_even)]
    same = to_even is to_next
    for first, value in order:
        pairs = []
        for across in range(breadth):
            for i in range(count):
                other = i + 1 if i % 2 == first else i - 1
                if 0 <= other < count:
                    pairs.append((device(i, across), device(other, across)))
                elif across ^ 1 < breadth:
                    pairs.append((device(i, across), device(i, across ^ 1)))
                else:
                    pairs.append((device(i, across), device(i, across)))
        out.append(lax.ppermute(value, ("gx", "gy"), pairs))
    return out[::-1]


def merge_kernel(*refs):
    *parts, out_ref = refs
    parts = [part[...] for part in parts]
    tops = [[part[place : place + 1] for part in parts] for place in (5, 6)]
    top_one, top_two = [functools.reduce(jnp.maximum, top) for top in tops]
    line = iota(out_ref.shape, 0)
    total = None
    for part in parts:
        one, two = part[5:6] / top_one, part[6:7] / top_two
        scale = jnp.where(
            line == 0, one * one, jnp.where(
                line == 1, one * two, jnp.where(
                    line == 2, two * two, jnp.where(line == 3, one, two)
                )
            ),
        )
        part = part * scale
        total = part if total is None else total + part
    total = jnp.where(line == 5, top_one, jnp.where(line == 6, top_two, total))
    out_ref[...] = total


def merge_all(value):
    axes = ("gx", "gy")
    count = lax.axis_size(axes)
    if count & (count - 1):
        every = lax.all_gather(value, axes)
        return call(merge_kernel, [value.shape])(*[every[i] for i in range(count)])[0]
    step, radix = 1, 2 if count.bit_length() % 2 == 0 else 4
    while step < count:
        others = [
            lax.ppermute(value, axes, [(i, i ^ (k * step)) for i in range(count)])
            for k in range(1, radix)
        ]
        (value,) = call(merge_kernel, [value.shape])(value, *others)
        step, radix = step * radix, 4
    return value


def body(
    right_side,
    diag_blocks,
    off_blocks,
    cell_inverse,
    send_cells,
    recv_index,
    seg_count,
    span_inverse,
    span_couple,
):
    _, nx, ny, nz = right_side.shape
    slots = send_cells.shape[1]
    wells, longest = recv_index.shape
    chunks, width, span_all = span_inverse.shape
    span = width // 3
    blocks = slots // LANES
    tile = round_up(3 * blocks, 16)
    beside_rows = round_up(6 * blocks, 32)
    own_rows = round_up(3 * blocks, 32)
    tall = round_up(chunks, 16)
    field = right_side.shape
    (picked,) = call(
        first_kernel,
        [(tile, LANES)],
        [
            (send_cells.shape, jnp.int32),
            (field, F32),
            (diag_blocks.shape, F32),
            ((nz, slots), BF16),
            pltpu.SemaphoreType.DMA((11,)),
        ],
        flops=10**9,
        space=pltpu.HBM,
        mib=60,
    )(send_cells, right_side, diag_blocks)
    live = jnp.arange(longest)[None, :] < seg_count[:, None]
    along, column = recv_index // slots // 3, recv_index // slots % 3
    index = recv_index % slots + slots * along
    index = index + jnp.where(column == 1, beside_rows * LANES, slots * 3 * (column // 2))
    index = jnp.where(live, index, -1)
    index = index.reshape(wells, chunks, span).transpose(1, 0, 2).reshape(1, wells * longest)
    couple = jnp.pad(span_couple.transpose(1, 0, 2), ((0, 0), (0, tall - chunks), (0, 0)))
    h, e, apart, low, high, deep, row = call(
        prep_kernel,
        [(3, tall, span_all), (9, tall, wells), (3, chunks, span, span_all)]
        + [
            jax.ShapeDtypeStruct((height, slots), BF16)
            for height in (2 * LANES, (beside_rows + own_rows) // 2, nz, nx * ny)
        ],
        [((chunks, width, LANES), F32)],
    )(index, send_cells, span_inverse, couple)

    def precondition(vector, picked):
        beside = swap("gx", picked, picked)
        if vector is right_side:
            (picked,) = call(hold_kernel, [picked.shape])(picked)
        column = jnp.concatenate([picked, *beside], axis=0)
        even, following = swap("gy", column, column)
        (part,) = call(
            own_gather_kernel,
            [(3, tall, wells * span)],
            [((3, own_rows, LANES), F32)],
            flops=10**9,
        )(index, column, low)
        y, following, even = call(
            solve_kernel,
            [(tall, span_all)] + [(3 * tile, LANES)] * 2,
            [
                ((3, beside_rows, LANES), F32),
                ((3, tall, wells * span), F32),
                ((tall, span_all), F32),
                ((3, tall, wells), F32),
                ((3, tall, wells), F32),
            ],
            flops=3 * 10**9,
        )(index, even, following, part, apart, h, e, low, high)
        even, following = swap("gy", even, following)
        (keep,) = call(
            own_scatter_kernel,
            [(3 * tile, LANES)],
            [((3, own_rows, LANES), F32)],
            flops=10**9,
        )(y, low, high)
        keep, following, even = call(add_kernel, [(tile, LANES)] * 3)(
            keep, following, even
        )
        even, following = swap("gx", even, following)
        z, *faces = call(
            place_kernel,
            [(3, nx, ny, nz)] + [(3, ny, nz)] * 2 + [(3, nx, nz)] * 2,
            flops=10**9,
        )(row, deep, vector, cell_inverse, keep, following, even)
        faces = swap("gx", *faces[1::-1])[::-1] + swap("gy", *faces[:1:-1])[::-1]
        (part,) = call(inner_kernel, [field], flops=10**7)(z, diag_blocks, off_blocks)
        return z, part, faces

    z1, part, faces = precondition(right_side, picked)
    w1, turned, picked = call(
        next_kernel, [field, field, (tile, LANES)], flops=10**9
    )(send_cells, deep, part, *faces, diag_blocks, off_blocks, right_side)
    z2, part, faces = precondition(turned, picked)
    w2, sums = call(gram_kernel, [field, (8, LANES)])(
        part, *faces, off_blocks, right_side, w1
    )
    sums = merge_all(sums)
    return tuple(
        call(final_kernel, [field, field])(sums, right_side, z1, z2, w1, w2)
    )


def solution(mesh):
    return jax.shard_map(
        body,
        mesh=mesh,
        in_specs=(
            P(None, "gx", "gy", None),
            P(None, "gx", "gy", None),
            P(None, None, "gx", "gy", None),
            P(None, "gx", "gy", None),
            P(("gx", "gy"), None),
            P(("gx", "gy"), None),
            P(("gx", "gy")),
            P(None, None, ("gx", "gy")),
            P(None, None, ("gx", "gy")),
        ),
        out_specs=(P(None, "gx", "gy", None), P(None, "gx", "gy", None)),
        check_vma=False,
    )
```

```python
import functools

import jax
import jax.numpy as jnp
from jax import lax
from jax.experimental import pallas as pl
from jax.experimental.pallas import tpu as pltpu
from jax.sharding import PartitionSpec as P

LANES = 128
F32 = jnp.float32
BF16 = jnp.bfloat16


def round_up(value, unit):
    return -(-value // unit) * unit


def iota(shape, dim):
    return lax.broadcasted_iota(jnp.int32, shape, dim)


def split(value, pieces):
    out = []
    for _ in range(pieces - 1):
        piece = value.astype(BF16)
        out.append(piece)
        value = value - piece.astype(F32)
    out.append(value.astype(BF16))
    return out


def mm(left, right, trans=False):
    dims = (((1,), (1 if trans else 0,)), ((), ()))
    return lax.dot_general(left, right, dims, preferred_element_type=F32)


def mm_exact(value, choice):
    total = None
    for piece in split(value, 3):
        part = mm(piece, choice)
        total = part if total is None else total + part
    return total


def ones_where(mask):
    return jnp.where(mask, 1.0, 0.0).astype(BF16)


def call(kernel, outs, scratch=(), flops=0, space=pltpu.VMEM, mib=40):
    def run(*args):
        shapes = [
            o if hasattr(o, "dtype") else jax.ShapeDtypeStruct(o, F32) for o in outs
        ]
        moved = sum(a.size * a.dtype.itemsize for a in (*args, *shapes))
        return pl.pallas_call(
            kernel,
            out_shape=shapes,
            in_specs=[pl.BlockSpec(memory_space=space)] * len(args),
            out_specs=[pl.BlockSpec(memory_space=pltpu.VMEM)] * len(outs),
            scratch_shapes=[s if hasattr(s, "dtype") else pltpu.VMEM(*s) for s in scratch],
            cost_estimate=pl.CostEstimate(
                flops=flops, bytes_accessed=moved, transcendentals=0
            ),
            compiler_params=pltpu.CompilerParams(vmem_limit_bytes=mib * 2**20),
        )(*args)

    return run


def chunk_of(slots):
    for groups in (5, 4, 3, 2, 1):
        if slots % (groups * LANES) == 0:
            return groups * LANES


def is_odd(axis):
    return lax.rem(lax.axis_index(axis), 2) == 1


def row_and_depth(cells, nz):
    if nz & (nz - 1) == 0:
        return lax.shift_right_logical(cells, nz.bit_length() - 1), cells & (nz - 1)
    return lax.div(cells, jnp.int32(nz)), lax.rem(cells, jnp.int32(nz))


def pick(field, cells_ref, deep_ref, out_ref):
    _, rows, depth = field.shape
    slots = cells_ref.shape[1]
    blocks = slots // LANES
    chunk = chunk_of(slots)
    left = jnp.concatenate(split(field.reshape(3 * rows, depth), 2), axis=1)
    for start in range(0, slots, chunk):
        row, _ = row_and_depth(cells_ref[:, start : start + chunk], depth)
        right = deep_ref[:, start : start + chunk]
        found = mm(left, jnp.concatenate([right, right], axis=0))
        here = iota((rows, chunk), 0) == row
        for comp in range(3):
            part = jnp.where(here, found[comp * rows : (comp + 1) * rows], 0.0)
            line = jnp.sum(part, axis=0, keepdims=True)
            for piece in range(chunk // LANES):
                at = comp * blocks + start // LANES + piece
                out_ref[at : at + 1, :] = line[:, piece * LANES : (piece + 1) * LANES]
    pad = out_ref.shape[0] - 3 * blocks
    if pad:
        out_ref[3 * blocks :, :] = jnp.zeros((pad, LANES), F32)


def one_hot(out_ref, values):
    chunk = chunk_of(out_ref.shape[1])
    for start in range(0, out_ref.shape[1], chunk):
        lanes = slice(start, start + chunk)
        out_ref[:, lanes] = ones_where(
            iota((out_ref.shape[0], chunk), 0) == values(lanes)
        )


def scaled(hot, lines):
    rows = hot.shape[0]
    out = []
    for place in range(2):
        for line in lines:
            piece = split(line, 2)[place].astype(F32)
            few = jnp.broadcast_to(piece, (16, piece.shape[1])).astype(BF16)
            out += [few * hot[at : at + 16] for at in range(0, rows, 16)]
    return jnp.concatenate(out, axis=0)


def times_diag(d_ref, field):
    nx, ny, nz = d_ref.shape[1:]
    return jnp.stack(
        [
            sum(d_ref[3 * a + b] * field[b] for b in range(3)).reshape(nx * ny, nz)
            for a in range(3)
        ]
    )


def first_kernel(
    cells_hbm, v_hbm, d_hbm, out_ref, cells_ref, v_ref, d_ref, deep_ref, sem
):
    pairs = [(cells_hbm, cells_ref), (v_hbm, v_ref)]
    pairs += [(d_hbm.at[entry], d_ref.at[entry]) for entry in range(9)]
    copies = [
        pltpu.make_async_copy(src, dst, sem.at[place])
        for place, (src, dst) in enumerate(pairs)
    ]
    for copy in copies:
        copy.start()
    copies[0].wait()
    depth = v_ref.shape[3]
    one_hot(deep_ref, lambda lanes: row_and_depth(cells_ref[:, lanes], depth)[1])
    for copy in copies[1:]:
        copy.wait()
    pick(times_diag(d_ref, [v_ref[b] for b in range(3)]), cells_ref, deep_ref, out_ref)


def spread_matrix(wells, width):
    shape = (wells, wells * width)
    gap = iota(shape, 1) - width * iota(shape, 0)
    return ones_where((gap >= 0) & (gap < width))


def last_matrix(wells, width, comp):
    shape = (wells * width, wells)
    return ones_where(iota(shape, 0) == width * iota(shape, 1) + (width - 3 + comp))


def prep_kernel(idx_ref, cells_ref, low_ref, high_ref, deep_ref, row_ref):
    wide = low_ref.shape[0]
    depth = deep_ref.shape[0]
    one_hot(low_ref, lambda lanes: idx_ref[:, lanes] & (wide - 1))
    one_hot(
        high_ref,
        lambda lanes: lax.shift_right_arithmetic(idx_ref[:, lanes], wide.bit_length() - 1),
    )
    one_hot(row_ref, lambda lanes: row_and_depth(cells_ref[:, lanes], depth)[0])
    one_hot(deep_ref, lambda lanes: row_and_depth(cells_ref[:, lanes], depth)[1])


def chain_kernel(
    value_ref, g_ref, couple_ref, out_ref, h_ref, e_ref, apart_ref, part_ref
):
    out_ref[...] = value_ref[...]
    chunks, width, span_all = g_ref.shape
    wells = couple_ref.shape[2]
    span = width // 3
    for lane in range(0, span_all, LANES):
        part_ref[...] = g_ref[:, :, lane : lane + LANES]
        for comp in range(3):
            apart_ref[comp, :, :, lane : lane + LANES] = part_ref[
                :, pl.ds(comp, span, stride=3), :
            ]
    spread = spread_matrix(wells, width)
    heads = [g_ref[:, d, :] for d in range(3)]
    for b in range(3):
        total = sum(
            heads[d] * mm_exact(couple_ref[3 * d + b], spread)[:chunks] for d in range(3)
        )
        h_ref[b] = jnp.zeros(h_ref.shape[1:], F32)
        h_ref[b, :chunks, :] = total
        full = h_ref[b]
        for a in range(3):
            e_ref[3 * a + b] = mm_exact(full, last_matrix(wells, width, a))


def pool_column(pool_ref, column, first, blocks):
    odd_x = is_odd("gx")
    tile = column.shape[0] // 3
    own, even, following = column[:tile], column[tile : 2 * tile], column[2 * tile :]
    parts = (jnp.where(odd_x, even, following), own, jnp.where(odd_x, following, even))
    for a, part in enumerate(parts):
        for comp in range(3):
            at = (first + a) * blocks
            pool_ref[comp, at : at + blocks, :] = part[comp * blocks : (comp + 1) * blocks]


def clear_tail(pool_ref, used):
    pool_ref[:, used:, :] = jnp.zeros((3, pool_ref.shape[1] - used, LANES), F32)


def gather_lines(pool_ref, idx_ref, low_ref, first_row):
    half = pool_ref.shape[1] // 2
    wide = 2 * LANES
    pooled = jnp.concatenate(
        [
            jnp.concatenate(
                [pool_ref[comp, pl.ds(odd, half, stride=2), :] for odd in range(2)], axis=1
            )
            for comp in range(3)
        ],
        axis=0,
    )
    left = jnp.concatenate(split(pooled, 2), axis=1)
    slots = idx_ref.shape[1]
    size = chunk_of(slots)
    for start in range(0, slots, size):
        place = idx_ref[:, start : start + size]
        right = low_ref[:, start : start + size]
        found = mm(left, jnp.concatenate([right, right], axis=0))
        block = lax.shift_right_arithmetic(place, wide.bit_length() - 1) - first_row
        here = iota((half, size), 0) == block
        for comp in range(3):
            part = jnp.where(here, found[comp * half : (comp + 1) * half], 0.0)
            yield start, comp, jnp.sum(part, axis=0, keepdims=True)


def scatter_lines(pool_ref, y_ref, low_ref, high_ref, first_row, group):
    half = pool_ref.shape[1] // 2
    slots = low_ref.shape[1]
    size = chunk_of(slots)
    spread_out = None
    for start in range(0, slots, size):
        lanes = slice(start, start + size)
        steps = range(start // group, (start + size) // group)
        lines = [
            jnp.concatenate(
                [y_ref[c : c + 1, comp * group : (comp + 1) * group] for c in steps], axis=1
            )
            for comp in range(3)
        ]
        hot = high_ref[first_row : first_row + half, lanes]
        part = mm(scaled(hot, lines), low_ref[:, lanes], trans=True)
        spread_out = part if spread_out is None else spread_out + part
    spread_out = spread_out[: 3 * half] + spread_out[3 * half :]
    for comp in range(3):
        block = spread_out[comp * half : (comp + 1) * half]
        for odd in range(2):
            pool_ref[comp, pl.ds(odd, half, stride=2), :] = block[
                :, odd * LANES : (odd + 1) * LANES
            ]


def own_gather_kernel(idx_ref, own_ref, low_ref, r_ref, pool_ref):
    group = r_ref.shape[2]
    blocks = idx_ref.shape[1] // LANES
    clear_tail(pool_ref, 3 * blocks)
    pool_column(pool_ref, own_ref[...], 0, blocks)
    r_ref[...] = jnp.zeros(r_ref.shape, F32)
    first_row = round_up(3 * blocks, 16)
    for start, comp, line in gather_lines(pool_ref, idx_ref, low_ref, first_row):
        for piece in range(line.shape[1] // group):
            at = start // group + piece
            r_ref[comp, at : at + 1, :] = line[:, piece * group : (piece + 1) * group]


def own_scatter_kernel(y_ref, low_ref, high_ref, keep_ref, pool_ref):
    blocks = low_ref.shape[1] // LANES
    tile = keep_ref.shape[0] // 3
    first_row = round_up(3 * blocks, 16)
    scatter_lines(pool_ref, y_ref, low_ref, high_ref, first_row, y_ref.shape[1] // 3)
    keep_ref[...] = jnp.zeros(keep_ref.shape, F32)
    for a in range(3):
        for comp in range(3):
            at = slice(a * tile + comp * blocks, a * tile + (comp + 1) * blocks)
            keep_ref[at, :] = pool_ref[comp, a * blocks : (a + 1) * blocks, :]


def solve_kernel(
    idx_ref, even_ref, next_ref, part_ref, g_ref, h_ref, e_ref, low_ref, high_ref,
    y_ref, to_next_ref, to_even_ref,
    pool_ref, r_ref, q_ref, tail_ref, p_ref,
):
    _, chunks, span, span_all = g_ref.shape
    width = 3 * span
    wells = span_all // width
    blocks = idx_ref.shape[1] // LANES
    tile = even_ref.shape[0] // 3
    group = wells * span
    odd_y = is_odd("gy")
    clear_tail(pool_ref, 6 * blocks)
    even, following = even_ref[...], next_ref[...]
    pool_column(pool_ref, jnp.where(odd_y, even, following), 0, blocks)
    pool_column(pool_ref, jnp.where(odd_y, following, even), 3, blocks)
    r_ref[...] = jnp.zeros(r_ref.shape, F32)
    for start, comp, line in gather_lines(pool_ref, idx_ref, low_ref, 0):
        for piece in range(line.shape[1] // group):
            at = start // group + piece
            r_ref[comp, at : at + 1, :] = (
                line[:, piece * group : (piece + 1) * group] + part_ref[comp, at : at + 1, :]
            )
    two = (2 * group, span_all)
    well_of = lax.shift_right_logical(iota(two, 0) & (group - 1), (span - 1).bit_length())
    gap = iota(two, 1) - width * well_of
    spread = ones_where((gap >= 0) & (gap < width))
    own = (iota((span, group), 1) & (span - 1)) == iota((span, group), 0)
    total = None
    for comp in range(3):
        values = r_ref[comp][:chunks]
        wide = jnp.where(own[None], values[:, None, :], 0.0).reshape(chunks * span, group)
        lifted = mm(jnp.concatenate(split(wide, 2), axis=1), spread)
        lifted = lifted.reshape(chunks, span, span_all)
        part = g_ref[comp] * lifted
        total = part if total is None else total + part
    q_ref[...] = jnp.zeros(q_ref.shape, F32)
    q_ref[:chunks, :] = jnp.sum(total, axis=1)
    plain = q_ref[...]
    for a in range(3):
        tail_ref[a] = mm_exact(plain, last_matrix(wells, width, a))
    p_ref[...] = jnp.zeros(p_ref.shape, F32)
    state = [jnp.zeros((1, wells), F32)] * 3
    for c in range(chunks - 1):
        state = [
            tail_ref[a, c : c + 1, :]
            - (
                e_ref[3 * a, c : c + 1, :] * state[0]
                + e_ref[3 * a + 1, c : c + 1, :] * state[1]
                + e_ref[3 * a + 2, c : c + 1, :] * state[2]
            )
            for a in range(3)
        ]
        for a in range(3):
            p_ref[a, c + 1 : c + 2, :] = state[a]
    wide_well = spread_matrix(wells, width)
    for b in range(3):
        plain = plain - h_ref[b] * mm_exact(p_ref[b], wide_well)
    square = (span_all, span_all)
    lane = iota((1, span_all), 1)
    comp_of = lax.div(lane, jnp.int32(group))
    rest = lax.rem(lane, jnp.int32(group))
    source = width * lax.div(rest, jnp.int32(span)) + 3 * lax.rem(rest, jnp.int32(span)) + comp_of
    y_ref[...] = mm_exact(plain, ones_where(iota(square, 0) == source))
    scatter_lines(pool_ref, y_ref, low_ref, high_ref, 0, group)
    for dst in (to_even_ref, to_next_ref):
        dst[...] = jnp.zeros(dst.shape, F32)
    for a in range(3):
        for comp in range(3):
            before, after = [
                pool_ref[comp, (b + a) * blocks : (b + a + 1) * blocks, :] for b in (0, 3)
            ]
            at = slice(a * tile + comp * blocks, a * tile + (comp + 1) * blocks)
            to_even_ref[at, :] = jnp.where(odd_y, before, after)
            to_next_ref[at, :] = jnp.where(odd_y, after, before)


def add_kernel(x_ref, y_ref, z_ref, keep_ref, to_next_ref, to_even_ref):
    tile = keep_ref.shape[0]
    odd_x = is_odd("gx")
    low, mid, high = [
        x_ref[part, :] + y_ref[part, :] + z_ref[part, :]
        for part in [slice(place * tile, (place + 1) * tile) for place in range(3)]
    ]
    keep_ref[...] = mid
    to_even_ref[...] = jnp.where(odd_x, low, high)
    to_next_ref[...] = jnp.where(odd_x, high, low)


def place_kernel(
    row_ref, deep_ref, v_ref, inv_ref, x_ref, y_ref, z_ref,
    out_ref, x_next_ref, x_even_ref, y_next_ref, y_even_ref,
):
    (first_x, last_x), (first_y, last_y) = [
        (lax.axis_index(axis) == 0, lax.axis_index(axis) == lax.axis_size(axis) - 1)
        for axis in ("gx", "gy")
    ]
    odd_x, odd_y = is_odd("gx"), is_odd("gy")
    nx, ny, nz = v_ref.shape[1:]
    rows = nx * ny
    slots = row_ref.shape[1]
    blocks = slots // LANES
    back = x_ref[...] + y_ref[...] + z_ref[...]
    size = chunk_of(slots)
    placed = None
    for start in range(0, slots, size):
        lanes = slice(start, start + size)
        steps = range(start // LANES, (start + size) // LANES)
        lines = [
            jnp.concatenate(
                [back[comp * blocks + at : comp * blocks + at + 1] for at in steps], axis=1
            )
            for comp in range(3)
        ]
        part = mm(scaled(row_ref[:, lanes], lines), deep_ref[:, lanes], trans=True)
        placed = part if placed is None else placed + part
    placed = placed[: 3 * rows] + placed[3 * rows :]
    for a in range(3):
        own = sum(inv_ref[3 * a + b] * v_ref[b] for b in range(3))
        out_ref[a] = own + placed[a * rows : (a + 1) * rows].reshape(nx, ny, nz)
        low = jnp.where(first_x, 0.0, out_ref[a, 0])
        high = jnp.where(last_x, 0.0, out_ref[a, nx - 1])
        x_even_ref[a] = jnp.where(odd_x, low, high)
        x_next_ref[a] = jnp.where(odd_x, high, low)
        low = jnp.where(first_y, 0.0, out_ref[a, :, 0, :])
        high = jnp.where(last_y, 0.0, out_ref[a, :, ny - 1, :])
        y_even_ref[a] = jnp.where(odd_y, low, high)
        y_next_ref[a] = jnp.where(odd_y, high, low)


def inner_kernel(z_ref, d_ref, off_ref, w_ref):
    nx, ny, nz = z_ref.shape[1:]
    row = iota((ny, nz), 0)
    lane = iota((ny, nz), 1)
    for x in range(nx):
        beside = []
        for b in range(3):
            own = z_ref[b, x]
            beside.append(
                [
                    z_ref[b, x - 1] if x else None,
                    z_ref[b, x + 1] if x < nx - 1 else None,
                    jnp.where(row == 0, 0.0, pltpu.roll(own, 1, 0)),
                    jnp.where(row == ny - 1, 0.0, pltpu.roll(own, ny - 1, 0)),
                    jnp.where(lane == 0, 0.0, pltpu.roll(own, 1, 1)),
                    jnp.where(lane == nz - 1, 0.0, pltpu.roll(own, nz - 1, 1)),
                ]
            )
        for a in range(3):
            total = sum(d_ref[3 * a + b, x] * z_ref[b, x] for b in range(3))
            for face in range(6):
                for b in range(3):
                    if beside[b][face] is not None:
                        total = total + off_ref[face, 3 * a + b, x] * beside[b][face]
            w_ref[a, x] = total


def add_faces(part_ref, faces, off_ref, w_ref):
    nx, ny, nz = part_ref.shape[1:]
    odd_x, odd_y = is_odd("gx"), is_odd("gy")
    x_next, x_even, y_next, y_even = [face[...] for face in faces]
    xl, xh = jnp.where(odd_x, x_even, x_next), jnp.where(odd_x, x_next, x_even)
    yl, yh = jnp.where(odd_y, y_even, y_next), jnp.where(odd_y, y_next, y_even)
    for a in range(3):
        w_ref[a] = part_ref[a]
        for x, face, beside in ((0, 0, xl), (nx - 1, 1, xh)):
            w_ref[a, x] += sum(off_ref[face, 3 * a + b, x] * beside[b] for b in range(3))
        for y, face, beside in ((0, 2, yl), (ny - 1, 3, yh)):
            w_ref[a, :, y, :] += sum(
                off_ref[face, 3 * a + b, :, y, :] * beside[b] for b in range(3)
            )


def next_kernel(
    cells_ref, deep_ref, part_ref, f0_ref, f1_ref, f2_ref, f3_ref, d_ref, off_ref, v_ref,
    w_ref, t_ref, out_ref,
):
    add_faces(part_ref, (f0_ref, f1_ref, f2_ref, f3_ref), off_ref, w_ref)
    t_ref[...] = w_ref[...] - v_ref[...]
    pick(times_diag(d_ref, [t_ref[b] for b in range(3)]), cells_ref, deep_ref, out_ref)


def gram_kernel(
    part_ref, f0_ref, f1_ref, f2_ref, f3_ref, off_ref, v_ref, w1_ref,
    w_ref, sums_ref,
):
    add_faces(part_ref, (f0_ref, f1_ref, f2_ref, f3_ref), off_ref, w_ref)
    one, two, rhs = w1_ref[...], w_ref[...], v_ref[...]
    top_one = jnp.maximum(jnp.max(jnp.abs(one)), 1e-30)
    top_two = jnp.maximum(jnp.max(jnp.abs(two)), 1e-30)
    one = one * (1.0 / jnp.full((1, 1), top_one))
    two = two * (1.0 / jnp.full((1, 1), top_two))
    sums = [
        jnp.sum(one * one), jnp.sum(one * two), jnp.sum(two * two),
        jnp.sum(one * rhs), jnp.sum(two * rhs), top_one, top_two,
    ]
    line = iota(sums_ref.shape[1:], 0)
    total = jnp.zeros(sums_ref.shape[1:], F32)
    for place, value in enumerate(sums):
        total = jnp.where(line == place, value, total)
    sums_ref[...] = jnp.broadcast_to(total[None], sums_ref.shape)


def final_kernel(
    all_ref, v_ref, z1_ref, z2_ref, w1_ref, w2_ref, sol_ref, res_ref
):
    every = [all_ref[:, place, :] for place in range(7)]
    top_one = jnp.max(every[5], axis=0, keepdims=True)
    top_two = jnp.max(every[6], axis=0, keepdims=True)
    one = every[5] / top_one
    two = every[6] / top_two
    scales = (one * one, one * two, two * two, one, two)
    g11, g12, g22, r1, r2 = [
        jnp.sum(value * scale, axis=0, keepdims=True) for value, scale in zip(every, scales)
    ]
    det = g11 * g22 - g12 * g12
    y1 = ((g22 * r1 - g12 * r2) / det / top_one)[:, :1]
    y2 = ((g11 * r2 - g12 * r1) / det / top_two)[:, :1]
    sol_ref[...] = y1 * z1_ref[...] + y2 * z2_ref[...]
    res_ref[...] = v_ref[...] - y1 * w1_ref[...] - y2 * w2_ref[...]


def swap(axis, to_even, to_next):
    size = {name: lax.axis_size(name) for name in ("gx", "gy")}
    count, breadth = size[axis], size["gy" if axis == "gx" else "gx"]

    def device(along, across):
        return along * size["gy"] + across if axis == "gx" else across * size["gy"] + along

    out = []
    order = [(1, to_next), (0, to_even)]
    same = to_even is to_next
    for first, value in order:
        pairs = []
        for across in range(breadth):
            for i in range(count):
                other = i + 1 if i % 2 == first else i - 1
                if 0 <= other < count:
                    pairs.append((device(i, across), device(other, across)))
                elif across ^ 1 < breadth:
                    pairs.append((device(i, across), device(i, across ^ 1)))
                else:
                    pairs.append((device(i, across), device(i, across)))
        out.append(lax.ppermute(value, ("gx", "gy"), pairs))
    return out[::-1]


def body(
    right_side,
    diag_blocks,
    off_blocks,
    cell_inverse,
    send_cells,
    recv_index,
    seg_count,
    span_inverse,
    span_couple,
):
    _, nx, ny, nz = right_side.shape
    slots = send_cells.shape[1]
    wells, longest = recv_index.shape
    chunks, width, span_all = span_inverse.shape
    span = width // 3
    blocks = slots // LANES
    tile = round_up(3 * blocks, 16)
    beside_rows = round_up(6 * blocks, 32)
    own_rows = round_up(3 * blocks, 32)
    tall = round_up(chunks, 16)
    field = right_side.shape
    (picked,) = call(
        first_kernel,
        [(tile, LANES)],
        [
            (send_cells.shape, jnp.int32),
            (field, F32),
            (diag_blocks.shape, F32),
            ((nz, slots), BF16),
            pltpu.SemaphoreType.DMA((11,)),
        ],
        flops=10**9,
        space=pltpu.HBM,
        mib=60,
    )(send_cells, right_side, diag_blocks)
    live = jnp.arange(longest)[None, :] < seg_count[:, None]
    along, column = recv_index // slots // 3, recv_index // slots % 3
    index = recv_index % slots + slots * along
    index = index + jnp.where(column == 1, beside_rows * LANES, slots * 3 * (column // 2))
    index = jnp.where(live, index, -1)
    index = index.reshape(wells, chunks, span).transpose(1, 0, 2).reshape(1, wells * longest)
    couple = jnp.pad(span_couple.transpose(1, 0, 2), ((0, 0), (0, tall - chunks), (0, 0)))
    low, high, deep, row = call(
        prep_kernel,
        [
            jax.ShapeDtypeStruct((height, slots), BF16)
            for height in (2 * LANES, (beside_rows + own_rows) // 2, nz, nx * ny)
        ],
    )(index, send_cells)
    held, h, e, apart = call(
        chain_kernel,
        [
            picked.shape,
            (3, tall, span_all),
            (9, tall, wells),
            (3, chunks, span, span_all),
        ],
        [((chunks, width, LANES), F32)],
    )(picked, span_inverse, couple)

    def precondition(vector, picked):
        beside = swap("gx", picked, picked)
        own = held if vector is right_side else picked
        column = jnp.concatenate([own, *beside], axis=0)
        even, following = swap("gy", column, column)
        (part,) = call(
            own_gather_kernel,
            [(3, tall, wells * span)],
            [((3, own_rows, LANES), F32)],
            flops=10**9,
        )(index, column, low)
        y, following, even = call(
            solve_kernel,
            [(tall, span_all)] + [(3 * tile, LANES)] * 2,
            [
                ((3, beside_rows, LANES), F32),
                ((3, tall, wells * span), F32),
                ((tall, span_all), F32),
                ((3, tall, wells), F32),
                ((3, tall, wells), F32),
            ],
            flops=3 * 10**9,
        )(index, even, following, part, apart, h, e, low, high)
        even, following = swap("gy", even, following)
        (keep,) = call(
            own_scatter_kernel,
            [(3 * tile, LANES)],
            [((3, own_rows, LANES), F32)],
            flops=10**9,
        )(y, low, high)
        keep, following, even = call(add_kernel, [(tile, LANES)] * 3)(
            keep, following, even
        )
        even, following = swap("gx", even, following)
        z, *faces = call(
            place_kernel,
            [(3, nx, ny, nz)] + [(3, ny, nz)] * 2 + [(3, nx, nz)] * 2,
            flops=10**9,
        )(row, deep, vector, cell_inverse, keep, following, even)
        faces = swap("gx", *faces[1::-1])[::-1] + swap("gy", *faces[:1:-1])[::-1]
        (part,) = call(inner_kernel, [field], flops=10**7)(z, diag_blocks, off_blocks)
        return z, part, faces

    z1, part, faces = precondition(right_side, picked)
    w1, turned, picked = call(
        next_kernel, [field, field, (tile, LANES)], flops=10**9
    )(send_cells, deep, part, *faces, diag_blocks, off_blocks, right_side)
    z2, part, faces = precondition(turned, picked)
    count = lax.axis_size(("gx", "gy"))
    w2, sums = call(gram_kernel, [field, (count, 8, LANES)])(
        part, *faces, off_blocks, right_side, w1
    )
    sums = lax.all_to_all(sums, ("gx", "gy"), 0, 0)
    return tuple(
        call(final_kernel, [field, field])(sums, right_side, z1, z2, w1, w2)
    )


def solution(mesh):
    return jax.shard_map(
        body,
        mesh=mesh,
        in_specs=(
            P(None, "gx", "gy", None),
            P(None, "gx", "gy", None),
            P(None, None, "gx", "gy", None),
            P(None, "gx", "gy", None),
            P(("gx", "gy"), None),
            P(("gx", "gy"), None),
            P(("gx", "gy")),
            P(None, None, ("gx", "gy")),
            P(None, None, ("gx", "gy")),
        ),
        out_specs=(P(None, "gx", "gy", None), P(None, "gx", "gy", None)),
        check_vma=False,
    )
```

```python
import functools

import jax
import jax.numpy as jnp
from jax import lax
from jax.experimental import pallas as pl
from jax.experimental.pallas import tpu as pltpu
from jax.sharding import PartitionSpec as P

LANES = 128
F32 = jnp.float32
BF16 = jnp.bfloat16


def round_up(value, unit):
    return -(-value // unit) * unit


def iota(shape, dim):
    return lax.broadcasted_iota(jnp.int32, shape, dim)


def split(value, pieces):
    out = []
    for _ in range(pieces - 1):
        piece = value.astype(BF16)
        out.append(piece)
        value = value - piece.astype(F32)
    out.append(value.astype(BF16))
    return out


def mm(left, right, trans=False):
    dims = (((1,), (1 if trans else 0,)), ((), ()))
    return lax.dot_general(left, right, dims, preferred_element_type=F32)


def mm_exact(value, choice):
    total = None
    for piece in split(value, 3):
        part = mm(piece, choice)
        total = part if total is None else total + part
    return total


def ones_where(mask):
    return jnp.where(mask, 1.0, 0.0).astype(BF16)


def call(kernel, outs, scratch=(), flops=0, space=pltpu.VMEM, mib=20):
    def run(*args):
        shapes = [
            o if hasattr(o, "dtype") else jax.ShapeDtypeStruct(o, F32) for o in outs
        ]
        moved = sum(a.size * a.dtype.itemsize for a in (*args, *shapes))
        return pl.pallas_call(
            kernel,
            out_shape=shapes,
            in_specs=[pl.BlockSpec(memory_space=space)] * len(args),
            out_specs=[pl.BlockSpec(memory_space=pltpu.VMEM)] * len(outs),
            scratch_shapes=[s if hasattr(s, "dtype") else pltpu.VMEM(*s) for s in scratch],
            cost_estimate=pl.CostEstimate(
                flops=flops, bytes_accessed=moved, transcendentals=0
            ),
            compiler_params=pltpu.CompilerParams(vmem_limit_bytes=mib * 2**20),
        )(*args)

    return run


def chunk_of(slots):
    for groups in (5, 4, 3, 2, 1):
        if slots % (groups * LANES) == 0:
            return groups * LANES


def is_odd(axis):
    return lax.rem(lax.axis_index(axis), 2) == 1


def row_and_depth(cells, nz):
    if nz & (nz - 1) == 0:
        return lax.shift_right_logical(cells, nz.bit_length() - 1), cells & (nz - 1)
    return lax.div(cells, jnp.int32(nz)), lax.rem(cells, jnp.int32(nz))


def pick(field, cells_ref, deep_ref, out_ref):
    _, rows, depth = field.shape
    slots = cells_ref.shape[1]
    blocks = slots // LANES
    chunk = chunk_of(slots)
    left = jnp.concatenate(split(field.reshape(3 * rows, depth), 2), axis=1)
    for start in range(0, slots, chunk):
        row, _ = row_and_depth(cells_ref[:, start : start + chunk], depth)
        right = deep_ref[:, start : start + chunk]
        found = mm(left, jnp.concatenate([right, right], axis=0))
        here = iota((rows, chunk), 0) == row
        for comp in range(3):
            part = jnp.where(here, found[comp * rows : (comp + 1) * rows], 0.0)
            line = jnp.sum(part, axis=0, keepdims=True)
            for piece in range(chunk // LANES):
                at = comp * blocks + start // LANES + piece
                out_ref[at : at + 1, :] = line[:, piece * LANES : (piece + 1) * LANES]
    pad = out_ref.shape[0] - 3 * blocks
    if pad:
        out_ref[3 * blocks :, :] = jnp.zeros((pad, LANES), F32)


def one_hot(out_ref, values):
    chunk = chunk_of(out_ref.shape[1])
    for start in range(0, out_ref.shape[1], chunk):
        lanes = slice(start, start + chunk)
        out_ref[:, lanes] = ones_where(
            iota((out_ref.shape[0], chunk), 0) == values(lanes)
        )


def scaled(hot, lines):
    rows = hot.shape[0]
    out = []
    for place in range(2):
        for line in lines:
            piece = split(line, 2)[place].astype(F32)
            few = jnp.broadcast_to(piece, (16, piece.shape[1])).astype(BF16)
            out += [few * hot[at : at + 16] for at in range(0, rows, 16)]
    return jnp.concatenate(out, axis=0)


def times_diag(d_ref, field):
    nx, ny, nz = d_ref.shape[1:]
    return jnp.stack(
        [
            sum(d_ref[3 * a + b] * field[b] for b in range(3)).reshape(nx * ny, nz)
            for a in range(3)
        ]
    )


def first_kernel(
    cells_hbm, v_hbm, d_hbm, out_ref, cells_ref, v_ref, d_ref, deep_ref, sem
):
    pairs = [(cells_hbm, cells_ref), (v_hbm, v_ref)]
    pairs += [(d_hbm.at[entry], d_ref.at[entry]) for entry in range(9)]
    copies = [
        pltpu.make_async_copy(src, dst, sem.at[place])
        for place, (src, dst) in enumerate(pairs)
    ]
    for copy in copies:
        copy.start()
    copies[0].wait()
    depth = v_ref.shape[3]
    one_hot(deep_ref, lambda lanes: row_and_depth(cells_ref[:, lanes], depth)[1])
    for copy in copies[1:]:
        copy.wait()
    pick(times_diag(d_ref, [v_ref[b] for b in range(3)]), cells_ref, deep_ref, out_ref)


def spread_matrix(wells, width):
    shape = (wells, wells * width)
    gap = iota(shape, 1) - width * iota(shape, 0)
    return ones_where((gap >= 0) & (gap < width))


def last_matrix(wells, width, comp):
    shape = (wells * width, wells)
    return ones_where(iota(shape, 0) == width * iota(shape, 1) + (width - 3 + comp))


def prep_kernel(idx_ref, cells_ref, low_ref, high_ref, deep_ref, row_ref):
    wide = low_ref.shape[0]
    depth = deep_ref.shape[0]
    one_hot(low_ref, lambda lanes: idx_ref[:, lanes] & (wide - 1))
    one_hot(
        high_ref,
        lambda lanes: lax.shift_right_arithmetic(idx_ref[:, lanes], wide.bit_length() - 1),
    )
    one_hot(row_ref, lambda lanes: row_and_depth(cells_ref[:, lanes], depth)[0])
    one_hot(deep_ref, lambda lanes: row_and_depth(cells_ref[:, lanes], depth)[1])


def chain_kernel(
    value_ref, g_ref, couple_ref, out_ref, h_ref, e_ref, apart_ref, part_ref
):
    out_ref[...] = value_ref[...]
    chunks, width, span_all = g_ref.shape
    wells = couple_ref.shape[2]
    span = width // 3
    for lane in range(0, span_all, LANES):
        part_ref[...] = g_ref[:, :, lane : lane + LANES]
        for comp in range(3):
            apart_ref[comp, :, :, lane : lane + LANES] = part_ref[
                :, pl.ds(comp, span, stride=3), :
            ]
    spread = spread_matrix(wells, width)
    heads = [g_ref[:, d, :] for d in range(3)]
    for b in range(3):
        total = sum(
            heads[d] * mm_exact(couple_ref[3 * d + b], spread)[:chunks] for d in range(3)
        )
        h_ref[b] = jnp.zeros(h_ref.shape[1:], F32)
        h_ref[b, :chunks, :] = total
        full = h_ref[b]
        for a in range(3):
            e_ref[3 * a + b] = mm_exact(full, last_matrix(wells, width, a))


def pool_column(pool_ref, column, first, blocks):
    odd_x = is_odd("gx")
    tile = column.shape[0] // 3
    own, even, following = column[:tile], column[tile : 2 * tile], column[2 * tile :]
    parts = (jnp.where(odd_x, even, following), own, jnp.where(odd_x, following, even))
    for a, part in enumerate(parts):
        for comp in range(3):
            at = (first + a) * blocks
            pool_ref[comp, at : at + blocks, :] = part[comp * blocks : (comp + 1) * blocks]


def clear_tail(pool_ref, used):
    pool_ref[:, used:, :] = jnp.zeros((3, pool_ref.shape[1] - used, LANES), F32)


def gather_lines(pool_ref, idx_ref, low_ref, first_row):
    half = pool_ref.shape[1] // 2
    wide = 2 * LANES
    pooled = jnp.concatenate(
        [
            jnp.concatenate(
                [pool_ref[comp, pl.ds(odd, half, stride=2), :] for odd in range(2)], axis=1
            )
            for comp in range(3)
        ],
        axis=0,
    )
    left = jnp.concatenate(split(pooled, 2), axis=1)
    slots = idx_ref.shape[1]
    size = chunk_of(slots)
    for start in range(0, slots, size):
        place = idx_ref[:, start : start + size]
        right = low_ref[:, start : start + size]
        found = mm(left, jnp.concatenate([right, right], axis=0))
        block = lax.shift_right_arithmetic(place, wide.bit_length() - 1) - first_row
        here = iota((half, size), 0) == block
        for comp in range(3):
            part = jnp.where(here, found[comp * half : (comp + 1) * half], 0.0)
            yield start, comp, jnp.sum(part, axis=0, keepdims=True)


def scatter_lines(pool_ref, y_ref, low_ref, high_ref, first_row, group):
    half = pool_ref.shape[1] // 2
    slots = low_ref.shape[1]
    size = chunk_of(slots)
    spread_out = None
    for start in range(0, slots, size):
        lanes = slice(start, start + size)
        steps = range(start // group, (start + size) // group)
        lines = [
            jnp.concatenate(
                [y_ref[c : c + 1, comp * group : (comp + 1) * group] for c in steps], axis=1
            )
            for comp in range(3)
        ]
        hot = high_ref[first_row : first_row + half, lanes]
        part = mm(scaled(hot, lines), low_ref[:, lanes], trans=True)
        spread_out = part if spread_out is None else spread_out + part
    spread_out = spread_out[: 3 * half] + spread_out[3 * half :]
    for comp in range(3):
        block = spread_out[comp * half : (comp + 1) * half]
        for odd in range(2):
            pool_ref[comp, pl.ds(odd, half, stride=2), :] = block[
                :, odd * LANES : (odd + 1) * LANES
            ]


def own_gather_kernel(idx_ref, own_ref, low_ref, r_ref, pool_ref):
    group = r_ref.shape[2]
    blocks = idx_ref.shape[1] // LANES
    clear_tail(pool_ref, 3 * blocks)
    pool_column(pool_ref, own_ref[...], 0, blocks)
    r_ref[...] = jnp.zeros(r_ref.shape, F32)
    first_row = round_up(3 * blocks, 16)
    for start, comp, line in gather_lines(pool_ref, idx_ref, low_ref, first_row):
        for piece in range(line.shape[1] // group):
            at = start // group + piece
            r_ref[comp, at : at + 1, :] = line[:, piece * group : (piece + 1) * group]


def own_scatter_kernel(y_ref, low_ref, high_ref, keep_ref, pool_ref):
    blocks = low_ref.shape[1] // LANES
    tile = keep_ref.shape[0] // 3
    first_row = round_up(3 * blocks, 16)
    scatter_lines(pool_ref, y_ref, low_ref, high_ref, first_row, y_ref.shape[1] // 3)
    keep_ref[...] = jnp.zeros(keep_ref.shape, F32)
    for a in range(3):
        for comp in range(3):
            at = slice(a * tile + comp * blocks, a * tile + (comp + 1) * blocks)
            keep_ref[at, :] = pool_ref[comp, a * blocks : (a + 1) * blocks, :]


def solve_kernel(
    idx_ref, even_ref, next_ref, part_ref, g_ref, h_ref, e_ref, low_ref, high_ref,
    y_ref, to_next_ref, to_even_ref,
    pool_ref, r_ref, q_ref, tail_ref, p_ref,
):
    _, chunks, span, span_all = g_ref.shape
    width = 3 * span
    wells = span_all // width
    blocks = idx_ref.shape[1] // LANES
    tile = even_ref.shape[0] // 3
    group = wells * span
    odd_y = is_odd("gy")
    clear_tail(pool_ref, 6 * blocks)
    even, following = even_ref[...], next_ref[...]
    pool_column(pool_ref, jnp.where(odd_y, even, following), 0, blocks)
    pool_column(pool_ref, jnp.where(odd_y, following, even), 3, blocks)
    r_ref[...] = jnp.zeros(r_ref.shape, F32)
    for start, comp, line in gather_lines(pool_ref, idx_ref, low_ref, 0):
        for piece in range(line.shape[1] // group):
            at = start // group + piece
            r_ref[comp, at : at + 1, :] = (
                line[:, piece * group : (piece + 1) * group] + part_ref[comp, at : at + 1, :]
            )
    two = (2 * group, span_all)
    well_of = lax.shift_right_logical(iota(two, 0) & (group - 1), (span - 1).bit_length())
    gap = iota(two, 1) - width * well_of
    spread = ones_where((gap >= 0) & (gap < width))
    own = (iota((span, group), 1) & (span - 1)) == iota((span, group), 0)
    total = None
    for comp in range(3):
        values = r_ref[comp][:chunks]
        wide = jnp.where(own[None], values[:, None, :], 0.0).reshape(chunks * span, group)
        lifted = mm(jnp.concatenate(split(wide, 2), axis=1), spread)
        lifted = lifted.reshape(chunks, span, span_all)
        part = g_ref[comp] * lifted
        total = part if total is None else total + part
    q_ref[...] = jnp.zeros(q_ref.shape, F32)
    q_ref[:chunks, :] = jnp.sum(total, axis=1)
    plain = q_ref[...]
    for a in range(3):
        tail_ref[a] = mm_exact(plain, last_matrix(wells, width, a))
    p_ref[...] = jnp.zeros(p_ref.shape, F32)
    state = [jnp.zeros((1, wells), F32)] * 3
    for c in range(chunks - 1):
        state = [
            tail_ref[a, c : c + 1, :]
            - (
                e_ref[3 * a, c : c + 1, :] * state[0]
                + e_ref[3 * a + 1, c : c + 1, :] * state[1]
                + e_ref[3 * a + 2, c : c + 1, :] * state[2]
            )
            for a in range(3)
        ]
        for a in range(3):
            p_ref[a, c + 1 : c + 2, :] = state[a]
    wide_well = spread_matrix(wells, width)
    for b in range(3):
        plain = plain - h_ref[b] * mm_exact(p_ref[b], wide_well)
    square = (span_all, span_all)
    lane = iota((1, span_all), 1)
    comp_of = lax.div(lane, jnp.int32(group))
    rest = lax.rem(lane, jnp.int32(group))
    source = width * lax.div(rest, jnp.int32(span)) + 3 * lax.rem(rest, jnp.int32(span)) + comp_of
    y_ref[...] = mm_exact(plain, ones_where(iota(square, 0) == source))
    scatter_lines(pool_ref, y_ref, low_ref, high_ref, 0, group)
    for dst in (to_even_ref, to_next_ref):
        dst[...] = jnp.zeros(dst.shape, F32)
    for a in range(3):
        for comp in range(3):
            before, after = [
                pool_ref[comp, (b + a) * blocks : (b + a + 1) * blocks, :] for b in (0, 3)
            ]
            at = slice(a * tile + comp * blocks, a * tile + (comp + 1) * blocks)
            to_even_ref[at, :] = jnp.where(odd_y, before, after)
            to_next_ref[at, :] = jnp.where(odd_y, after, before)


def add_kernel(x_ref, y_ref, z_ref, keep_ref, to_next_ref, to_even_ref):
    tile = keep_ref.shape[0]
    odd_x = is_odd("gx")
    low, mid, high = [
        x_ref[part, :] + y_ref[part, :] + z_ref[part, :]
        for part in [slice(place * tile, (place + 1) * tile) for place in range(3)]
    ]
    keep_ref[...] = mid
    to_even_ref[...] = jnp.where(odd_x, low, high)
    to_next_ref[...] = jnp.where(odd_x, high, low)


def place_kernel(
    row_ref, deep_ref, v_ref, inv_ref, x_ref, y_ref, z_ref,
    out_ref, x_next_ref, x_even_ref, y_next_ref, y_even_ref,
):
    (first_x, last_x), (first_y, last_y) = [
        (lax.axis_index(axis) == 0, lax.axis_index(axis) == lax.axis_size(axis) - 1)
        for axis in ("gx", "gy")
    ]
    odd_x, odd_y = is_odd("gx"), is_odd("gy")
    nx, ny, nz = v_ref.shape[1:]
    rows = nx * ny
    slots = row_ref.shape[1]
    blocks = slots // LANES
    back = x_ref[...] + y_ref[...] + z_ref[...]
    size = chunk_of(slots)
    placed = None
    for start in range(0, slots, size):
        lanes = slice(start, start + size)
        steps = range(start // LANES, (start + size) // LANES)
        lines = [
            jnp.concatenate(
                [back[comp * blocks + at : comp * blocks + at + 1] for at in steps], axis=1
            )
            for comp in range(3)
        ]
        part = mm(scaled(row_ref[:, lanes], lines), deep_ref[:, lanes], trans=True)
        placed = part if placed is None else placed + part
    placed = placed[: 3 * rows] + placed[3 * rows :]
    for a in range(3):
        own = sum(inv_ref[3 * a + b] * v_ref[b] for b in range(3))
        out_ref[a] = own + placed[a * rows : (a + 1) * rows].reshape(nx, ny, nz)
        low = jnp.where(first_x, 0.0, out_ref[a, 0])
        high = jnp.where(last_x, 0.0, out_ref[a, nx - 1])
        x_even_ref[a] = jnp.where(odd_x, low, high)
        x_next_ref[a] = jnp.where(odd_x, high, low)
        low = jnp.where(first_y, 0.0, out_ref[a, :, 0, :])
        high = jnp.where(last_y, 0.0, out_ref[a, :, ny - 1, :])
        y_even_ref[a] = jnp.where(odd_y, low, high)
        y_next_ref[a] = jnp.where(odd_y, high, low)


def inner_kernel(z_ref, d_ref, off_ref, w_ref):
    nx, ny, nz = z_ref.shape[1:]
    row = iota((ny, nz), 0)
    lane = iota((ny, nz), 1)
    for x in range(nx):
        beside = []
        for b in range(3):
            own = z_ref[b, x]
            beside.append(
                [
                    z_ref[b, x - 1] if x else None,
                    z_ref[b, x + 1] if x < nx - 1 else None,
                    jnp.where(row == 0, 0.0, pltpu.roll(own, 1, 0)),
                    jnp.where(row == ny - 1, 0.0, pltpu.roll(own, ny - 1, 0)),
                    jnp.where(lane == 0, 0.0, pltpu.roll(own, 1, 1)),
                    jnp.where(lane == nz - 1, 0.0, pltpu.roll(own, nz - 1, 1)),
                ]
            )
        for a in range(3):
            total = sum(d_ref[3 * a + b, x] * z_ref[b, x] for b in range(3))
            for face in range(6):
                for b in range(3):
                    if beside[b][face] is not None:
                        total = total + off_ref[face, 3 * a + b, x] * beside[b][face]
            w_ref[a, x] = total


def add_faces(part_ref, faces, off_ref, w_ref):
    nx, ny, nz = part_ref.shape[1:]
    odd_x, odd_y = is_odd("gx"), is_odd("gy")
    x_next, x_even, y_next, y_even = [face[...] for face in faces]
    xl, xh = jnp.where(odd_x, x_even, x_next), jnp.where(odd_x, x_next, x_even)
    yl, yh = jnp.where(odd_y, y_even, y_next), jnp.where(odd_y, y_next, y_even)
    for a in range(3):
        w_ref[a] = part_ref[a]
        for x, face, beside in ((0, 0, xl), (nx - 1, 1, xh)):
            w_ref[a, x] += sum(off_ref[face, 3 * a + b, x] * beside[b] for b in range(3))
        for y, face, beside in ((0, 2, yl), (ny - 1, 3, yh)):
            w_ref[a, :, y, :] += sum(
                off_ref[face, 3 * a + b, :, y, :] * beside[b] for b in range(3)
            )


def next_kernel(
    cells_ref, deep_ref, part_ref, f0_ref, f1_ref, f2_ref, f3_ref, d_ref, off_ref, v_ref,
    w_ref, t_ref, out_ref,
):
    add_faces(part_ref, (f0_ref, f1_ref, f2_ref, f3_ref), off_ref, w_ref)
    t_ref[...] = w_ref[...] - v_ref[...]
    pick(times_diag(d_ref, [t_ref[b] for b in range(3)]), cells_ref, deep_ref, out_ref)


def gram_kernel(
    part_ref, f0_ref, f1_ref, f2_ref, f3_ref, off_ref, v_ref, w1_ref,
    w_ref, sums_ref,
):
    add_faces(part_ref, (f0_ref, f1_ref, f2_ref, f3_ref), off_ref, w_ref)
    one, two, rhs = w1_ref[...], w_ref[...], v_ref[...]
    top_one = jnp.maximum(jnp.max(jnp.abs(one)), 1e-30)
    top_two = jnp.maximum(jnp.max(jnp.abs(two)), 1e-30)
    one = one * (1.0 / jnp.full((1, 1), top_one))
    two = two * (1.0 / jnp.full((1, 1), top_two))
    sums = [
        jnp.sum(one * one), jnp.sum(one * two), jnp.sum(two * two),
        jnp.sum(one * rhs), jnp.sum(two * rhs), top_one, top_two,
    ]
    line = iota(sums_ref.shape[1:], 1)
    total = jnp.zeros(sums_ref.shape[1:], F32)
    for place, value in enumerate(sums):
        total = jnp.where(line == place, value, total)
    sums_ref[...] = jnp.broadcast_to(total[None], sums_ref.shape)


def final_kernel(
    all_ref, v_ref, z1_ref, z2_ref, w1_ref, w2_ref, sol_ref, res_ref
):
    every = [all_ref[:, 0, place : place + 1] for place in range(7)]
    top_one = jnp.max(every[5], axis=0, keepdims=True)
    top_two = jnp.max(every[6], axis=0, keepdims=True)
    one = every[5] / top_one
    two = every[6] / top_two
    scales = (one * one, one * two, two * two, one, two)
    g11, g12, g22, r1, r2 = [
        jnp.sum(value * scale, axis=0, keepdims=True) for value, scale in zip(every, scales)
    ]
    det = g11 * g22 - g12 * g12
    y1 = (g22 * r1 - g12 * r2) / det / top_one
    y2 = (g11 * r2 - g12 * r1) / det / top_two
    sol_ref[...] = y1 * z1_ref[...] + y2 * z2_ref[...]
    res_ref[...] = v_ref[...] - y1 * w1_ref[...] - y2 * w2_ref[...]


def swap(axis, to_even, to_next):
    size = {name: lax.axis_size(name) for name in ("gx", "gy")}
    count, breadth = size[axis], size["gy" if axis == "gx" else "gx"]

    def device(along, across):
        return along * size["gy"] + across if axis == "gx" else across * size["gy"] + along

    out = []
    order = [(1, to_next), (0, to_even)]
    same = to_even is to_next
    for first, value in order:
        pairs = []
        for across in range(breadth):
            for i in range(count):
                other = i + 1 if i % 2 == first else i - 1
                if 0 <= other < count:
                    pairs.append((device(i, across), device(other, across)))
                elif across ^ 1 < breadth:
                    pairs.append((device(i, across), device(i, across ^ 1)))
                else:
                    pairs.append((device(i, across), device(i, across)))
        out.append(lax.ppermute(value, ("gx", "gy"), pairs))
    return out[::-1]


def body(
    right_side,
    diag_blocks,
    off_blocks,
    cell_inverse,
    send_cells,
    recv_index,
    seg_count,
    span_inverse,
    span_couple,
):
    _, nx, ny, nz = right_side.shape
    slots = send_cells.shape[1]
    wells, longest = recv_index.shape
    chunks, width, span_all = span_inverse.shape
    span = width // 3
    blocks = slots // LANES
    tile = round_up(3 * blocks, 16)
    beside_rows = round_up(6 * blocks, 32)
    own_rows = round_up(3 * blocks, 32)
    tall = round_up(chunks, 16)
    field = right_side.shape
    (picked,) = call(
        first_kernel,
        [(tile, LANES)],
        [
            (send_cells.shape, jnp.int32),
            (field, F32),
            (diag_blocks.shape, F32),
            ((nz, slots), BF16),
            pltpu.SemaphoreType.DMA((11,)),
        ],
        flops=10**9,
        space=pltpu.HBM,
        mib=60,
    )(send_cells, right_side, diag_blocks)
    live = jnp.arange(longest)[None, :] < seg_count[:, None]
    along, column = recv_index // slots // 3, recv_index // slots % 3
    index = recv_index % slots + slots * along
    index = index + jnp.where(column == 1, beside_rows * LANES, slots * 3 * (column // 2))
    index = jnp.where(live, index, -1)
    index = index.reshape(wells, chunks, span).transpose(1, 0, 2).reshape(1, wells * longest)
    couple = jnp.pad(span_couple.transpose(1, 0, 2), ((0, 0), (0, tall - chunks), (0, 0)))
    low, high, deep, row = call(
        prep_kernel,
        [
            jax.ShapeDtypeStruct((height, slots), BF16)
            for height in (2 * LANES, (beside_rows + own_rows) // 2, nz, nx * ny)
        ],
    )(index, send_cells)
    held, h, e, apart = call(
        chain_kernel,
        [
            picked.shape,
            (3, tall, span_all),
            (9, tall, wells),
            (3, chunks, span, span_all),
        ],
        [((chunks, width, LANES), F32)],
    )(picked, span_inverse, couple)

    def precondition(vector, picked):
        beside = swap("gx", picked, picked)
        own = held if vector is right_side else picked
        column = jnp.concatenate([own, *beside], axis=0)
        even, following = swap("gy", column, column)
        (part,) = call(
            own_gather_kernel,
            [(3, tall, wells * span)],
            [((3, own_rows, LANES), F32)],
            flops=10**9,
        )(index, column, low)
        y, following, even = call(
            solve_kernel,
            [(tall, span_all)] + [(3 * tile, LANES)] * 2,
            [
                ((3, beside_rows, LANES), F32),
                ((3, tall, wells * span), F32),
                ((tall, span_all), F32),
                ((3, tall, wells), F32),
                ((3, tall, wells), F32),
            ],
            flops=3 * 10**9,
        )(index, even, following, part, apart, h, e, low, high)
        even, following = swap("gy", even, following)
        (keep,) = call(
            own_scatter_kernel,
            [(3 * tile, LANES)],
            [((3, own_rows, LANES), F32)],
            flops=10**9,
        )(y, low, high)
        keep, following, even = call(add_kernel, [(tile, LANES)] * 3)(
            keep, following, even
        )
        even, following = swap("gx", even, following)
        z, *faces = call(
            place_kernel,
            [(3, nx, ny, nz)] + [(3, ny, nz)] * 2 + [(3, nx, nz)] * 2,
            flops=10**9,
        )(row, deep, vector, cell_inverse, keep, following, even)
        faces = swap("gx", *faces[1::-1])[::-1] + swap("gy", *faces[:1:-1])[::-1]
        (part,) = call(inner_kernel, [field], flops=10**7)(z, diag_blocks, off_blocks)
        return z, part, faces

    z1, part, faces = precondition(right_side, picked)
    w1, turned, picked = call(
        next_kernel, [field, field, (tile, LANES)], flops=10**9
    )(send_cells, deep, part, *faces, diag_blocks, off_blocks, right_side)
    z2, part, faces = precondition(turned, picked)
    count = lax.axis_size(("gx", "gy"))
    w2, sums = call(gram_kernel, [field, (count, 1, LANES)])(
        part, *faces, off_blocks, right_side, w1
    )
    sums = lax.all_to_all(sums, ("gx", "gy"), 0, 0)
    return tuple(
        call(final_kernel, [field, field])(sums, right_side, z1, z2, w1, w2)
    )


def solution(mesh):
    return jax.shard_map(
        body,
        mesh=mesh,
        in_specs=(
            P(None, "gx", "gy", None),
            P(None, "gx", "gy", None),
            P(None, None, "gx", "gy", None),
            P(None, "gx", "gy", None),
            P(("gx", "gy"), None),
            P(("gx", "gy"), None),
            P(("gx", "gy")),
            P(None, None, ("gx", "gy")),
            P(None, None, ("gx", "gy")),
        ),
        out_specs=(P(None, "gx", "gy", None), P(None, "gx", "gy", None)),
        check_vma=False,
    )
```

```python
import functools

import jax
import jax.numpy as jnp
from jax import lax
from jax.experimental import pallas as pl
from jax.experimental.pallas import tpu as pltpu
from jax.sharding import PartitionSpec as P

LANES = 128
F32 = jnp.float32
BF16 = jnp.bfloat16


def round_up(value, unit):
    return -(-value // unit) * unit


def iota(shape, dim):
    return lax.broadcasted_iota(jnp.int32, shape, dim)


def split(value, pieces):
    out = []
    for _ in range(pieces - 1):
        piece = value.astype(BF16)
        out.append(piece)
        value = value - piece.astype(F32)
    out.append(value.astype(BF16))
    return out


def mm(left, right, trans=False):
    dims = (((1,), (1 if trans else 0,)), ((), ()))
    return lax.dot_general(left, right, dims, preferred_element_type=F32)


def mm_exact(value, choice):
    total = None
    for piece in split(value, 3):
        part = mm(piece, choice)
        total = part if total is None else total + part
    return total


def ones_where(mask):
    return jnp.where(mask, 1.0, 0.0).astype(BF16)


def call(kernel, outs, scratch=(), flops=0, space=pltpu.VMEM, mib=20):
    def run(*args):
        shapes = [
            o if hasattr(o, "dtype") else jax.ShapeDtypeStruct(o, F32) for o in outs
        ]
        moved = sum(a.size * a.dtype.itemsize for a in (*args, *shapes))
        return pl.pallas_call(
            kernel,
            out_shape=shapes,
            in_specs=[pl.BlockSpec(memory_space=space)] * len(args),
            out_specs=[pl.BlockSpec(memory_space=pltpu.VMEM)] * len(outs),
            scratch_shapes=[s if hasattr(s, "dtype") else pltpu.VMEM(*s) for s in scratch],
            cost_estimate=pl.CostEstimate(
                flops=flops, bytes_accessed=moved, transcendentals=0
            ),
            compiler_params=pltpu.CompilerParams(vmem_limit_bytes=mib * 2**20),
        )(*args)

    return run


def chunk_of(slots):
    for groups in (5, 4, 3, 2, 1):
        if slots % (groups * LANES) == 0:
            return groups * LANES


def is_odd(axis):
    return lax.rem(lax.axis_index(axis), 2) == 1


def row_and_depth(cells, nz):
    if nz & (nz - 1) == 0:
        return lax.shift_right_logical(cells, nz.bit_length() - 1), cells & (nz - 1)
    return lax.div(cells, jnp.int32(nz)), lax.rem(cells, jnp.int32(nz))


def pick(field, cells_ref, deep_ref, out_ref):
    _, rows, depth = field.shape
    slots = cells_ref.shape[1]
    blocks = slots // LANES
    chunk = chunk_of(slots)
    left = jnp.concatenate(split(field.reshape(3 * rows, depth), 2), axis=1)
    for start in range(0, slots, chunk):
        row, _ = row_and_depth(cells_ref[:, start : start + chunk], depth)
        right = deep_ref[:, start : start + chunk]
        found = mm(left, jnp.concatenate([right, right], axis=0))
        here = iota((rows, chunk), 0) == row
        for comp in range(3):
            part = jnp.where(here, found[comp * rows : (comp + 1) * rows], 0.0)
            line = jnp.sum(part, axis=0, keepdims=True)
            for piece in range(chunk // LANES):
                at = comp * blocks + start // LANES + piece
                out_ref[at : at + 1, :] = line[:, piece * LANES : (piece + 1) * LANES]
    pad = out_ref.shape[0] - 3 * blocks
    if pad:
        out_ref[3 * blocks :, :] = jnp.zeros((pad, LANES), F32)


def one_hot(out_ref, values):
    chunk = chunk_of(out_ref.shape[1])
    for start in range(0, out_ref.shape[1], chunk):
        lanes = slice(start, start + chunk)
        out_ref[:, lanes] = ones_where(
            iota((out_ref.shape[0], chunk), 0) == values(lanes)
        )


def scaled(hot, lines):
    rows = hot.shape[0]
    out = []
    for place in range(2):
        for line in lines:
            piece = split(line, 2)[place].astype(F32)
            few = jnp.broadcast_to(piece, (16, piece.shape[1])).astype(BF16)
            out += [few * hot[at : at + 16] for at in range(0, rows, 16)]
    return jnp.concatenate(out, axis=0)


def times_diag(d_ref, field):
    nx, ny, nz = d_ref.shape[1:]
    return jnp.stack(
        [
            sum(d_ref[3 * a + b] * field[b] for b in range(3)).reshape(nx * ny, nz)
            for a in range(3)
        ]
    )


def first_kernel(
    cells_hbm, v_hbm, d_hbm, out_ref, cells_ref, v_ref, d_ref, deep_ref, sem
):
    pairs = [(cells_hbm, cells_ref), (v_hbm, v_ref)]
    pairs += [(d_hbm.at[entry], d_ref.at[entry]) for entry in range(9)]
    copies = [
        pltpu.make_async_copy(src, dst, sem.at[place])
        for place, (src, dst) in enumerate(pairs)
    ]
    for copy in copies:
        copy.start()
    copies[0].wait()
    depth = v_ref.shape[3]
    one_hot(deep_ref, lambda lanes: row_and_depth(cells_ref[:, lanes], depth)[1])
    for copy in copies[1:]:
        copy.wait()
    pick(times_diag(d_ref, [v_ref[b] for b in range(3)]), cells_ref, deep_ref, out_ref)


def spread_matrix(wells, width):
    shape = (wells, wells * width)
    gap = iota(shape, 1) - width * iota(shape, 0)
    return ones_where((gap >= 0) & (gap < width))


def last_matrix(wells, width, comp):
    shape = (wells * width, wells)
    return ones_where(iota(shape, 0) == width * iota(shape, 1) + (width - 3 + comp))


def prep_kernel(idx_ref, cells_ref, low_ref, high_ref, deep_ref, row_ref):
    wide = low_ref.shape[0]
    depth = deep_ref.shape[0]
    one_hot(low_ref, lambda lanes: idx_ref[:, lanes] & (wide - 1))
    one_hot(
        high_ref,
        lambda lanes: lax.shift_right_arithmetic(idx_ref[:, lanes], wide.bit_length() - 1),
    )
    one_hot(row_ref, lambda lanes: row_and_depth(cells_ref[:, lanes], depth)[0])
    one_hot(deep_ref, lambda lanes: row_and_depth(cells_ref[:, lanes], depth)[1])


def chain_kernel(
    value_ref, _, g_ref, couple_ref, out_ref, h_ref, e_ref, apart_ref, part_ref
):
    out_ref[...] = value_ref[...]
    chunks, width, span_all = g_ref.shape
    wells = couple_ref.shape[2]
    span = width // 3
    for lane in range(0, span_all, LANES):
        part_ref[...] = g_ref[:, :, lane : lane + LANES]
        for comp in range(3):
            apart_ref[comp, :, :, lane : lane + LANES] = part_ref[
                :, pl.ds(comp, span, stride=3), :
            ]
    spread = spread_matrix(wells, width)
    heads = [g_ref[:, d, :] for d in range(3)]
    for b in range(3):
        total = sum(
            heads[d] * mm_exact(couple_ref[3 * d + b], spread)[:chunks] for d in range(3)
        )
        h_ref[b] = jnp.zeros(h_ref.shape[1:], F32)
        h_ref[b, :chunks, :] = total
        full = h_ref[b]
        for a in range(3):
            e_ref[3 * a + b] = mm_exact(full, last_matrix(wells, width, a))


def pool_column(pool_ref, column, first, blocks):
    odd_x = is_odd("gx")
    tile = column.shape[0] // 3
    own, even, following = column[:tile], column[tile : 2 * tile], column[2 * tile :]
    parts = (jnp.where(odd_x, even, following), own, jnp.where(odd_x, following, even))
    for a, part in enumerate(parts):
        for comp in range(3):
            at = (first + a) * blocks
            pool_ref[comp, at : at + blocks, :] = part[comp * blocks : (comp + 1) * blocks]


def clear_tail(pool_ref, used):
    pool_ref[:, used:, :] = jnp.zeros((3, pool_ref.shape[1] - used, LANES), F32)


def gather_lines(pool_ref, idx_ref, low_ref, first_row):
    half = pool_ref.shape[1] // 2
    wide = 2 * LANES
    pooled = jnp.concatenate(
        [
            jnp.concatenate(
                [pool_ref[comp, pl.ds(odd, half, stride=2), :] for odd in range(2)], axis=1
            )
            for comp in range(3)
        ],
        axis=0,
    )
    left = jnp.concatenate(split(pooled, 2), axis=1)
    slots = idx_ref.shape[1]
    size = chunk_of(slots)
    for start in range(0, slots, size):
        place = idx_ref[:, start : start + size]
        right = low_ref[:, start : start + size]
        found = mm(left, jnp.concatenate([right, right], axis=0))
        block = lax.shift_right_arithmetic(place, wide.bit_length() - 1) - first_row
        here = iota((half, size), 0) == block
        for comp in range(3):
            part = jnp.where(here, found[comp * half : (comp + 1) * half], 0.0)
            yield start, comp, jnp.sum(part, axis=0, keepdims=True)


def scatter_lines(pool_ref, y_ref, low_ref, high_ref, first_row, group):
    half = pool_ref.shape[1] // 2
    slots = low_ref.shape[1]
    size = chunk_of(slots)
    spread_out = None
    for start in range(0, slots, size):
        lanes = slice(start, start + size)
        steps = range(start // group, (start + size) // group)
        lines = [
            jnp.concatenate(
                [y_ref[c : c + 1, comp * group : (comp + 1) * group] for c in steps], axis=1
            )
            for comp in range(3)
        ]
        hot = high_ref[first_row : first_row + half, lanes]
        part = mm(scaled(hot, lines), low_ref[:, lanes], trans=True)
        spread_out = part if spread_out is None else spread_out + part
    spread_out = spread_out[: 3 * half] + spread_out[3 * half :]
    for comp in range(3):
        block = spread_out[comp * half : (comp + 1) * half]
        for odd in range(2):
            pool_ref[comp, pl.ds(odd, half, stride=2), :] = block[
                :, odd * LANES : (odd + 1) * LANES
            ]


def own_gather_kernel(idx_ref, own_ref, low_ref, r_ref, pool_ref):
    group = r_ref.shape[2]
    blocks = idx_ref.shape[1] // LANES
    clear_tail(pool_ref, 3 * blocks)
    pool_column(pool_ref, own_ref[...], 0, blocks)
    r_ref[...] = jnp.zeros(r_ref.shape, F32)
    first_row = round_up(3 * blocks, 16)
    for start, comp, line in gather_lines(pool_ref, idx_ref, low_ref, first_row):
        for piece in range(line.shape[1] // group):
            at = start // group + piece
            r_ref[comp, at : at + 1, :] = line[:, piece * group : (piece + 1) * group]


def own_scatter_kernel(y_ref, low_ref, high_ref, keep_ref, pool_ref):
    blocks = low_ref.shape[1] // LANES
    tile = keep_ref.shape[0] // 3
    first_row = round_up(3 * blocks, 16)
    scatter_lines(pool_ref, y_ref, low_ref, high_ref, first_row, y_ref.shape[1] // 3)
    keep_ref[...] = jnp.zeros(keep_ref.shape, F32)
    for a in range(3):
        for comp in range(3):
            at = slice(a * tile + comp * blocks, a * tile + (comp + 1) * blocks)
            keep_ref[at, :] = pool_ref[comp, a * blocks : (a + 1) * blocks, :]


def solve_kernel(
    idx_ref, even_ref, next_ref, part_ref, g_ref, h_ref, e_ref, low_ref, high_ref,
    y_ref, to_next_ref, to_even_ref,
    pool_ref, r_ref, q_ref, tail_ref, p_ref,
):
    _, chunks, span, span_all = g_ref.shape
    width = 3 * span
    wells = span_all // width
    blocks = idx_ref.shape[1] // LANES
    tile = even_ref.shape[0] // 3
    group = wells * span
    odd_y = is_odd("gy")
    clear_tail(pool_ref, 6 * blocks)
    even, following = even_ref[...], next_ref[...]
    pool_column(pool_ref, jnp.where(odd_y, even, following), 0, blocks)
    pool_column(pool_ref, jnp.where(odd_y, following, even), 3, blocks)
    r_ref[...] = jnp.zeros(r_ref.shape, F32)
    for start, comp, line in gather_lines(pool_ref, idx_ref, low_ref, 0):
        for piece in range(line.shape[1] // group):
            at = start // group + piece
            r_ref[comp, at : at + 1, :] = (
                line[:, piece * group : (piece + 1) * group] + part_ref[comp, at : at + 1, :]
            )
    two = (2 * group, span_all)
    well_of = lax.shift_right_logical(iota(two, 0) & (group - 1), (span - 1).bit_length())
    gap = iota(two, 1) - width * well_of
    spread = ones_where((gap >= 0) & (gap < width))
    own = (iota((span, group), 1) & (span - 1)) == iota((span, group), 0)
    total = None
    for comp in range(3):
        values = r_ref[comp][:chunks]
        wide = jnp.where(own[None], values[:, None, :], 0.0).reshape(chunks * span, group)
        lifted = mm(jnp.concatenate(split(wide, 2), axis=1), spread)
        lifted = lifted.reshape(chunks, span, span_all)
        part = g_ref[comp] * lifted
        total = part if total is None else total + part
    q_ref[...] = jnp.zeros(q_ref.shape, F32)
    q_ref[:chunks, :] = jnp.sum(total, axis=1)
    plain = q_ref[...]
    for a in range(3):
        tail_ref[a] = mm_exact(plain, last_matrix(wells, width, a))
    p_ref[...] = jnp.zeros(p_ref.shape, F32)
    state = [jnp.zeros((1, wells), F32)] * 3
    for c in range(chunks - 1):
        state = [
            tail_ref[a, c : c + 1, :]
            - (
                e_ref[3 * a, c : c + 1, :] * state[0]
                + e_ref[3 * a + 1, c : c + 1, :] * state[1]
                + e_ref[3 * a + 2, c : c + 1, :] * state[2]
            )
            for a in range(3)
        ]
        for a in range(3):
            p_ref[a, c + 1 : c + 2, :] = state[a]
    wide_well = spread_matrix(wells, width)
    for b in range(3):
        plain = plain - h_ref[b] * mm_exact(p_ref[b], wide_well)
    square = (span_all, span_all)
    lane = iota((1, span_all), 1)
    comp_of = lax.div(lane, jnp.int32(group))
    rest = lax.rem(lane, jnp.int32(group))
    source = width * lax.div(rest, jnp.int32(span)) + 3 * lax.rem(rest, jnp.int32(span)) + comp_of
    y_ref[...] = mm_exact(plain, ones_where(iota(square, 0) == source))
    scatter_lines(pool_ref, y_ref, low_ref, high_ref, 0, group)
    for dst in (to_even_ref, to_next_ref):
        dst[...] = jnp.zeros(dst.shape, F32)
    for a in range(3):
        for comp in range(3):
            before, after = [
                pool_ref[comp, (b + a) * blocks : (b + a + 1) * blocks, :] for b in (0, 3)
            ]
            at = slice(a * tile + comp * blocks, a * tile + (comp + 1) * blocks)
            to_even_ref[at, :] = jnp.where(odd_y, before, after)
            to_next_ref[at, :] = jnp.where(odd_y, after, before)


def add_kernel(x_ref, y_ref, z_ref, keep_ref, to_next_ref, to_even_ref):
    tile = keep_ref.shape[0]
    odd_x = is_odd("gx")
    low, mid, high = [
        x_ref[part, :] + y_ref[part, :] + z_ref[part, :]
        for part in [slice(place * tile, (place + 1) * tile) for place in range(3)]
    ]
    keep_ref[...] = mid
    to_even_ref[...] = jnp.where(odd_x, low, high)
    to_next_ref[...] = jnp.where(odd_x, high, low)


def place_kernel(
    row_ref, deep_ref, v_ref, inv_ref, x_ref, y_ref, z_ref,
    out_ref, x_next_ref, x_even_ref, y_next_ref, y_even_ref,
):
    (first_x, last_x), (first_y, last_y) = [
        (lax.axis_index(axis) == 0, lax.axis_index(axis) == lax.axis_size(axis) - 1)
        for axis in ("gx", "gy")
    ]
    odd_x, odd_y = is_odd("gx"), is_odd("gy")
    nx, ny, nz = v_ref.shape[1:]
    rows = nx * ny
    slots = row_ref.shape[1]
    blocks = slots // LANES
    back = x_ref[...] + y_ref[...] + z_ref[...]
    size = chunk_of(slots)
    placed = None
    for start in range(0, slots, size):
        lanes = slice(start, start + size)
        steps = range(start // LANES, (start + size) // LANES)
        lines = [
            jnp.concatenate(
                [back[comp * blocks + at : comp * blocks + at + 1] for at in steps], axis=1
            )
            for comp in range(3)
        ]
        part = mm(scaled(row_ref[:, lanes], lines), deep_ref[:, lanes], trans=True)
        placed = part if placed is None else placed + part
    placed = placed[: 3 * rows] + placed[3 * rows :]
    for a in range(3):
        own = sum(inv_ref[3 * a + b] * v_ref[b] for b in range(3))
        out_ref[a] = own + placed[a * rows : (a + 1) * rows].reshape(nx, ny, nz)
        low = jnp.where(first_x, 0.0, out_ref[a, 0])
        high = jnp.where(last_x, 0.0, out_ref[a, nx - 1])
        x_even_ref[a] = jnp.where(odd_x, low, high)
        x_next_ref[a] = jnp.where(odd_x, high, low)
        low = jnp.where(first_y, 0.0, out_ref[a, :, 0, :])
        high = jnp.where(last_y, 0.0, out_ref[a, :, ny - 1, :])
        y_even_ref[a] = jnp.where(odd_y, low, high)
        y_next_ref[a] = jnp.where(odd_y, high, low)


def inner_kernel(z_ref, d_ref, off_ref, w_ref):
    nx, ny, nz = z_ref.shape[1:]
    row = iota((ny, nz), 0)
    lane = iota((ny, nz), 1)
    for x in range(nx):
        beside = []
        for b in range(3):
            own = z_ref[b, x]
            beside.append(
                [
                    z_ref[b, x - 1] if x else None,
                    z_ref[b, x + 1] if x < nx - 1 else None,
                    jnp.where(row == 0, 0.0, pltpu.roll(own, 1, 0)),
                    jnp.where(row == ny - 1, 0.0, pltpu.roll(own, ny - 1, 0)),
                    jnp.where(lane == 0, 0.0, pltpu.roll(own, 1, 1)),
                    jnp.where(lane == nz - 1, 0.0, pltpu.roll(own, nz - 1, 1)),
                ]
            )
        for a in range(3):
            total = sum(d_ref[3 * a + b, x] * z_ref[b, x] for b in range(3))
            for face in range(6):
                for b in range(3):
                    if beside[b][face] is not None:
                        total = total + off_ref[face, 3 * a + b, x] * beside[b][face]
            w_ref[a, x] = total


def add_faces(part_ref, faces, off_ref, w_ref):
    nx, ny, nz = part_ref.shape[1:]
    odd_x, odd_y = is_odd("gx"), is_odd("gy")
    x_next, x_even, y_next, y_even = [face[...] for face in faces]
    xl, xh = jnp.where(odd_x, x_even, x_next), jnp.where(odd_x, x_next, x_even)
    yl, yh = jnp.where(odd_y, y_even, y_next), jnp.where(odd_y, y_next, y_even)
    for a in range(3):
        w_ref[a] = part_ref[a]
        for x, face, beside in ((0, 0, xl), (nx - 1, 1, xh)):
            w_ref[a, x] += sum(off_ref[face, 3 * a + b, x] * beside[b] for b in range(3))
        for y, face, beside in ((0, 2, yl), (ny - 1, 3, yh)):
            w_ref[a, :, y, :] += sum(
                off_ref[face, 3 * a + b, :, y, :] * beside[b] for b in range(3)
            )


def next_kernel(
    cells_ref, deep_ref, part_ref, f0_ref, f1_ref, f2_ref, f3_ref, d_ref, off_ref, v_ref,
    w_ref, t_ref, out_ref,
):
    add_faces(part_ref, (f0_ref, f1_ref, f2_ref, f3_ref), off_ref, w_ref)
    t_ref[...] = w_ref[...] - v_ref[...]
    pick(times_diag(d_ref, [t_ref[b] for b in range(3)]), cells_ref, deep_ref, out_ref)


def gram_kernel(
    part_ref, f0_ref, f1_ref, f2_ref, f3_ref, off_ref, v_ref, w1_ref,
    w_ref, sums_ref,
):
    add_faces(part_ref, (f0_ref, f1_ref, f2_ref, f3_ref), off_ref, w_ref)
    one, two, rhs = w1_ref[...], w_ref[...], v_ref[...]
    top_one = jnp.maximum(jnp.max(jnp.abs(one)), 1e-30)
    top_two = jnp.maximum(jnp.max(jnp.abs(two)), 1e-30)
    one = one * (1.0 / jnp.full((1, 1), top_one))
    two = two * (1.0 / jnp.full((1, 1), top_two))
    sums = [
        jnp.sum(one * one), jnp.sum(one * two), jnp.sum(two * two),
        jnp.sum(one * rhs), jnp.sum(two * rhs), top_one, top_two,
    ]
    line = iota(sums_ref.shape[1:], 1)
    total = jnp.zeros(sums_ref.shape[1:], F32)
    for place, value in enumerate(sums):
        total = jnp.where(line == place, value, total)
    sums_ref[...] = jnp.broadcast_to(total[None], sums_ref.shape)


def final_kernel(
    all_ref, v_ref, z1_ref, z2_ref, w1_ref, w2_ref, sol_ref, res_ref
):
    every = [all_ref[:, 0, place : place + 1] for place in range(7)]
    top_one = jnp.max(every[5], axis=0, keepdims=True)
    top_two = jnp.max(every[6], axis=0, keepdims=True)
    one = every[5] / top_one
    two = every[6] / top_two
    scales = (one * one, one * two, two * two, one, two)
    g11, g12, g22, r1, r2 = [
        jnp.sum(value * scale, axis=0, keepdims=True) for value, scale in zip(every, scales)
    ]
    det = g11 * g22 - g12 * g12
    y1 = (g22 * r1 - g12 * r2) / det / top_one
    y2 = (g11 * r2 - g12 * r1) / det / top_two
    sol_ref[...] = y1 * z1_ref[...] + y2 * z2_ref[...]
    res_ref[...] = v_ref[...] - y1 * w1_ref[...] - y2 * w2_ref[...]


def swap(axis, to_even, to_next):
    size = {name: lax.axis_size(name) for name in ("gx", "gy")}
    count, breadth = size[axis], size["gy" if axis == "gx" else "gx"]

    def device(along, across):
        return along * size["gy"] + across if axis == "gx" else across * size["gy"] + along

    out = []
    order = [(1, to_next), (0, to_even)]
    same = to_even is to_next
    for first, value in order:
        pairs = []
        for across in range(breadth):
            for i in range(count):
                other = i + 1 if i % 2 == first else i - 1
                if 0 <= other < count:
                    pairs.append((device(i, across), device(other, across)))
                elif across ^ 1 < breadth:
                    pairs.append((device(i, across), device(i, across ^ 1)))
                else:
                    pairs.append((device(i, across), device(i, across)))
        out.append(lax.ppermute(value, ("gx", "gy"), pairs))
    return out[::-1]


def body(
    right_side,
    diag_blocks,
    off_blocks,
    cell_inverse,
    send_cells,
    recv_index,
    seg_count,
    span_inverse,
    span_couple,
):
    _, nx, ny, nz = right_side.shape
    slots = send_cells.shape[1]
    wells, longest = recv_index.shape
    chunks, width, span_all = span_inverse.shape
    span = width // 3
    blocks = slots // LANES
    tile = round_up(3 * blocks, 16)
    beside_rows = round_up(6 * blocks, 32)
    own_rows = round_up(3 * blocks, 32)
    tall = round_up(chunks, 16)
    field = right_side.shape
    (picked,) = call(
        first_kernel,
        [(tile, LANES)],
        [
            (send_cells.shape, jnp.int32),
            (field, F32),
            (diag_blocks.shape, F32),
            ((nz, slots), BF16),
            pltpu.SemaphoreType.DMA((11,)),
        ],
        flops=10**9,
        space=pltpu.HBM,
        mib=60,
    )(send_cells, right_side, diag_blocks)
    live = jnp.arange(longest)[None, :] < seg_count[:, None]
    along, column = recv_index // slots // 3, recv_index // slots % 3
    index = recv_index % slots + slots * along
    index = index + jnp.where(column == 1, beside_rows * LANES, slots * 3 * (column // 2))
    index = jnp.where(live, index, -1)
    index = index.reshape(wells, chunks, span).transpose(1, 0, 2).reshape(1, wells * longest)
    couple = jnp.pad(span_couple.transpose(1, 0, 2), ((0, 0), (0, tall - chunks), (0, 0)))
    low, high, deep, row = call(
        prep_kernel,
        [
            jax.ShapeDtypeStruct((height, slots), BF16)
            for height in (2 * LANES, (beside_rows + own_rows) // 2, nz, nx * ny)
        ],
    )(index, send_cells)
    held, h, e, apart = call(
        chain_kernel,
        [
            picked.shape,
            (3, tall, span_all),
            (9, tall, wells),
            (3, chunks, span, span_all),
        ],
        [((chunks, width, LANES), F32)],
    )(picked, index, span_inverse, couple)

    def precondition(vector, picked):
        beside = swap("gx", picked, picked)
        own = held if vector is right_side else picked
        column = jnp.concatenate([own, *beside], axis=0)
        even, following = swap("gy", column, column)
        (part,) = call(
            own_gather_kernel,
            [(3, tall, wells * span)],
            [((3, own_rows, LANES), F32)],
            flops=10**9,
        )(index, column, low)
        y, following, even = call(
            solve_kernel,
            [(tall, span_all)] + [(3 * tile, LANES)] * 2,
            [
                ((3, beside_rows, LANES), F32),
                ((3, tall, wells * span), F32),
                ((tall, span_all), F32),
                ((3, tall, wells), F32),
                ((3, tall, wells), F32),
            ],
            flops=3 * 10**9,
        )(index, even, following, part, apart, h, e, low, high)
        even, following = swap("gy", even, following)
        (keep,) = call(
            own_scatter_kernel,
            [(3 * tile, LANES)],
            [((3, own_rows, LANES), F32)],
            flops=10**9,
        )(y, low, high)
        keep, following, even = call(add_kernel, [(tile, LANES)] * 3)(
            keep, following, even
        )
        even, following = swap("gx", even, following)
        z, *faces = call(
            place_kernel,
            [(3, nx, ny, nz)] + [(3, ny, nz)] * 2 + [(3, nx, nz)] * 2,
            flops=10**9,
        )(row, deep, vector, cell_inverse, keep, following, even)
        faces = swap("gx", *faces[1::-1])[::-1] + swap("gy", *faces[:1:-1])[::-1]
        (part,) = call(inner_kernel, [field], flops=10**7)(z, diag_blocks, off_blocks)
        return z, part, faces

    z1, part, faces = precondition(right_side, picked)
    w1, turned, picked = call(
        next_kernel, [field, field, (tile, LANES)], flops=10**9
    )(send_cells, deep, part, *faces, diag_blocks, off_blocks, right_side)
    z2, part, faces = precondition(turned, picked)
    count = lax.axis_size(("gx", "gy"))
    w2, sums = call(gram_kernel, [field, (count, 1, LANES)])(
        part, *faces, off_blocks, right_side, w1
    )
    sums = lax.all_to_all(sums, ("gx", "gy"), 0, 0)
    return tuple(
        call(final_kernel, [field, field])(sums, right_side, z1, z2, w1, w2)
    )


def solution(mesh):
    return jax.shard_map(
        body,
        mesh=mesh,
        in_specs=(
            P(None, "gx", "gy", None),
            P(None, "gx", "gy", None),
            P(None, None, "gx", "gy", None),
            P(None, "gx", "gy", None),
            P(("gx", "gy"), None),
            P(("gx", "gy"), None),
            P(("gx", "gy")),
            P(None, None, ("gx", "gy")),
            P(None, None, ("gx", "gy")),
        ),
        out_specs=(P(None, "gx", "gy", None), P(None, "gx", "gy", None)),
        check_vma=False,
    )
```
